32 devices in a mesh: section: 4 (over y, x), dp: 8 (over z, core).
Axes of the slice: x: 2, y: 2, z: 4, core: 2. Of those that a mesh axis runs over, the one named last changes fastest.
Arguments:
- inputs: bfloat16 [4, 16, 196, 256], P(None, 'dp'), may hold values from -6 to 6
- cotangent: bfloat16 [4, 16, 196, 256], P(None, 'dp'), may hold values from -6 to 6
- routes: int32 [2, 4, 16, 49, 4], P(None, None, 'dp'), may hold values from 0 to 48, all different within a row
- vectors: float32 [4, 16, 256], P('section'), may hold values from -1.2 to 1.48
- in_weight: bfloat16 [4, 256, 768], P('section'), may hold values from -0.375 to 0.375
- out_weight: bfloat16 [4, 768, 256], P('section'), may hold values from -0.75 to 0.75
Outputs:
- final: bfloat16 [4, 16, 196, 256], P('section', 'dp')
- input_grad: bfloat16 [4, 16, 196, 256], P('section', 'dp')
- grad_vectors: float32 [4, 16, 256], P('section')
- grad_in_weight: float32 [4, 256, 768], P('section')
- grad_out_weight: float32 [4, 768, 256], P('section')
The draws below stay inside these ranges and needn't reach their ends.
Inputs may be any that keep to these rules, and one draw needn't show every extreme that they name: `routes`: each row names 4 different regions of the same image.
All inputs are finite; a program needn't handle non-finite values.
Results may differ from the reference program's by a relative error of at most 0.02.
Values may be sent and summed in bfloat16 or wider, within the bound.
A program may use at most 192 MiB of HBM per device.

```python
import jax
import jax.numpy as jnp
from jax import lax

D = 256
HEADS = 8
HEAD_DIM = 32
HID = 768
SIDE = 14
WIN = 7
TOPK = 4
LAYERS = 2
MICRO = 4
VEC_ROWS = 16
MB_IMG = 2
PATCHES = 196
REGIONS = 49
INSIDE = 4
BATCH = 16
SECTIONS = 4


def draw_vectors(key, part):
    key = jax.random.fold_in(key, 7)
    base_draw = jnp.clip(jax.random.normal(key, (SECTIONS, VEC_ROWS, D), jnp.float32), -4.0, 4.0)
    row_index = jnp.arange(VEC_ROWS)[None, :, None]
    row_scale = jnp.where(row_index == 0, 0.12, jnp.where(row_index < 6, 0.3, jnp.where(row_index < 15, 0.25, 0.3)))
    return jnp.where(row_index == 0, 1.0, 0.0) + row_scale * base_draw


def block_scale(own_key, dims, cuts, low, largest):
    level, own = 1.0, jax.random.fold_in(own_key, 6)
    for position, blocks in cuts:
        heights = jnp.exp(jax.random.uniform(jax.random.fold_in(own, position), (blocks,), jnp.float32, low / len(cuts), largest / len(cuts)))
        level = level * jnp.repeat(heights, dims[position] // blocks).reshape([-1 if axis == position else 1 for axis in range(len(dims))])
    return level


def different_ones(stream_key, rows, count, top, lift):
    ranking = jax.random.permutation(jax.random.fold_in(stream_key, 1), count)
    boost = ranking
    for power in range(3):
        boost = boost * boost // count
    boost = boost * lift // count
    chance = jax.random.randint(jax.random.fold_in(stream_key, 2), (rows, count), 0, 4096) + boost
    fixed_rows = jax.random.permutation(jax.random.fold_in(stream_key, 3), rows)[jnp.arange(count) % rows]
    chance = jnp.where(jnp.arange(rows)[:, None] == fixed_rows[None, :], 1 << 14, chance)
    priority = chance * count + jnp.arange(count)
    return lax.top_k(priority.astype(jnp.int32), top)[1].astype(jnp.int32)


def bell_draw(own_key, extent, deviation, reach, cuts=(), held_as=jnp.bfloat16):
    values = jax.random.normal(own_key, extent, jnp.float32) * deviation
    if len(cuts) > 0:
        values = block_scale(own_key, extent, cuts, -0.22, 0.18) * values
    return jnp.clip(values, min=-reach, max=reach).astype(held_as)


def setup_inputs(seed: int = 0) -> dict:
    arg_keys = jax.random.split(jax.random.key(seed), 7)
    return {
        "inputs": bell_draw(arg_keys[0], (MICRO, BATCH, PATCHES, D), 1.0, 6.0, ((1, 8),)),
        "cotangent": bell_draw(arg_keys[1], (MICRO, BATCH, PATCHES, D), 1.0, 6.0, ((1, 8),)),
        "routes": different_ones(arg_keys[2], LAYERS * MICRO * BATCH * REGIONS, REGIONS, TOPK, 0).reshape((LAYERS, MICRO, BATCH, REGIONS, TOPK)),
        "vectors": draw_vectors(jax.random.fold_in(arg_keys[6], 71), 0),
        "in_weight": bell_draw(arg_keys[4], (SECTIONS, D, HID), D ** -0.5, 0.375, ((0, 4),)),
        "out_weight": bell_draw(arg_keys[5], (SECTIONS, HID, D), (D // 4) ** -0.5, 0.75, ((0, 4),)),
    }


HIGHEST = lax.Precision.HIGHEST
EPSILON = 1e-06

@jax.custom_vjp
def low(v):
    return lax.optimization_barrier(v.astype(jnp.bfloat16)).astype(jnp.float32)

@jax.custom_vjp
def low_back(v):
    return v

def low_keep(v):
    return (low(v), None)

def low_pass(kept, grad):
    return (grad,)

def back_keep(v):
    return (v, None)

def back_low(kept, grad):
    return (low(grad),)
low.defvjp(low_keep, low_pass)
low_back.defvjp(back_keep, back_low)

def layer_norm(values, gain, offset):
    average = lax.optimization_barrier(jnp.mean(values, axis=-1, keepdims=True))
    centred = values - average
    spread = lax.optimization_barrier(jnp.mean(centred * centred, axis=-1, keepdims=True))
    return centred * lax.rsqrt(spread + EPSILON) * gain + offset

def to_regions(tokens):
    images = tokens.shape[0]
    channels = tokens.shape[-1]
    cell_side = SIDE // WIN
    grid_view = tokens.reshape(images, WIN, cell_side, WIN, cell_side, channels).transpose(0, 1, 3, 2, 4, 5)
    return grid_view.reshape(images, WIN * WIN, cell_side * cell_side, channels)

def from_regions(regions):
    images = regions.shape[0]
    channels = regions.shape[-1]
    cell_side = SIDE // WIN
    grid_view = regions.reshape(images, WIN, WIN, cell_side, cell_side, channels).transpose(0, 1, 3, 2, 4, 5)
    return grid_view.reshape(images, SIDE * SIDE, channels)

def pick_regions(region_rows, indices):
    return region_rows[indices]

def attention_section(current, section_table, weight_in, weight_out, route_rows):
    images = current.shape[0]
    grid_view = current.reshape(images, SIDE, SIDE, D)
    padded = jnp.pad(grid_view, ((0, 0), (1, 1), (1, 1), (0, 0)))
    mixed = grid_view + section_table[15]
    for row_shift in range(3):
        for col_shift in range(3):
            window_view = padded[:, row_shift:row_shift + SIDE, col_shift:col_shift + SIDE, :]
            mixed = mixed + window_view * section_table[6 + 3 * row_shift + col_shift]
    mixed = mixed.reshape(images, PATCHES, D)
    normed = low(layer_norm(mixed, section_table[0], section_table[1]))
    projected = low(low_back(jnp.einsum('bpc,cf->bpf', normed, weight_in, precision=HIGHEST)))
    queries = to_regions(projected[:, :, :D]).reshape(images, REGIONS, INSIDE, HEADS, HEAD_DIM)
    routed_keys = jax.vmap(pick_regions)(to_regions(projected[:, :, D:2 * D]), route_rows)
    routed_values = jax.vmap(pick_regions)(to_regions(projected[:, :, 2 * D:]), route_rows)
    routed_keys = routed_keys.reshape(images, REGIONS, TOPK * INSIDE, HEADS, HEAD_DIM)
    routed_values = routed_values.reshape(images, REGIONS, TOPK * INSIDE, HEADS, HEAD_DIM)
    scores = low_back(jnp.einsum('bgphd,bgjhd->bghpj', queries, routed_keys, precision=HIGHEST) * HEAD_DIM ** (-0.5))
    weights = low(jax.nn.softmax(scores, axis=-1))
    attended = low(low_back(jnp.einsum('bghpj,bgjhd->bgphd', weights, routed_values, precision=HIGHEST)))
    attended = from_regions(attended.reshape(images, REGIONS, INSIDE, D))
    branch = low_back(jnp.einsum('bpc,cf->bpf', attended, weight_out[:D], precision=HIGHEST) + section_table[2])
    return mixed + branch

def dense_section(current, section_table, weight_in, weight_out):
    normed = low(layer_norm(current, section_table[0], section_table[1]))
    hidden = low_back(jnp.einsum('bpc,cf->bpf', normed, weight_in, precision=HIGHEST) + section_table[3:6].reshape(HID))
    active = low(jax.nn.gelu(hidden, approximate=False))
    branch = low_back(jnp.einsum('bpf,fc->bpc', active, weight_out, precision=HIGHEST) + section_table[2])
    return current + branch

def network(start_value, vectors, weights_in, weights_out, group_routes):
    current = low_back(start_value)
    for section_number in range(SECTIONS):
        if section_number % 2 == 0:
            current = attention_section(current, vectors[section_number], weights_in[section_number], weights_out[section_number], group_routes[section_number // 2])
        else:
            current = dense_section(current, vectors[section_number], weights_in[section_number], weights_out[section_number])
        current = low_back(low(current))
    return current

def reference(inputs, cotangent, routes, vectors, in_weight, out_weight):
    images = MICRO * BATCH
    group_size = MICRO * MB_IMG
    step_count = images // group_size
    start_groups = inputs.astype(jnp.float32).reshape(step_count, group_size, PATCHES, D)
    back_groups = cotangent.astype(jnp.float32).reshape(step_count, group_size, PATCHES, D)
    route_groups = routes.reshape(LAYERS, step_count, group_size, REGIONS, TOPK).transpose(1, 0, 2, 3, 4)
    weights_in = in_weight.astype(jnp.float32)
    weights_out = out_weight.astype(jnp.float32)

    def one_group(totals, pieces):
        start_block, back_block, group_routes = pieces

        def run(start_value, vector_value, in_value, out_value):
            return network(start_value, vector_value, in_value, out_value, group_routes)
        result, pullback = jax.vjp(run, start_block, vectors, weights_in, weights_out)
        grad_start, grad_vectors, grad_in, grad_out = pullback(back_block)
        totals = (totals[0] + grad_vectors, totals[1] + grad_in, totals[2] + grad_out)
        return (totals, (result, grad_start))
    zero_totals = (jnp.zeros_like(vectors), jnp.zeros_like(weights_in), jnp.zeros_like(weights_out))
    totals, (results, grad_starts) = lax.scan(one_group, zero_totals, (start_groups, back_groups, route_groups))
    final_rows = results.reshape(MICRO, BATCH, PATCHES, D).astype(jnp.bfloat16)
    first_rows = grad_starts.reshape(MICRO, BATCH, PATCHES, D).astype(jnp.bfloat16)
    return (final_rows, first_rows, totals[0] / images, totals[1] / images, totals[2] / images)
```

```python
import functools

import jax
import jax.numpy as jnp
from jax import lax
from jax.experimental import pallas as pl
from jax.experimental.pallas import tpu as pltpu
from jax.sharding import PartitionSpec as P

D = 256
HEADS = 8
HEAD_DIM = 32
HID = 768
SIDE = 14
WIN = 7
TOPK = 4
SECTIONS = 4
VEC_ROWS = 16
PATCHES = 196
REGIONS = 49
EPSILON = 1e-06

PITCH = 16
LIVE = SIDE * PITCH
ROWS = 256
HALO = 24
NEGATIVE = -1e30
LOG2E = 1.4426950408889634
SCALE = HEAD_DIM ** (-0.5)

BF = jnp.bfloat16
F32 = jnp.float32


def dot(a, b, ca=1, cb=0):
    return lax.dot_general(
        a, b, (((ca,), (cb,)), ((), ())), preferred_element_type=jnp.float32
    )


def iota(shape, dim):
    return lax.broadcasted_iota(jnp.int32, shape, dim)


def one_hot(cond):
    return jnp.where(cond, 1.0, 0.0).astype(BF)


def rows_of(i, count=LIVE):
    return pl.ds(pl.multiple_of(i * ROWS, ROWS), count)


def col_sum(x):
    return jnp.sum(x, axis=0, keepdims=True)


def ln_stats(x):
    average = jnp.mean(x, axis=-1, keepdims=True)
    centred = x - average
    spread = jnp.mean(centred * centred, axis=-1, keepdims=True)
    inverse = lax.rsqrt(spread + EPSILON)
    return centred * inverse, inverse


def gelu_pair(x):
    a = jnp.abs(x)
    t = 1.0 / (1.0 + a * (0.3275911 * 0.7071067811865476))
    e = jnp.exp2(x * x * (-0.5 * LOG2E))
    w = t * (0.5 * 1.061405429) + (0.5 * -1.453152027)
    w = w * t + (0.5 * 1.421413741)
    w = w * t + (0.5 * -0.284496736)
    w = w * t + (0.5 * 0.254829592)
    w = w * t * e
    phi = jnp.where(x >= 0, 1.0 - w, w)
    return x * phi, phi + x * e * 0.3989422804014327


def live_mask():
    token = iota((LIVE, D), 0)
    return (token & (PITCH - 1)) < SIDE


def region_one_hot(shape, token_dim):
    token = iota(shape, token_dim)
    region = iota(shape, 1 - token_dim)
    r, c = token >> 4, token & (PITCH - 1)
    own = (r >> 1) * WIN + (c >> 1)
    return one_hot((own == region) & (c < SIDE) & (r < SIDE))


def compute_kernel(
    n,
    x_ref, cot_ref, routes_ref, vec_ref, win_ref, wout_ref,
    fin_ref, gin_ref, gvec_ref, ga_ref, gb_ref,
    hs, zh, inv, nm, pr, pt, at, act, gp, bias, mixed, g, dproj, cv, dom, qm, dsb, tmp, dqt, km, wide,
):
    eye = one_hot(iota((ROWS, ROWS), 0) == iota((ROWS, ROWS), 1))

    def transposed(x):
        return dot(eye, x, 1, 1)

    def head_lanes(h):
        return (iota((ROWS, D), 1) >> 5) == h

    def spread():
        t, p = iota((ROWS, PATCHES), 0), iota((ROWS, PATCHES), 1)
        r, c = t >> 4, t & (PITCH - 1)
        return one_hot((p == r * SIDE + c) & (c < SIDE) & (r < SIDE))

    def gather():
        p, t = iota((PATCHES, ROWS), 0), iota((PATCHES, ROWS), 1)
        r, c = t >> 4, t & (PITCH - 1)
        return one_hot((p == r * SIDE + c) & (c < SIDE) & (r < SIDE))

    zero_tail = jnp.zeros((ROWS - LIVE, D), F32)
    tail = lambda i: pl.ds(i * ROWS + LIVE, ROWS - LIVE)
    cv[0:HALO] = jnp.zeros((HALO, D), F32)
    cv[HALO + LIVE : HALO + LIVE + HALO] = jnp.zeros((HALO, D), F32)
    zero_wide = jnp.zeros((ROWS - LIVE, HID), BF)
    for i in range(n):
        for s in range(SECTIONS):
            nm[s, tail(i)] = zero_tail.astype(BF)
            hs[s, tail(i)] = zero_tail.astype(BF)
        for a in range(2):
            pr[a, tail(i)] = zero_wide
            act[a, tail(i)] = zero_wide
            at[a, tail(i)] = zero_tail.astype(BF)
        g[tail(i)] = zero_tail.astype(BF)
        dproj[tail(i)] = zero_wide

    spread_one = spread()
    key_region = region_one_hot((LIVE, REGIONS), 0)
    query_region = region_one_hot((REGIONS, ROWS), 1)
    for i in range(n):
        hs[0, pl.ds(i * ROWS, ROWS)] = dot(spread_one, x_ref[i]).astype(BF)
        g[pl.ds(i * ROWS, ROWS)] = dot(spread_one, cot_ref[i]).astype(BF)
        for a in range(2):
            picks = routes_ref[a, i]
            lane = iota((REGIONS, REGIONS), 1)
            routed = jnp.zeros((REGIONS, REGIONS), F32)
            for k in range(TOPK):
                routed = routed + jnp.where(picks[:, k : k + 1] == lane, 1.0, 0.0)
            by_region = dot(key_region, routed.astype(BF), 1, 1).astype(BF)
            bias[a, i] = (1.0 - dot(by_region, query_region)) * NEGATIVE

    def conv_load(x):
        cv[HALO : HALO + LIVE] = x

    def conv_at(r, shift):
        return cv[pl.ds(HALO + r * PITCH + shift, PITCH)]

    def attention_forward(s):
        a = s // 2
        vec = vec_ref.at[s]

        def image(i, carry):
            rows = rows_of(i)
            conv_load(hs[s, rows].astype(F32))
            for r in range(SIDE):
                total = conv_at(r, 0) + vec[15:16]
                for u in range(3):
                    for v in range(3):
                        j = 6 + 3 * u + v
                        total = total + conv_at(r, (u - 1) * PITCH + v - 1) * vec[j : j + 1]
                mixed[r * PITCH : (r + 1) * PITCH] = total
            hat, inverse = ln_stats(mixed[...])
            zh[s, rows] = hat
            inv[s, rows] = inverse
            normed = (hat * vec[0:1] + vec[1:2]).astype(BF)
            nm[s, rows] = normed
            pr[a, rows] = dot(normed, win_ref[s]).astype(BF)
            whole = rows_of(i, ROWS)
            tmp[...] = transposed(pr[a, whole, 2 * D : 3 * D]).astype(BF)

            def head(h, carry):
                lanes = pl.ds(pl.multiple_of(h * ROWS, ROWS), ROWS)
                own = pl.ds(pl.multiple_of(h * HEAD_DIM, HEAD_DIM), HEAD_DIM)
                keys = jnp.where(head_lanes(h)[:LIVE], pr[a, rows, D : 2 * D], jnp.zeros((), BF))
                scores = dot(keys, pr[a, whole, 0:D], 1, 1) * (SCALE * LOG2E) + bias[a, i]
                expo = jnp.exp2(scores - jnp.max(scores, axis=0, keepdims=True))
                weights = (expo * (1.0 / col_sum(expo))).astype(BF)
                pt[a, i, :, lanes] = weights
                dqt[own] = dot(tmp[own, 0:LIVE], weights)
                return carry

            lax.fori_loop(0, HEADS, head, 0)
            attended = transposed(dqt[...].astype(BF)).astype(BF)
            at[a, whole] = attended
            out = mixed[...] + dot(attended[:LIVE], wout_ref[s, 0:D]) + vec[2:3]
            hs[s + 1, rows] = out.astype(BF)
            return carry

        lax.fori_loop(0, n, image, 0)

    def dense_forward(s):
        a = s // 2
        vec = vec_ref.at[s]

        def image(i, carry):
            rows = rows_of(i)
            start = hs[s, rows].astype(F32)
            hat, inverse = ln_stats(start)
            zh[s, rows] = hat
            inv[s, rows] = inverse
            normed = (hat * vec[0:1] + vec[1:2]).astype(BF)
            nm[s, rows] = normed
            for j in range(3):
                lanes = slice(j * D, (j + 1) * D)
                hidden = dot(normed, win_ref[s, :, lanes]) + vec[3 + j : 4 + j]
                value, slope = gelu_pair(hidden)
                act[a, rows, lanes] = value.astype(BF)
                gp[a, rows, lanes] = slope
            out = start + dot(act[a, rows], wout_ref[s]) + vec[2:3]
            if s + 1 < SECTIONS:
                hs[s + 1, rows] = jnp.where(live_mask(), out, 0.0).astype(BF)
            else:
                dom[0:LIVE] = out.astype(BF)
                dom[LIVE:ROWS] = jnp.zeros((ROWS - LIVE, D), BF)
                fin_ref[i] = dot(gather(), dom[0:ROWS]).astype(BF)
            return carry

        lax.fori_loop(0, n, image, 0)

    def norm_backward(s, rows, d_normed):
        vec = vec_ref.at[s]
        hat = zh[s, rows]
        scaled = d_normed * vec[0:1]
        first = jnp.mean(scaled, axis=-1, keepdims=True)
        second = jnp.mean(scaled * hat, axis=-1, keepdims=True)
        gvec_ref[s, 0:1] += col_sum(d_normed * hat)
        gvec_ref[s, 1:2] += col_sum(d_normed)
        return inv[s, rows] * (scaled - first - hat * second)

    def dense_backward(s):
        a = s // 2

        def image(i, carry):
            rows = rows_of(i)
            grad = g[rows]
            gvec_ref[s, 2:3] += col_sum(grad.astype(F32))
            for j in range(3):
                lanes = slice(j * D, (j + 1) * D)
                d_active = dot(grad, wout_ref[s, lanes], 1, 1)
                d_hidden = (d_active * gp[a, rows, lanes]).astype(BF)
                dproj[rows, lanes] = d_hidden
                gvec_ref[s, 3 + j : 4 + j] += col_sum(d_hidden.astype(F32))
            d_normed = dot(dproj[rows], win_ref[s], 1, 1)
            out = grad.astype(F32) + norm_backward(s, rows, d_normed)
            wide[rows] = out.astype(BF)
            return carry

        lax.fori_loop(0, n, image, 0)
        ga_ref[s] = dot(nm[s], dproj[...], 0, 0)
        gb_ref[s] = dot(act[a], g[...], 0, 0)
        for i in range(n):
            g[pl.ds(i * ROWS, LIVE)] = wide[pl.ds(i * ROWS, LIVE)]

    def attention_backward(s):
        a = s // 2
        vec = vec_ref.at[s]

        def image(i, carry):
            rows = rows_of(i)
            whole = rows_of(i, ROWS)
            grad = g[rows]
            gvec_ref[s, 2:3] += col_sum(grad.astype(F32))
            d_attended = dot(g[whole], wout_ref[s, 0:D], 1, 1).astype(BF)
            tmp[...] = transposed(pr[a, whole, D : 2 * D]).astype(BF)
            km[...] = d_attended

            def head(h, carry):
                lanes = pl.ds(pl.multiple_of(h * ROWS, ROWS), ROWS)
                own = pl.ds(pl.multiple_of(h * HEAD_DIM, HEAD_DIM), HEAD_DIM)
                mine = head_lanes(h)
                nothing = jnp.zeros((), BF)
                values = jnp.where(mine[:LIVE], pr[a, rows, 2 * D : 3 * D], nothing)
                d_weights = dot(values, km[...], 1, 1)
                weights = pt[a, i, :, lanes].astype(F32)
                both = weights * d_weights
                d_scores = (both - weights * col_sum(both)).astype(BF)
                dsb[:, lanes] = d_scores
                dqt[own] = dot(tmp[own, 0:LIVE], d_scores)
                dom[lanes] = jnp.where(mine, km[...], nothing)
                qm[lanes] = jnp.where(mine, pr[a, whole, 0:D], nothing)
                return carry

            lax.fori_loop(0, HEADS, head, 0)
            dproj[rows, 0:D] = (transposed(dqt[...].astype(BF))[:LIVE] * SCALE).astype(BF)
            dproj[rows, D : 2 * D] = (dot(dsb[...], qm[...]) * SCALE).astype(BF)
            dproj[rows, 2 * D : 3 * D] = dot(pt[a, i], dom[...]).astype(BF)
            d_normed = dot(dproj[rows], win_ref[s], 1, 1)
            d_mixed = grad.astype(F32) + norm_backward(s, rows, d_normed)
            gvec_ref[s, 15:16] += col_sum(d_mixed)
            conv_load(d_mixed)
            taps = [jnp.zeros((PITCH, D), F32) for _ in range(9)]
            for r in range(SIDE):
                here = hs[s, pl.ds(pl.multiple_of(i * ROWS + r * PITCH, PITCH), PITCH)].astype(F32)
                total = conv_at(r, 0)
                for u in range(3):
                    for v in range(3):
                        j = 3 * u + v
                        moved = conv_at(r, (1 - u) * PITCH + 1 - v)
                        total = total + moved * vec[6 + j : 7 + j]
                        taps[j] = taps[j] + moved * here
                token = iota((PITCH, D), 0)
                total = jnp.where(token < SIDE, total, 0.0)
                wide[pl.ds(pl.multiple_of(i * ROWS + r * PITCH, PITCH), PITCH)] = total.astype(BF)
            for j in range(9):
                gvec_ref[s, 6 + j : 7 + j] += col_sum(taps[j])
            return carry

        lax.fori_loop(0, n, image, 0)
        ga_ref[s] = dot(nm[s], dproj[...], 0, 0)
        gb_ref[s, 0:D] = dot(at[a], g[...], 0, 0)
        gb_ref[s, D:HID] = jnp.zeros((HID - D, D), F32)
        for i in range(n):
            g[pl.ds(i * ROWS, LIVE)] = wide[pl.ds(i * ROWS, LIVE)]

    gvec_ref[...] = jnp.zeros_like(gvec_ref)
    attention_forward(0)
    dense_forward(1)
    attention_forward(2)
    dense_forward(3)
    dense_backward(3)
    attention_backward(2)
    dense_backward(1)
    attention_backward(0)
    for i in range(n):
        gin_ref[i] = dot(gather(), g[pl.ds(i * ROWS, ROWS)]).astype(BF)


def compute(x, cot, routes, vec, win, wout):
    n = x.shape[0]
    total = n * ROWS
    vmem = pl.BlockSpec(memory_space=pltpu.VMEM)
    return pl.pallas_call(
        functools.partial(compute_kernel, n),
        out_shape=(
            jax.ShapeDtypeStruct(x.shape, BF),
            jax.ShapeDtypeStruct(x.shape, BF),
            jax.ShapeDtypeStruct((SECTIONS, VEC_ROWS, D), F32),
            jax.ShapeDtypeStruct((SECTIONS, D, HID), F32),
            jax.ShapeDtypeStruct((SECTIONS, HID, D), F32),
        ),
        in_specs=[vmem] * 6,
        out_specs=(vmem,) * 5,
        scratch_shapes=[
            pltpu.VMEM((SECTIONS, total, D), BF),
            pltpu.VMEM((SECTIONS, total, D), F32),
            pltpu.VMEM((SECTIONS, total, 1), F32),
            pltpu.VMEM((SECTIONS, total, D), BF),
            pltpu.VMEM((2, total, HID), BF),
            pltpu.VMEM((2, n, LIVE, HEADS * ROWS), BF),
            pltpu.VMEM((2, total, D), BF),
            pltpu.VMEM((2, total, HID), BF),
            pltpu.VMEM((2, total, HID), F32),
            pltpu.VMEM((2, n, LIVE, ROWS), F32),
            pltpu.VMEM((LIVE, D), F32),
            pltpu.VMEM((total, D), BF),
            pltpu.VMEM((total, HID), BF),
            pltpu.VMEM((LIVE + 2 * HALO, D), F32),
            pltpu.VMEM((HEADS * ROWS, D), BF),
            pltpu.VMEM((HEADS * ROWS, D), BF),
            pltpu.VMEM((LIVE, HEADS * ROWS), BF),
            pltpu.VMEM((D, ROWS), BF),
            pltpu.VMEM((D, ROWS), F32),
            pltpu.VMEM((ROWS, D), BF),
            pltpu.VMEM((total, D), BF),
        ],
        compiler_params=pltpu.CompilerParams(vmem_limit_bytes=56 * 1024 * 1024),
        name="two_layers",
    )(x, cot, routes, vec, win, wout)


def per_device(inputs, cotangent, routes, vectors, in_weight, out_weight):
    section = lax.axis_index("section")
    x = lax.dynamic_index_in_dim(inputs, section, 0, keepdims=False)
    cot = lax.dynamic_index_in_dim(cotangent, section, 0, keepdims=False)
    picks = lax.dynamic_index_in_dim(routes, section, 1, keepdims=False)
    vec = lax.all_gather(vectors[0], "section")
    win = lax.all_gather(in_weight[0], "section")
    wout = lax.all_gather(out_weight[0], "section")
    fin, gin, gvec, ga, gb = compute(x, cot, picks, vec, win, wout)
    images = inputs.shape[0] * inputs.shape[1] * lax.axis_size("dp")
    gvec, ga, gb = (lax.psum_scatter(v, "section") for v in (gvec, ga, gb))
    gvec, ga, gb = lax.psum((gvec, ga, gb), "dp")
    return (
        fin[None],
        gin[None],
        (gvec / images)[None],
        (ga / images)[None],
        (gb / images)[None],
    )


def solution(mesh):
    in_specs = (
        P(None, "dp", None, None),
        P(None, "dp", None, None),
        P(None, None, "dp", None, None),
        P("section", None, None),
        P("section", None, None),
        P("section", None, None),
    )
    out_specs = (
        P("section", "dp", None, None),
        P("section", "dp", None, None),
        P("section", None, None),
        P("section", None, None),
        P("section", None, None),
    )
    return jax.shard_map(
        per_device, mesh=mesh, in_specs=in_specs, out_specs=out_specs, check_vma=False
    )
```

```python
import functools

import jax
import jax.numpy as jnp
from jax import lax
from jax.experimental import pallas as pl
from jax.experimental.pallas import tpu as pltpu
from jax.sharding import PartitionSpec as P

D = 256
HEADS = 8
HEAD_DIM = 32
HID = 768
SIDE = 14
WIN = 7
TOPK = 4
SECTIONS = 4
VEC_ROWS = 16
PATCHES = 196
REGIONS = 49
BLOCK = 256
EPSILON = 1e-06

PITCH = 16
LIVE = SIDE * PITCH
ROWS = 256
HALO = 24
NEGATIVE = -1e30
LOG2E = 1.4426950408889634
SCALE = HEAD_DIM ** (-0.5)

BF = jnp.bfloat16
F32 = jnp.float32


def dot(a, b, ca=1, cb=0):
    return lax.dot_general(
        a, b, (((ca,), (cb,)), ((), ())), preferred_element_type=jnp.float32
    )


def iota(shape, dim):
    return lax.broadcasted_iota(jnp.int32, shape, dim)


def one_hot(cond):
    return jnp.where(cond, 1.0, 0.0).astype(BF)


def rows_of(i, count=LIVE):
    return pl.ds(pl.multiple_of(i * ROWS, ROWS), count)


def col_sum(x):
    return jnp.sum(x, axis=0, keepdims=True)


def ln_stats(x):
    average = jnp.mean(x, axis=-1, keepdims=True)
    centred = x - average
    spread = jnp.mean(centred * centred, axis=-1, keepdims=True)
    inverse = lax.rsqrt(spread + EPSILON)
    return centred * inverse, inverse


def gelu_pair(x):
    a = jnp.abs(x)
    t = 1.0 / (1.0 + a * (0.3275911 * 0.7071067811865476))
    e = jnp.exp2(x * x * (-0.5 * LOG2E))
    w = t * (0.5 * 1.061405429) + (0.5 * -1.453152027)
    w = w * t + (0.5 * 1.421413741)
    w = w * t + (0.5 * -0.284496736)
    w = w * t + (0.5 * 0.254829592)
    w = w * t * e
    phi = jnp.where(x >= 0, 1.0 - w, w)
    return x * phi, phi + x * e * 0.3989422804014327


def live_mask():
    token = iota((LIVE, D), 0)
    return (token & (PITCH - 1)) < SIDE


def region_one_hot(shape, token_dim):
    token = iota(shape, token_dim)
    region = iota(shape, 1 - token_dim)
    r, c = token >> 4, token & (PITCH - 1)
    own = (r >> 1) * WIN + (c >> 1)
    return one_hot((own == region) & (c < SIDE) & (r < SIDE))


def layers(
    n, before_section, after_grads, poll,
    x_ref, cot_ref, routes_ref, vec_ref, win_ref, wout_ref, fin_ref, gin_ref, gvec_ref, grad_ref,
    hs, zh, inv, nm, pr, pt, at, act, gp, bias, mixed, g, dproj, cv, dom, qm, dsb, tmp, dqt, km, wide,
):
    eye = one_hot(iota((ROWS, ROWS), 0) == iota((ROWS, ROWS), 1))

    def transposed(x):
        return dot(eye, x, 1, 1)

    def head_lanes(h):
        return (iota((ROWS, D), 1) >> 5) == h

    def spread():
        t, p = iota((ROWS, PATCHES), 0), iota((ROWS, PATCHES), 1)
        r, c = t >> 4, t & (PITCH - 1)
        return one_hot((p == r * SIDE + c) & (c < SIDE) & (r < SIDE))

    def gather():
        p, t = iota((PATCHES, ROWS), 0), iota((PATCHES, ROWS), 1)
        r, c = t >> 4, t & (PITCH - 1)
        return one_hot((p == r * SIDE + c) & (c < SIDE) & (r < SIDE))

    zero_tail = jnp.zeros((ROWS - LIVE, D), F32)
    tail = lambda i: pl.ds(i * ROWS + LIVE, ROWS - LIVE)
    cv[0:HALO] = jnp.zeros((HALO, D), F32)
    cv[HALO + LIVE : HALO + LIVE + HALO] = jnp.zeros((HALO, D), F32)
    zero_wide = jnp.zeros((ROWS - LIVE, HID), BF)
    for i in range(n):
        for s in range(SECTIONS):
            nm[s, tail(i)] = zero_tail.astype(BF)
            hs[s, tail(i)] = zero_tail.astype(BF)
        for a in range(2):
            pr[a, tail(i)] = zero_wide
            act[a, tail(i)] = zero_wide
            at[a, tail(i)] = zero_tail.astype(BF)
        g[tail(i)] = zero_tail.astype(BF)
        dproj[tail(i)] = zero_wide

    spread_one = spread()
    key_region = region_one_hot((LIVE, REGIONS), 0)
    query_region = region_one_hot((REGIONS, ROWS), 1)
    for i in range(n):
        hs[0, pl.ds(i * ROWS, ROWS)] = dot(spread_one, x_ref[i]).astype(BF)
        g[pl.ds(i * ROWS, ROWS)] = dot(spread_one, cot_ref[i]).astype(BF)
        for a in range(2):
            picks = routes_ref[a, i]
            lane = iota((REGIONS, REGIONS), 1)
            routed = jnp.zeros((REGIONS, REGIONS), F32)
            for k in range(TOPK):
                routed = routed + jnp.where(picks[:, k : k + 1] == lane, 1.0, 0.0)
            by_region = dot(key_region, routed.astype(BF), 1, 1).astype(BF)
            bias[a, i] = (1.0 - dot(by_region, query_region)) * NEGATIVE

    def conv_load(x):
        cv[HALO : HALO + LIVE] = x

    def conv_at(r, shift):
        return cv[pl.ds(HALO + r * PITCH + shift, PITCH)]

    def attention_forward(s):
        a = s // 2
        vec = vec_ref.at[s]

        def image(i, carry):
            rows = rows_of(i)
            conv_load(hs[s, rows].astype(F32))
            for r in range(SIDE):
                total = conv_at(r, 0) + vec[15:16]
                for u in range(3):
                    for v in range(3):
                        j = 6 + 3 * u + v
                        total = total + conv_at(r, (u - 1) * PITCH + v - 1) * vec[j : j + 1]
                mixed[r * PITCH : (r + 1) * PITCH] = total
            hat, inverse = ln_stats(mixed[...])
            zh[s, rows] = hat
            inv[s, rows] = inverse
            normed = (hat * vec[0:1] + vec[1:2]).astype(BF)
            nm[s, rows] = normed
            pr[a, rows] = dot(normed, win_ref[s]).astype(BF)
            whole = rows_of(i, ROWS)
            tmp[...] = transposed(pr[a, whole, 2 * D : 3 * D]).astype(BF)

            def head(h, carry):
                lanes = pl.ds(pl.multiple_of(h * ROWS, ROWS), ROWS)
                own = pl.ds(pl.multiple_of(h * HEAD_DIM, HEAD_DIM), HEAD_DIM)
                keys = jnp.where(head_lanes(h)[:LIVE], pr[a, rows, D : 2 * D], jnp.zeros((), BF))
                scores = dot(keys, pr[a, whole, 0:D], 1, 1) * (SCALE * LOG2E) + bias[a, i]
                expo = jnp.exp2(scores - jnp.max(scores, axis=0, keepdims=True))
                weights = (expo * (1.0 / col_sum(expo))).astype(BF)
                pt[a, i, :, lanes] = weights
                dqt[own] = dot(tmp[own, 0:LIVE], weights)
                return carry

            lax.fori_loop(0, HEADS, head, 0)
            attended = transposed(dqt[...].astype(BF)).astype(BF)
            at[a, whole] = attended
            out = mixed[...] + dot(attended[:LIVE], wout_ref[s, 0:D]) + vec[2:3]
            hs[s + 1, rows] = out.astype(BF)
            return carry

        lax.fori_loop(0, n, image, 0)

    def dense_forward(s):
        a = s // 2
        vec = vec_ref.at[s]

        def image(i, carry):
            rows = rows_of(i)
            start = hs[s, rows].astype(F32)
            hat, inverse = ln_stats(start)
            zh[s, rows] = hat
            inv[s, rows] = inverse
            normed = (hat * vec[0:1] + vec[1:2]).astype(BF)
            nm[s, rows] = normed
            for j in range(3):
                lanes = slice(j * D, (j + 1) * D)
                hidden = dot(normed, win_ref[s, :, lanes]) + vec[3 + j : 4 + j]
                value, slope = gelu_pair(hidden)
                act[a, rows, lanes] = value.astype(BF)
                gp[a, rows, lanes] = slope
            out = start + dot(act[a, rows], wout_ref[s]) + vec[2:3]
            if s + 1 < SECTIONS:
                hs[s + 1, rows] = jnp.where(live_mask(), out, 0.0).astype(BF)
            else:
                dom[0:LIVE] = out.astype(BF)
                dom[LIVE:ROWS] = jnp.zeros((ROWS - LIVE, D), BF)
                fin_ref[0, i] = dot(gather(), dom[0:ROWS]).astype(BF)
            return carry

        lax.fori_loop(0, n, image, 0)

    def norm_backward(s, rows, d_normed):
        vec = vec_ref.at[s]
        hat = zh[s, rows]
        scaled = d_normed * vec[0:1]
        first = jnp.mean(scaled, axis=-1, keepdims=True)
        second = jnp.mean(scaled * hat, axis=-1, keepdims=True)
        gvec_ref[s, 0:1] += col_sum(d_normed * hat)
        gvec_ref[s, 1:2] += col_sum(d_normed)
        return inv[s, rows] * (scaled - first - hat * second)

    def dense_backward(s):
        a = s // 2

        def image(i, carry):
            rows = rows_of(i)
            grad = g[rows]
            gvec_ref[s, 2:3] += col_sum(grad.astype(F32))
            for j in range(3):
                lanes = slice(j * D, (j + 1) * D)
                d_active = dot(grad, wout_ref[s, lanes], 1, 1)
                d_hidden = (d_active * gp[a, rows, lanes]).astype(BF)
                dproj[rows, lanes] = d_hidden
                gvec_ref[s, 3 + j : 4 + j] += col_sum(d_hidden.astype(F32))
            d_normed = dot(dproj[rows], win_ref[s], 1, 1)
            out = grad.astype(F32) + norm_backward(s, rows, d_normed)
            wide[rows] = out.astype(BF)

        for i in range(n):
            image(i, 0)
            poll()
        for j in range(3):
            lanes = slice(j * D, (j + 1) * D)
            grad_ref[j] = dot(nm[s], dproj[:, lanes], 0, 0)
            grad_ref[3 + j] = dot(act[a, :, lanes], g[...], 0, 0)
        after_grads(s)
        for i in range(n):
            g[pl.ds(i * ROWS, LIVE)] = wide[pl.ds(i * ROWS, LIVE)]

    def attention_backward(s):
        a = s // 2
        vec = vec_ref.at[s]

        def image(i, carry):
            rows = rows_of(i)
            whole = rows_of(i, ROWS)
            grad = g[rows]
            gvec_ref[s, 2:3] += col_sum(grad.astype(F32))
            d_attended = dot(g[whole], wout_ref[s, 0:D], 1, 1).astype(BF)
            tmp[...] = transposed(pr[a, whole, D : 2 * D]).astype(BF)
            km[...] = d_attended

            def head(h, carry):
                lanes = pl.ds(pl.multiple_of(h * ROWS, ROWS), ROWS)
                own = pl.ds(pl.multiple_of(h * HEAD_DIM, HEAD_DIM), HEAD_DIM)
                mine = head_lanes(h)
                nothing = jnp.zeros((), BF)
                values = jnp.where(mine[:LIVE], pr[a, rows, 2 * D : 3 * D], nothing)
                d_weights = dot(values, km[...], 1, 1)
                weights = pt[a, i, :, lanes].astype(F32)
                both = weights * d_weights
                d_scores = (both - weights * col_sum(both)).astype(BF)
                dsb[:, lanes] = d_scores
                dqt[own] = dot(tmp[own, 0:LIVE], d_scores)
                dom[lanes] = jnp.where(mine, km[...], nothing)
                qm[lanes] = jnp.where(mine, pr[a, whole, 0:D], nothing)
                return carry

            lax.fori_loop(0, HEADS, head, 0)
            poll()
            dproj[rows, 0:D] = (transposed(dqt[...].astype(BF))[:LIVE] * SCALE).astype(BF)
            dproj[rows, D : 2 * D] = (dot(dsb[...], qm[...]) * SCALE).astype(BF)
            dproj[rows, 2 * D : 3 * D] = dot(pt[a, i], dom[...]).astype(BF)
            d_normed = dot(dproj[rows], win_ref[s], 1, 1)
            d_mixed = grad.astype(F32) + norm_backward(s, rows, d_normed)
            gvec_ref[s, 15:16] += col_sum(d_mixed)
            conv_load(d_mixed)
            taps = [jnp.zeros((PITCH, D), F32) for _ in range(9)]
            for r in range(SIDE):
                here = hs[s, pl.ds(pl.multiple_of(i * ROWS + r * PITCH, PITCH), PITCH)].astype(F32)
                total = conv_at(r, 0)
                for u in range(3):
                    for v in range(3):
                        j = 3 * u + v
                        moved = conv_at(r, (1 - u) * PITCH + 1 - v)
                        total = total + moved * vec[6 + j : 7 + j]
                        taps[j] = taps[j] + moved * here
                token = iota((PITCH, D), 0)
                total = jnp.where(token < SIDE, total, 0.0)
                wide[pl.ds(pl.multiple_of(i * ROWS + r * PITCH, PITCH), PITCH)] = total.astype(BF)
            for j in range(9):
                gvec_ref[s, 6 + j : 7 + j] += col_sum(taps[j])

        for i in range(n):
            image(i, 0)
            poll()
        for j in range(3):
            grad_ref[j] = dot(nm[s], dproj[:, j * D : (j + 1) * D], 0, 0)
        grad_ref[3] = dot(at[a], g[...], 0, 0)
        after_grads(s)
        for i in range(n):
            g[pl.ds(i * ROWS, LIVE)] = wide[pl.ds(i * ROWS, LIVE)]

    gvec_ref[...] = jnp.zeros_like(gvec_ref)
    for s in range(SECTIONS):
        before_section(s)
        (attention_forward, dense_forward)[s % 2](s)
    dense_backward(3)
    attention_backward(2)
    dense_backward(1)
    attention_backward(0)
    for i in range(n):
        gin_ref[0, i] = dot(gather(), g[pl.ds(i * ROWS, ROWS)]).astype(BF)


def layer_scratch(n):
    total = n * ROWS
    return [
        pltpu.VMEM((SECTIONS, total, D), BF),
        pltpu.VMEM((SECTIONS, total, D), F32),
        pltpu.VMEM((SECTIONS, total, 1), F32),
        pltpu.VMEM((SECTIONS, total, D), BF),
        pltpu.VMEM((2, total, HID), BF),
        pltpu.VMEM((2, n, LIVE, HEADS * ROWS), BF),
        pltpu.VMEM((2, total, D), BF),
        pltpu.VMEM((2, total, HID), BF),
        pltpu.VMEM((2, total, HID), F32),
        pltpu.VMEM((2, n, LIVE, ROWS), F32),
        pltpu.VMEM((LIVE, D), F32),
        pltpu.VMEM((total, D), BF),
        pltpu.VMEM((total, HID), BF),
        pltpu.VMEM((LIVE + 2 * HALO, D), F32),
        pltpu.VMEM((HEADS * ROWS, D), BF),
        pltpu.VMEM((HEADS * ROWS, D), BF),
        pltpu.VMEM((LIVE, HEADS * ROWS), BF),
        pltpu.VMEM((D, ROWS), BF),
        pltpu.VMEM((D, ROWS), F32),
        pltpu.VMEM((ROWS, D), BF),
        pltpu.VMEM((total, D), BF),
    ]


def compute_kernel(n, *refs):
    x_ref, cot_ref, routes_ref, vec_ref, win_ref, wout_ref, fin_ref, gin_ref, gvec_ref, ga_ref, gb_ref, grad_ref = refs[:12]

    def after_grads(s):
        for j in range(3):
            ga_ref[s, :, j * D : (j + 1) * D] = grad_ref[j]
            if s % 2 == 1 or j == 0:
                gb_ref[s, j * D : (j + 1) * D] = grad_ref[3 + j]
            else:
                gb_ref[s, j * D : (j + 1) * D] = jnp.zeros((D, D), F32)

    layers(
        n, lambda s: None, after_grads, lambda: None,
        x_ref, cot_ref, routes_ref, vec_ref, win_ref, wout_ref, fin_ref, gin_ref, gvec_ref, grad_ref, *refs[12:],
    )


def compute(x, cot, routes, vec, win, wout):
    n = x.shape[0]
    vmem = pl.BlockSpec(memory_space=pltpu.VMEM)
    return pl.pallas_call(
        functools.partial(compute_kernel, n),
        out_shape=(
            jax.ShapeDtypeStruct((1,) + x.shape, BF),
            jax.ShapeDtypeStruct((1,) + x.shape, BF),
            jax.ShapeDtypeStruct((SECTIONS, VEC_ROWS, D), F32),
            jax.ShapeDtypeStruct((SECTIONS, D, HID), F32),
            jax.ShapeDtypeStruct((SECTIONS, HID, D), F32),
        ),
        in_specs=[vmem] * 6,
        out_specs=(vmem,) * 5,
        scratch_shapes=[pltpu.VMEM((6, BLOCK, BLOCK), F32)] + layer_scratch(n),
        compiler_params=pltpu.CompilerParams(vmem_limit_bytes=56 * 1024 * 1024),
        name="layers_alone",
    )(x, cot, routes, vec, win, wout)


MESH = pl.DeviceIdType.MESH
HALF = BLOCK // 2
PART = HALF // SECTIONS


def blocks_of(t):
    return 6 if t % 2 == 1 else 4


def whole_kernel(
    n, dp, images,
    inputs_ref, cot_in_ref, routes_in_ref, vec_own, win_own, wout_own,
    fin_ref, gin_ref, gvec_ref, ga_ref, gb_ref,
    x_ref, cot_ref, routes_ref, vec_ref, win_ref, wout_ref, gvec_part, grad_ref,
    own_half, send_half, got_half, half_sum, got_part, part_sum, got_dp, result, vec_got, vec_sum, vec_dp,
    in_sem, w_send, w_recv, f_send, f_recv, v_send, v_recv, h_send, h_recv, p_send, p_recv, d_send, d_recv, r_send, r_recv,
    gv_send, gv_recv, gd_send, gd_recv,
    *scratch,
):
    me, j = lax.axis_index("section"), lax.axis_index("dp")
    core = lax.rem(j, 2)
    steps = (dp // 2).bit_length() - 1
    peers = [(lax.bitwise_xor(me, k), j) for k in range(1, SECTIONS)]
    crossed = [(lax.bitwise_xor(me, k), lax.bitwise_xor(j, 1)) for k in range(1, SECTIONS)]
    mate = (me, lax.bitwise_xor(j, 1))
    along = [(me, lax.bitwise_xor(j, 2 << b)) for b in range(steps)]
    waiting = []

    def remote(src, dst, send, recv, device):
        return pltpu.make_async_remote_copy(src, dst, send, recv, device_id=device, device_id_type=MESH)

    def go(copy, when=None):
        if when is None:
            copy.start()
        else:
            pl.when(when)(lambda: copy.start())
        waiting.append((copy, when))

    loads = [
        pltpu.make_async_copy(inputs_ref.at[me], x_ref, in_sem.at[0]),
        pltpu.make_async_copy(cot_in_ref.at[me], cot_ref, in_sem.at[1]),
        pltpu.make_async_copy(routes_in_ref.at[0, me], routes_ref.at[0], in_sem.at[2]),
        pltpu.make_async_copy(routes_in_ref.at[1, me], routes_ref.at[1], in_sem.at[3]),
    ]
    for copy in loads:
        copy.start()

    barrier = pltpu.get_barrier_semaphore()
    everyone = peers + crossed + [mate] + along
    for device in everyone:
        pl.semaphore_signal(barrier, inc=1, device_id=device, device_id_type=MESH)
    pl.semaphore_wait(barrier, len(everyone))

    own_rows = pl.ds(pl.multiple_of(core * HALF, HALF), HALF)
    tail_rows = pl.ds(pl.multiple_of(D + core * D, D), D)
    pieces = [(win_own, win_ref, own_rows), (wout_own, wout_ref, own_rows), (wout_own, wout_ref, tail_rows)]

    def has(piece, t):
        return piece < 2 or t % 2 == 1

    odd = lax.rem(me, 2) == 1
    for k, device in enumerate(peers):
        go(remote(vec_own.at[0], vec_ref.at[me], v_send.at[k], v_recv.at[k], device))
    for p, (source, target, rows) in enumerate(pieces):
        for k, device in enumerate(peers):
            go(remote(source.at[0, rows], target.at[me, rows], w_send.at[p, k], w_recv.at[p, me], device), None if p < 2 else odd)
    vec_ref[me] = vec_own[0]
    win_ref[me] = win_own[0]
    wout_ref[me] = wout_own[0]
    for copy in loads:
        copy.wait()
    for k, device in enumerate(peers):
        remote(vec_own.at[0], vec_ref.at[me], v_send.at[k], v_recv.at[k], device).wait_recv()

    def forward_weights(t):
        for p, (source, target, rows) in enumerate(pieces):
            if has(p, t):
                spot = target.at[t, rows]

                @pl.when(me != t)
                def _():
                    remote(spot, spot, w_send.at[p, 0], w_recv.at[p, t], mate).wait_recv()

                go(remote(spot, spot, f_send.at[p, t], f_recv.at[p, t], mate), me != t)

    def before_section(t):
        if t == 0:
            forward_weights(0)
        for p, (source, target, rows) in enumerate(pieces):
            if has(p, t):
                spot = target.at[t, rows]

                @pl.when(me != t)
                def _():
                    remote(spot, spot, f_send.at[p, t], f_recv.at[p, t], mate).wait_recv()

        if t + 1 < SECTIONS:
            forward_weights(t + 1)

    other_rows = pl.ds(pl.multiple_of((1 - core) * HALF, HALF), HALF)
    todo = []

    def poll():
        if todo:
            todo.pop(0)()

    def after_grads(t):
        count = blocks_of(t)
        blocks = pl.ds(0, count)
        for b in range(count):
            send_half[t, b] = grad_ref[b, other_rows].astype(BF)
        halves = remote(send_half.at[t, blocks], got_half.at[t, blocks], h_send.at[t], h_recv.at[t], mate)
        go(halves)
        for b in range(count):
            own_half[t, b] = grad_ref[b, own_rows].astype(BF)

        def quarter(k):
            return pl.ds(pl.multiple_of(k * PART, PART), PART)

        parts = [
            remote(
                half_sum.at[t, blocks, quarter(device[0])], got_part.at[t, k, blocks], p_send.at[t, k], p_recv.at[t, k], device
            )
            for k, device in enumerate(peers)
        ]

        def add_halves():
            halves.wait_recv()
            for b in range(count):
                half_sum[t, b] = (own_half[t, b].astype(F32) + got_half[t, b].astype(F32)).astype(BF)
            for copy in parts:
                go(copy)

        doubling = [
            remote(part_sum.at[t, b, blocks], got_dp.at[t, b, blocks], d_send.at[t, b], d_recv.at[t, b], along[b])
            for b in range(steps)
        ]

        def deliver():
            spot = result.at[blocks, core, quarter(me)]
            last = part_sum.at[t, steps, blocks]
            for k, device in enumerate(peers + crossed):
                go(remote(last, spot, r_send.at[t, k], r_recv.at[core, me], device), device[0] == t)
            go(remote(last, spot, r_send.at[t, 6], r_recv.at[core, me], mate), me == t)

            @pl.when(me == t)
            def _():
                for b in range(count):
                    result[b, core, quarter(me)] = part_sum[t, steps, b]

        def add_parts():
            for copy in parts:
                copy.wait_recv()
            for b in range(count):
                total = half_sum[t, b, quarter(me)].astype(F32)
                for k in range(SECTIONS - 1):
                    total = total + got_part[t, k, b].astype(F32)
                part_sum[t, 0, b] = total.astype(BF)
            if steps > 0:
                go(doubling[0])
            else:
                deliver()

        def add_dp(step):
            def run():
                doubling[step].wait_recv()
                for b in range(count):
                    total = part_sum[t, step, b].astype(F32) + got_dp[t, step, b].astype(F32)
                    part_sum[t, step + 1, b] = total.astype(BF)
                if step + 1 < steps:
                    go(doubling[step + 1])
                else:
                    deliver()

            return run

        todo.append(add_halves)
        todo.append(add_parts)
        for step in range(steps):
            todo.append(add_dp(step))

    layers(
        n, before_section, after_grads, poll,
        x_ref, cot_ref, routes_ref, vec_ref, win_ref, wout_ref, fin_ref, gin_ref, gvec_part, grad_ref, *scratch,
    )

    copies = [
        remote(gvec_part.at[device[0]], vec_got.at[k], gv_send.at[k], gv_recv.at[k], device) for k, device in enumerate(peers)
    ]
    for copy in copies:
        go(copy)
    poll()
    for copy in copies:
        copy.wait_recv()
    vec_sum[0] = gvec_part[me] + vec_got[0] + vec_got[1] + vec_got[2]
    for b in range(steps + 1):
        copy = remote(vec_sum.at[b], vec_dp.at[b], gd_send.at[b], gd_recv.at[b], (me, lax.bitwise_xor(j, 1 << b)))
        go(copy)
        poll()
        copy.wait_recv()
        vec_sum[b + 1] = vec_sum[b] + vec_dp[b]
    while todo:
        poll()
    gvec_ref[0] = vec_sum[steps + 1] * (1.0 / images)

    for c in range(2):
        for k in range(SECTIONS):
            for parity in range(2):
                blocks = pl.ds(0, blocks_of(parity))
                spot = result.at[blocks, c, pl.ds(k * PART, PART)]

                @pl.when(((me != k) | (core != c)) & (lax.rem(me, 2) == parity))
                def _():
                    remote(spot, spot, r_send.at[0, 0], r_recv.at[c, k], mate).wait_recv()

    for b in range(3):
        for c in range(2):
            rows = slice(c * HALF, (c + 1) * HALF)
            ga_ref[0, rows, b * D : (b + 1) * D] = result[b, c].astype(F32) * (1.0 / images)
            gb_ref[0, b * D + c * HALF : b * D + (c + 1) * HALF] = result[3 + b, c].astype(F32) * (1.0 / images)

    @pl.when(lax.rem(me, 2) == 0)
    def _():
        gb_ref[0, D:HID] = jnp.zeros((HID - D, D), F32)

    for copy, when in waiting:
        if when is None:
            copy.wait_send()
        else:
            pl.when(when)(lambda copy=copy: copy.wait_send())


def per_device(inputs, cotangent, routes, vectors, in_weight, out_weight):
    n = inputs.shape[1]
    dp = lax.axis_size("dp")
    steps = (dp // 2).bit_length() - 1
    images = inputs.shape[0] * n * dp
    vmem = pl.BlockSpec(memory_space=pltpu.VMEM)
    hbm = pl.BlockSpec(memory_space=pl.ANY)
    dma = pltpu.SemaphoreType.DMA
    return pl.pallas_call(
        functools.partial(whole_kernel, n, dp, images),
        out_shape=(
            jax.ShapeDtypeStruct((1,) + inputs.shape[1:], BF),
            jax.ShapeDtypeStruct((1,) + inputs.shape[1:], BF),
            jax.ShapeDtypeStruct((1, VEC_ROWS, D), F32),
            jax.ShapeDtypeStruct((1, D, HID), F32),
            jax.ShapeDtypeStruct((1, HID, D), F32),
        ),
        in_specs=[hbm] * 3 + [vmem] * 3,
        out_specs=(vmem,) * 5,
        scratch_shapes=[
            pltpu.VMEM(inputs.shape[1:], BF),
            pltpu.VMEM(inputs.shape[1:], BF),
            pltpu.VMEM((2,) + routes.shape[2:], jnp.int32),
            pltpu.VMEM((SECTIONS, VEC_ROWS, D), F32),
            pltpu.VMEM((SECTIONS, D, HID), BF),
            pltpu.VMEM((SECTIONS, HID, D), BF),
            pltpu.VMEM((SECTIONS, VEC_ROWS, D), F32),
            pltpu.VMEM((6, BLOCK, BLOCK), F32),
            pltpu.VMEM((SECTIONS, 6, HALF, BLOCK), BF),
            pltpu.VMEM((SECTIONS, 6, HALF, BLOCK), BF),
            pltpu.VMEM((SECTIONS, 6, HALF, BLOCK), BF),
            pltpu.VMEM((SECTIONS, 6, HALF, BLOCK), BF),
            pltpu.VMEM((SECTIONS, 3, 6, PART, BLOCK), BF),
            pltpu.VMEM((SECTIONS, steps + 1, 6, PART, BLOCK), BF),
            pltpu.VMEM((SECTIONS, max(steps, 1), 6, PART, BLOCK), BF),
            pltpu.VMEM((6, 2, HALF, BLOCK), BF),
            pltpu.VMEM((3, VEC_ROWS, D), F32),
            pltpu.VMEM((steps + 2, VEC_ROWS, D), F32),
            pltpu.VMEM((steps + 1, VEC_ROWS, D), F32),
            dma((4,)),
            dma((3, 3)), dma((3, SECTIONS)),
            dma((3, SECTIONS)), dma((3, SECTIONS)),
            dma((3,)), dma((3,)),
            dma((SECTIONS,)), dma((SECTIONS,)),
            dma((SECTIONS, 3)), dma((SECTIONS, 3)),
            dma((SECTIONS, max(steps, 1))), dma((SECTIONS, max(steps, 1))),
            dma((SECTIONS, 7)), dma((2, SECTIONS)),
            dma((3,)), dma((3,)),
            dma((steps + 1,)), dma((steps + 1,)),
        ]
        + layer_scratch(n),
        compiler_params=pltpu.CompilerParams(
            vmem_limit_bytes=60 * 1024 * 1024, collective_id=0, has_side_effects=True
        ),
        name="two_layers",
    )(inputs, cotangent, routes, vectors, in_weight, out_weight)


def solution(mesh):
    in_specs = (
        P(None, "dp", None, None),
        P(None, "dp", None, None),
        P(None, None, "dp", None, None),
        P("section", None, None),
        P("section", None, None),
        P("section", None, None),
    )
    out_specs = (
        P("section", "dp", None, None),
        P("section", "dp", None, None),
        P("section", None, None),
        P("section", None, None),
        P("section", None, None),
    )
    return jax.shard_map(
        per_device, mesh=mesh, in_specs=in_specs, out_specs=out_specs, check_vma=False
    )
```

```python
import functools

import jax
import jax.numpy as jnp
from jax import lax
from jax.experimental import pallas as pl
from jax.experimental.pallas import tpu as pltpu
from jax.sharding import PartitionSpec as P

D = 256
HEADS = 8
HEAD_DIM = 32
HID = 768
SIDE = 14
WIN = 7
TOPK = 4
SECTIONS = 4
VEC_ROWS = 16
PATCHES = 196
REGIONS = 49
BLOCK = 256
EPSILON = 1e-06

PITCH = 16
LIVE = SIDE * PITCH
ROWS = 256
HALO = 24
CHUNK = 32
LANES = 128
NEGATIVE = -1e30
LOG2E = 1.4426950408889634
SCALE = HEAD_DIM ** (-0.5)

BF = jnp.bfloat16
F32 = jnp.float32


def dot(a, b, ca=1, cb=0):
    return lax.dot_general(
        a, b, (((ca,), (cb,)), ((), ())), preferred_element_type=jnp.float32
    )


def iota(shape, dim):
    return lax.broadcasted_iota(jnp.int32, shape, dim)


def one_hot(cond):
    return jnp.where(cond, 1.0, 0.0).astype(BF)


def rows_of(i, count=LIVE):
    return pl.ds(pl.multiple_of(i * ROWS, ROWS), count)


def col_sum(x):
    return jnp.sum(x, axis=0, keepdims=True)


def ln_stats(x):
    average = jnp.mean(x, axis=-1, keepdims=True)
    centred = x - average
    spread = jnp.mean(centred * centred, axis=-1, keepdims=True)
    inverse = lax.rsqrt(spread + EPSILON)
    return centred * inverse, inverse


def gelu_pair(x):
    a = jnp.abs(x)
    t = 1.0 / (1.0 + a * (0.3275911 * 0.7071067811865476))
    e = jnp.exp2(x * x * (-0.5 * LOG2E))
    w = t * (0.5 * 1.061405429) + (0.5 * -1.453152027)
    w = w * t + (0.5 * 1.421413741)
    w = w * t + (0.5 * -0.284496736)
    w = w * t + (0.5 * 0.254829592)
    w = w * t * e
    phi = jnp.where(x >= 0, 1.0 - w, w)
    return x * phi, phi + x * e * 0.3989422804014327


def region_one_hot(shape, token_dim):
    token = iota(shape, token_dim)
    region = iota(shape, 1 - token_dim)
    r, c = token >> 4, token & (PITCH - 1)
    own = (r >> 1) * WIN + (c >> 1)
    return one_hot((own == region) & (c < SIDE) & (r < SIDE))


def layers(
    n, at_point,
    x_ref, cot_ref, routes_ref, vec_ref, win_ref, wout_ref, fin_ref, gin_ref, gvec_ref, grad_ref,
    hs, zh, inv, nm, pr, pt, at, act, gp, bias, mixed, g, dproj, cv, cvl, cvr, dom, qm, dsb, tmp, dqt, km, wide,
):
    pairs = PATCHES * n

    def eye():
        return one_hot(iota((ROWS, ROWS), 0) == iota((ROWS, ROWS), 1))

    def transposed(x):
        return dot(eye(), x, 1, 1)

    def spread(i):
        t, p = iota((ROWS, pairs), 0), iota((ROWS, pairs), 1)
        r, c = t >> 4, t & (PITCH - 1)
        return one_hot((p == (r * SIDE + c) * n + i) & (c < SIDE) & (r < SIDE))

    def gather():
        p, t = iota((pairs, n * ROWS), 0), iota((pairs, n * ROWS), 1)
        r, c, i = (t & (ROWS - 1)) >> 4, t & (PITCH - 1), t >> 8
        return one_hot((p == (r * SIDE + c) * n + i) & (c < SIDE) & (r < SIDE))

    def chunks():
        return [slice(c, c + CHUNK) for c in range(0, LIVE, CHUNK)]

    def rows_at(i, c, count):
        return pl.ds(pl.multiple_of(i * ROWS + c, PITCH), count)

    def tail(i):
        return pl.ds(i * ROWS + LIVE, ROWS - LIVE)

    none = jnp.zeros((ROWS - LIVE, D), BF)
    none_wide = jnp.zeros((ROWS - LIVE, HID), BF)
    halo = jnp.zeros((HALO, D), F32)
    for buffer in (cv, cvl, cvr):
        buffer[0:HALO] = halo
        buffer[HALO + LIVE : HALO + LIVE + HALO] = halo
    for i in range(n):
        for s in range(SECTIONS):
            nm[s, tail(i)] = none
            hs[s, tail(i)] = none
        for a in range(2):
            pr[a, tail(i)] = none_wide
            act[a, tail(i)] = none_wide
            at[a, tail(i)] = none
        wide[tail(i)] = none
        dproj[tail(i)] = none_wide
    gvec_ref[...] = jnp.zeros_like(gvec_ref)

    at_point("inputs", 0)
    x_pairs = x_ref[...].reshape(pairs, D)
    cot_pairs = cot_ref[...].reshape(pairs, D)
    for i in range(n):
        spread_i = spread(i)
        hs[0, pl.ds(i * ROWS, ROWS)] = dot(spread_i, x_pairs).astype(BF)
        g[pl.ds(i * ROWS, ROWS)] = dot(spread_i, cot_pairs).astype(BF)

    def conv_load(r0, count, x):
        cv[pl.ds(HALO + r0, count)] = x

    def conv_shift():
        for rows in chunks():
            cvl[HALO + rows.start : HALO + rows.stop] = cv[HALO + rows.start - 1 : HALO + rows.stop - 1]
            cvr[HALO + rows.start : HALO + rows.stop] = cv[HALO + rows.start + 1 : HALO + rows.stop + 1]

    def conv_at(r, u, v):
        start = HALO + (r + u) * PITCH
        return (cvl, cv, cvr)[v + 1][start : start + PITCH]

    def attention_start(s):
        vec = vec_ref.at[s]

        def image(i, carry):
            for rows in chunks():
                conv_load(rows.start, CHUNK, hs[s, rows_at(i, rows.start, CHUNK)].astype(F32))
            conv_shift()
            for r in range(SIDE):
                total = conv_at(r, 0, 0) + vec[15:16]
                for u in (-1, 0, 1):
                    for v in (-1, 0, 1):
                        j = 6 + 3 * (u + 1) + v + 1
                        total = total + conv_at(r, u, v) * vec[j : j + 1]
                here = rows_at(i, r * PITCH, PITCH)
                mixed[here] = total
                hat, inverse = ln_stats(total)
                zh[s, here] = hat
                inv[s, here] = inverse
                nm[s, here] = (hat * vec[0:1] + vec[1:2]).astype(BF)
            return carry

        lax.fori_loop(0, n, image, 0)

    def route_bias():
        key_region = region_one_hot((LIVE, REGIONS), 0)
        query_region = region_one_hot((REGIONS, ROWS), 1)
        for i in range(n):
            for a in range(2):
                picks = routes_ref[a, i]
                region = iota((REGIONS, REGIONS), 0)
                routed = jnp.zeros((REGIONS, REGIONS), F32)
                for k in range(TOPK):
                    routed = routed + jnp.where(picks[k : k + 1] == region, 1.0, 0.0)
                by_region = dot(key_region, routed.astype(BF)).astype(BF)
                bias[a, i] = (1.0 - dot(by_region, query_region)) * NEGATIVE

    def half_of(h):
        return slice((h // 4) * LANES, (h // 4 + 1) * LANES)

    def own_lanes(h, count):
        return (iota((count, LANES), 1) >> 5) == h % 4

    def attention_forward(s):
        a = s // 2
        vec = vec_ref.at[s]

        def image(i, carry):
            rows = rows_of(i)
            whole = rows_of(i, ROWS)
            pr[a, rows] = dot(nm[s, rows], win_ref[s]).astype(BF)
            tmp[...] = transposed(pr[a, whole, 2 * D : 3 * D]).astype(BF)
            for h in range(HEADS):
                lanes = half_of(h)
                keys = jnp.where(own_lanes(h, LIVE), pr[a, rows, slice(D + lanes.start, D + lanes.stop)], jnp.zeros((), BF))
                scores = dot(keys, pr[a, whole, lanes], 1, 1) * (SCALE * LOG2E) + bias[a, i]
                expo = jnp.exp2(scores - jnp.max(scores, axis=0, keepdims=True))
                pt[a, i, :, h * ROWS : (h + 1) * ROWS] = (expo * (1.0 / col_sum(expo))).astype(BF)
            for h in range(HEADS):
                own = slice(h * HEAD_DIM, (h + 1) * HEAD_DIM)
                dqt[own] = dot(tmp[own, 0:LIVE], pt[a, i, :, h * ROWS : (h + 1) * ROWS])
            attended = transposed(dqt[...].astype(BF)).astype(BF)
            at[a, whole] = attended
            out = mixed[rows] + dot(attended[:LIVE], wout_ref[s, 0:D]) + vec[2:3]
            hs[s + 1, rows] = out.astype(BF)
            pl.when(i == 0)(lambda: at_point("next", s))
            return carry

        lax.fori_loop(0, n, image, 0)

    def dense_forward(s):
        a = s // 2
        vec = vec_ref.at[s]
        token = iota((CHUNK, D), 0)

        def image(i, carry):
            rows = rows_of(i)
            for part in chunks():
                here = rows_at(i, part.start, CHUNK)
                hat, inverse = ln_stats(hs[s, here].astype(F32))
                zh[s, here] = hat
                inv[s, here] = inverse
                nm[s, here] = (hat * vec[0:1] + vec[1:2]).astype(BF)
            for j in range(3):
                lanes = slice(j * D, (j + 1) * D)
                hidden = dot(nm[s, rows], win_ref[s, :, lanes]) + vec[3 + j : 4 + j]
                value, slope = gelu_pair(hidden)
                act[a, rows, lanes] = value.astype(BF)
                gp[a, rows, lanes] = slope
            out = hs[s, rows].astype(F32) + dot(act[a, rows], wout_ref[s]) + vec[2:3]
            if s + 1 < SECTIONS:
                live = (iota((LIVE, D), 0) & (PITCH - 1)) < SIDE
                hs[s + 1, rows] = jnp.where(live, out, 0.0).astype(BF)
            else:
                wide[rows] = out.astype(BF)
            pl.when(i == 0)(lambda: at_point("next", s))
            return carry

        lax.fori_loop(0, n, image, 0)

    def norm_backward(s, here, d_normed, sums):
        vec = vec_ref.at[s]
        hat = zh[s, here]
        product = d_normed * hat
        scaled = d_normed * vec[0:1]
        first = jnp.mean(scaled, axis=-1, keepdims=True)
        second = jnp.mean(product * vec[0:1], axis=-1, keepdims=True)
        sums[0] = sums[0] + fold(product)
        sums[1] = sums[1] + fold(d_normed)
        return inv[s, here] * (scaled - first - hat * second)

    def fold(x):
        return jnp.sum(x.reshape(x.shape[0] // 8, 8, x.shape[1]), axis=0)

    def empty():
        return jnp.zeros((8, D), F32)

    def add_row(s, row, total):
        gvec_ref[s, row : row + 1] += col_sum(total)

    def dense_backward(s):
        a = s // 2
        for i in range(n):
            rows = rows_of(i)
            for j in range(3):
                lanes = slice(j * D, (j + 1) * D)
                d_active = dot(g[rows], wout_ref[s, lanes], 1, 1)
                d_hidden = (d_active * gp[a, rows, lanes]).astype(BF)
                dproj[rows, lanes] = d_hidden
                add_row(s, 3 + j, fold(d_hidden.astype(F32)))
        for j in range(3):
            lanes = slice(j * D, (j + 1) * D)
            grad_ref[j] = dot(nm[s], dproj[:, lanes], 0, 0)
            grad_ref[3 + j] = dot(act[a, :, lanes], g[...], 0, 0)
        at_point("grads", s)
        for i in range(n):
            rows = rows_of(i)
            d_normed = dot(dproj[rows], win_ref[s], 1, 1)
            sums = [empty(), empty(), empty()]
            for part in chunks():
                here = rows_at(i, part.start, CHUNK)
                grad = g[here].astype(F32)
                sums[2] = sums[2] + fold(grad)
                out = grad + norm_backward(s, here, d_normed[part], sums)
                g[here] = out.astype(BF)
            for row in range(3):
                add_row(s, row, sums[row])
            at_point("image", 2 * s + i)

    def attention_backward(s):
        a = s // 2
        vec = vec_ref.at[s]
        nothing = jnp.zeros((), BF)
        grad_ref[3] = dot(at[a], g[...], 0, 0)
        for i in range(n):
            rows = rows_of(i)
            whole = rows_of(i, ROWS)
            km[...] = dot(g[whole], wout_ref[s, 0:D], 1, 1).astype(BF)
            tmp[...] = transposed(pr[a, whole, D : 2 * D]).astype(BF)
            for h in range(HEADS):
                lanes = half_of(h)
                row = slice(h * ROWS, (h + 1) * ROWS)
                dom[row] = jnp.where(own_lanes(h, ROWS), km[:, lanes], nothing)
                qm[row] = jnp.where(own_lanes(h, ROWS), pr[a, whole, lanes], nothing)
            for h in range(HEADS):
                lanes = half_of(h)
                row = slice(h * ROWS, (h + 1) * ROWS)
                values = jnp.where(own_lanes(h, LIVE), pr[a, rows, slice(2 * D + lanes.start, 2 * D + lanes.stop)], nothing)
                d_weights = dot(values, km[:, lanes], 1, 1)
                weights = pt[a, i, :, row].astype(F32)
                dsb[:, row] = (weights * (d_weights - col_sum(weights * d_weights))).astype(BF)
                if h == 3:
                    at_point("half", 2 * s + i)
            for half in range(2):
                lanes = slice(2 * D + half * LANES, 2 * D + (half + 1) * LANES)
                four = slice(half * 4 * ROWS, (half + 1) * 4 * ROWS)
                dproj[rows, lanes] = dot(pt[a, i, :, four], dom[four]).astype(BF)
            for h in range(HEADS):
                own = slice(h * HEAD_DIM, (h + 1) * HEAD_DIM)
                dqt[own] = dot(tmp[own, 0:LIVE], dsb[:, h * ROWS : (h + 1) * ROWS])
            for half in range(2):
                lanes = slice(D + half * LANES, D + (half + 1) * LANES)
                four = slice(half * 4 * ROWS, (half + 1) * 4 * ROWS)
                dproj[rows, lanes] = (dot(dsb[:, four], qm[four]) * SCALE).astype(BF)
            dproj[rows, 0:D] = (transposed(dqt[...].astype(BF))[:LIVE] * SCALE).astype(BF)
            at_point("image", 2 * s + i)
        for j in range(3):
            grad_ref[j] = dot(nm[s], dproj[:, j * D : (j + 1) * D], 0, 0)
        at_point("grads", s)
        for i in range(n):
            rows = rows_of(i)
            d_normed = dot(dproj[rows], win_ref[s], 1, 1)
            sums = [empty(), empty(), empty(), empty()]
            for part in chunks():
                here = rows_at(i, part.start, CHUNK)
                grad = g[here].astype(F32)
                sums[2] = sums[2] + fold(grad)
                d_mixed = grad + norm_backward(s, here, d_normed[part], sums)
                sums[3] = sums[3] + fold(d_mixed)
                conv_load(part.start, CHUNK, d_mixed)
            for row, total in zip((0, 1, 2, 15), sums):
                add_row(s, row, total)
            at_point("norm", 2 * s + i)
            conv_shift()
            taps = [empty() for _ in range(9)]
            for r in range(SIDE):
                here = rows_at(i, r * PITCH, PITCH)
                start = hs[s, here].astype(F32)
                total = conv_at(r, 0, 0)
                for u in (-1, 0, 1):
                    for v in (-1, 0, 1):
                        j = 3 * (u + 1) + v + 1
                        moved = conv_at(r, -u, -v)
                        total = total + moved * vec[6 + j : 7 + j]
                        taps[j] = taps[j] + fold(moved * start)
                g[here] = jnp.where(iota((PITCH, D), 0) < SIDE, total, 0.0).astype(BF)
            for j in range(9):
                add_row(s, 6 + j, taps[j])
            at_point("conv", 2 * s + i)

    at_point("vectors", 0)
    attention_start(0)
    route_bias()
    at_point("prepared", 0)
    for s in range(SECTIONS):
        at_point("weights", s)
        if s == 2:
            attention_start(s)
        (attention_forward, dense_forward)[s % 2](s)
    fin_ref[0] = dot(gather(), wide[...]).astype(BF).reshape(PATCHES, n, D)
    for s in reversed(range(SECTIONS)):
        (attention_backward, dense_backward)[s % 2](s)
    gin_ref[0] = dot(gather(), g[...]).astype(BF).reshape(PATCHES, n, D)


def layer_scratch(n):
    total = n * ROWS
    return [
        pltpu.VMEM((SECTIONS, total, D), BF),
        pltpu.VMEM((SECTIONS, total, D), F32),
        pltpu.VMEM((SECTIONS, total, 1), F32),
        pltpu.VMEM((SECTIONS, total, D), BF),
        pltpu.VMEM((2, total, HID), BF),
        pltpu.VMEM((2, n, LIVE, HEADS * ROWS), BF),
        pltpu.VMEM((2, total, D), BF),
        pltpu.VMEM((2, total, HID), BF),
        pltpu.VMEM((2, total, HID), F32),
        pltpu.VMEM((2, n, LIVE, ROWS), F32),
        pltpu.VMEM((total, D), F32),
        pltpu.VMEM((total, D), BF),
        pltpu.VMEM((total, HID), BF),
        pltpu.VMEM((LIVE + 2 * HALO, D), F32),
        pltpu.VMEM((LIVE + 2 * HALO, D), F32),
        pltpu.VMEM((LIVE + 2 * HALO, D), F32),
        pltpu.VMEM((HEADS * ROWS, LANES), BF),
        pltpu.VMEM((HEADS * ROWS, LANES), BF),
        pltpu.VMEM((LIVE, HEADS * ROWS), BF),
        pltpu.VMEM((D, ROWS), BF),
        pltpu.VMEM((D, ROWS), F32),
        pltpu.VMEM((ROWS, D), BF),
        pltpu.VMEM((total, D), BF),
    ]


def compute_kernel(n, *refs):
    x_ref, cot_ref, routes_ref, vec_ref, win_ref, wout_ref, fin_ref, gin_ref, gvec_ref, ga_ref, gb_ref, grad_ref = refs[:12]

    def at_point(name, s):
        if name != "grads":
            return
        for j in range(3):
            ga_ref[s, :, j * D : (j + 1) * D] = grad_ref[j]
            if s % 2 == 1 or j == 0:
                gb_ref[s, j * D : (j + 1) * D] = grad_ref[3 + j]
            else:
                gb_ref[s, j * D : (j + 1) * D] = jnp.zeros((D, D), F32)

    layers(
        n, at_point,
        x_ref, cot_ref, routes_ref, vec_ref, win_ref, wout_ref, fin_ref, gin_ref, gvec_ref, grad_ref, *refs[12:],
    )


def compute(x, cot, routes, vec, win, wout):
    n = x.shape[0]
    vmem = pl.BlockSpec(memory_space=pltpu.VMEM)
    by_token = jax.ShapeDtypeStruct((1, PATCHES, n, D), BF)
    fin, gin, gvec, ga, gb = pl.pallas_call(
        functools.partial(compute_kernel, n),
        out_shape=(
            by_token,
            by_token,
            jax.ShapeDtypeStruct((SECTIONS, VEC_ROWS, D), F32),
            jax.ShapeDtypeStruct((SECTIONS, D, HID), F32),
            jax.ShapeDtypeStruct((SECTIONS, HID, D), F32),
        ),
        in_specs=[vmem] * 6,
        out_specs=(vmem,) * 5,
        scratch_shapes=[pltpu.VMEM((6, BLOCK, BLOCK), F32)] + layer_scratch(n),
        compiler_params=pltpu.CompilerParams(vmem_limit_bytes=56 * 1024 * 1024),
        name="layers_alone",
    )(jnp.transpose(x, (1, 0, 2)), jnp.transpose(cot, (1, 0, 2)), jnp.swapaxes(routes, 2, 3), vec, win, wout)
    return jnp.transpose(fin, (0, 2, 1, 3)), jnp.transpose(gin, (0, 2, 1, 3)), gvec, ga, gb


MESH = pl.DeviceIdType.MESH
HALF = BLOCK // 2
PART = HALF // SECTIONS


def blocks_of(t):
    return 6 if t % 2 == 1 else 4


def shares_of(dp):
    chips = dp // 2
    near = min(chips, 4)
    split = min(near, 2)
    return near, PART // split, BLOCK // (near // split), (chips // near).bit_length() - 1


def whole_kernel(
    n, dp, images,
    inputs_ref, cot_in_ref, routes_in_ref, vec_own, win_own, wout_own,
    fin_ref, gin_ref, gvec_ref, ga_ref, gb_ref,
    x_ref, cot_ref, routes_ref, vec_ref, win_ref, wout_ref, gvec_part, grad_ref,
    own_half, send_half, got_half, half_sum, got_part, part_sum, got_near, share, got_far, result, vec_got, vec_sum, vec_mate, vec_near, vec_far,
    in_sem, w_send, w_recv, f_send, f_recv, v_send, v_recv, h_send, h_recv, p_send, p_recv, n_send, n_recv, d_send, d_recv,
    r_send, r_recv, m_send, m_recv, gv_send, gv_recv, gm_send, gm_recv, gn_send, gn_recv, gd_send, gd_recv,
    *scratch,
):
    me, j = lax.axis_index("section"), lax.axis_index("dp")
    core = lax.rem(j, 2)
    chip = j // 2
    near, piece_rows, piece_lanes, far_steps = shares_of(dp)
    place = lax.rem(chip, near)
    xor = lax.bitwise_xor

    def device(k, q, other=0):
        return (xor(me, k), xor(j, 2 * q + other))

    mate = device(0, 0, 1)
    sections = [device(k, 0) for k in range(1, SECTIONS)]
    around = [(k, q) for k in range(SECTIONS) for q in range(near) if (k, q) != (0, 0)]
    far = [(me, xor(j, 2 * near << b)) for b in range(far_steps)]
    waiting = []

    def remote(src, dst, send, recv, to):
        return pltpu.make_async_remote_copy(src, dst, send, recv, device_id=to, device_id_type=MESH)

    def when(condition, act):
        if condition is None:
            act()
        else:
            pl.when(condition)(act)

    def go(copy, condition=None):
        when(condition, lambda: copy.start())
        waiting.append((copy, condition))

    loads = [
        pltpu.make_async_copy(inputs_ref.at[me], x_ref, in_sem.at[0]),
        pltpu.make_async_copy(cot_in_ref.at[me], cot_ref, in_sem.at[1]),
        pltpu.make_async_copy(routes_in_ref.at[0, me], routes_ref.at[0], in_sem.at[2]),
        pltpu.make_async_copy(routes_in_ref.at[1, me], routes_ref.at[1], in_sem.at[3]),
        pltpu.make_async_copy(vec_own.at[0], vec_ref.at[me], in_sem.at[4]),
        pltpu.make_async_copy(win_own.at[0], win_ref.at[me], in_sem.at[5]),
        pltpu.make_async_copy(wout_own.at[0], wout_ref.at[me], in_sem.at[6]),
    ]
    for copy in loads:
        copy.start()

    barrier = pltpu.get_barrier_semaphore()
    everyone = [device(k, q) for k, q in around] + [mate] + far
    for to in everyone:
        pl.semaphore_signal(barrier, inc=1, device_id=to, device_id_type=MESH)
    pl.semaphore_wait(barrier, len(everyone))

    own_rows = pl.ds(pl.multiple_of(core * HALF, HALF), HALF)
    tail_rows = pl.ds(pl.multiple_of(D + core * D, D), D)
    pieces = [(win_own, win_ref, own_rows), (wout_own, wout_ref, own_rows), (wout_own, wout_ref, tail_rows)]

    def has(piece, t):
        return piece < 2 or t % 2 == 1

    odd = lax.rem(me, 2) == 1
    vec_copies = [remote(vec_own.at[0], vec_ref.at[me], v_send.at[k], v_recv.at[k], to) for k, to in enumerate(sections)]
    for copy in vec_copies:
        go(copy)
    for p, (source, target, rows) in enumerate(pieces):
        for k, to in enumerate(sections):
            go(remote(source.at[0, rows], target.at[me, rows], w_send.at[p, k], w_recv.at[p, me], to), None if p < 2 else odd)

    foreign = [me != t for t in range(SECTIONS)]
    hand_on, arrive = {}, {}
    for t in range(SECTIONS):
        for p in range(3):
            if has(p, t):
                spot = pieces[p][1].at[t, pieces[p][2]]
                arrive[t, p] = remote(spot, spot, w_send.at[p, 0], w_recv.at[p, t], mate)
                hand_on[t, p] = remote(spot, spot, f_send.at[p, t], f_recv.at[p, t], mate)
                waiting.append((hand_on[t, p], foreign[t]))

    def forward_weights(t, p):
        if has(p, t):

            @pl.when(foreign[t])
            def _():
                arrive[t, p].wait_recv()
                hand_on[t, p].start()

    def take_weights(t, p):
        if has(p, t):
            pl.when(foreign[t])(lambda: hand_on[t, p].wait_recv())

    other_rows = pl.ds(pl.multiple_of((1 - core) * HALF, HALF), HALF)

    def quarter(k):
        return pl.ds(pl.multiple_of(k * PART, PART), PART)

    def share_rows(q):
        return pl.multiple_of(lax.rem(q, PART // piece_rows) * piece_rows, piece_rows)

    def share_lanes(q):
        return pl.ds(pl.multiple_of((q // (PART // piece_rows)) * piece_lanes, piece_lanes), piece_lanes)

    def share_in_half(k, q):
        return pl.ds(pl.multiple_of(k * PART + share_rows(q), piece_rows), piece_rows), share_lanes(q)

    my_share = share_in_half(me, place)
    steps = {}

    def halves_start(t):
        count = blocks_of(t)
        blocks = pl.ds(0, count)
        for b in range(count):
            send_half[t, b] = grad_ref[b, other_rows].astype(BF)
        copy = remote(send_half.at[t, blocks], got_half.at[t, blocks], h_send.at[t], h_recv.at[t], mate)
        go(copy)
        for b in range(count):
            own_half[t, b] = grad_ref[b, own_rows].astype(BF)
        steps[t] = [copy]

    def halves_end(t):
        steps[t][0].wait_recv()
        for b in range(blocks_of(t)):
            half_sum[t, b] = (own_half[t, b].astype(F32) + got_half[t, b].astype(F32)).astype(BF)

    def parts_start(t):
        blocks = pl.ds(0, blocks_of(t))
        steps[t] = [
            remote(half_sum.at[t, blocks, quarter(to[0])], got_part.at[t, k, blocks], p_send.at[t, k], p_recv.at[t, k], to)
            for k, to in enumerate(sections)
        ]
        for copy in steps[t]:
            go(copy)

    def parts_end(t):
        for copy in steps[t]:
            copy.wait_recv()
        for b in range(blocks_of(t)):
            total = half_sum[t, b, quarter(me)].astype(F32)
            for k in range(SECTIONS - 1):
                total = total + got_part[t, k, b].astype(F32)
            part_sum[t, b] = total.astype(BF)

    def near_start(t):
        blocks = pl.ds(0, blocks_of(t))
        steps[t] = []
        for q in range(1, near):
            to_place = xor(place, q)
            source = part_sum.at[t, blocks, pl.ds(share_rows(to_place), piece_rows), share_lanes(to_place)]
            steps[t].append(remote(source, got_near.at[t, q, blocks], n_send.at[t, q], n_recv.at[t, q], device(0, q)))
        for copy in steps[t]:
            go(copy)

    def around_start(t):
        blocks = pl.ds(0, blocks_of(t))
        steps[t] = []
        for k, q in around:
            rows, lanes = share_in_half(xor(me, k), xor(place, q))
            slot = k * near + q
            source = half_sum.at[t, blocks, rows, lanes]
            steps[t].append(remote(source, got_near.at[t, slot, blocks], n_send.at[t, slot], n_recv.at[t, slot], device(k, q)))
        for copy in steps[t]:
            go(copy)

    def share_end(t, mine, slots):
        for copy in steps[t]:
            copy.wait_recv()
        for b in range(blocks_of(t)):
            total = mine(b).astype(F32)
            for slot in slots:
                total = total + got_near[t, slot, b].astype(F32)
            share[t, 0, b] = total.astype(BF)
        blocks = pl.ds(0, blocks_of(t))
        for step in range(far_steps):
            copy = remote(share.at[t, step, blocks], got_far.at[t, step, blocks], d_send.at[t, step], d_recv.at[t, step], far[step])
            go(copy)
            copy.wait_recv()
            for b in range(blocks_of(t)):
                share[t, step + 1, b] = (share[t, step, b].astype(F32) + got_far[t, step, b].astype(F32)).astype(BF)
        deliver(t)

    def near_end(t):
        rows = pl.ds(share_rows(place), piece_rows)
        share_end(t, lambda b: part_sum[t, b, rows, share_lanes(place)], range(1, near))

    def around_end(t):
        share_end(t, lambda b: half_sum[t, b, my_share[0], my_share[1]], [k * near + q for k, q in around])

    def deliver(t):
        blocks = pl.ds(0, blocks_of(t))
        last = share.at[t, far_steps, blocks]
        spot = result.at[blocks, core, my_share[0], my_share[1]]
        for q in range(near):
            to = (t, xor(j, 2 * q))
            go(remote(last, spot, r_send.at[t, q], r_recv.at[me, place], to), None if q > 0 else me != t)

        @pl.when(me == t)
        def _():
            for b in range(blocks_of(t)):
                result[b, core, my_share[0], my_share[1]] = share[t, far_steps, b]

    copies = {}

    def vectors_start():
        copies["sections"] = [
            remote(gvec_part.at[to[0]], vec_got.at[k], gv_send.at[k], gv_recv.at[k], to) for k, to in enumerate(sections)
        ]
        for copy in copies["sections"]:
            go(copy)

    def vectors_mate():
        for copy in copies["sections"]:
            copy.wait_recv()
        vec_sum[0] = gvec_part[me] + vec_got[0] + vec_got[1] + vec_got[2]
        copies["mate"] = remote(vec_sum.at[0], vec_mate, gm_send.at[0], gm_recv.at[0], mate)
        go(copies["mate"])

    def vectors_near():
        copies["mate"].wait_recv()
        vec_sum[1] = vec_sum[0] + vec_mate[...]
        copies["near"] = [remote(vec_sum.at[1], vec_near.at[q], gn_send.at[q], gn_recv.at[q], device(0, q)) for q in range(1, near)]
        for copy in copies["near"]:
            go(copy)

    def vectors_end():
        for copy in copies["near"]:
            copy.wait_recv()
        vec_near[0] = vec_sum[1]
        total = vec_near[place]
        for q in range(1, near):
            total = total + vec_near[xor(place, q)]
        vec_sum[2] = total
        for step in range(far_steps):
            copy = remote(vec_sum.at[2 + step], vec_far.at[step], gd_send.at[step], gd_recv.at[step], far[step])
            go(copy)
            copy.wait_recv()
            vec_sum[3 + step] = vec_sum[2 + step] + vec_far[step]
        gvec_ref[0] = vec_sum[2 + far_steps] * (1.0 / images)

    def on(act, *rest):
        return lambda: act(*rest)

    def inputs_here():
        for copy in loads[:4]:
            copy.wait()

    def vectors_here():
        for copy in vec_copies:
            copy.wait_recv()
        for copy in loads[4:]:
            copy.wait()

    plan = {
        ("inputs", 0): [inputs_here],
        ("vectors", 0): [vectors_here],
        ("prepared", 0): [on(forward_weights, 0, 0), on(forward_weights, 0, 1)],
    }
    for t in range(SECTIONS):
        plan["weights", t] = [on(take_weights, t, 0), on(take_weights, t, 1), on(take_weights, t, 2)]
        plan["next", t] = [on(forward_weights, t + 1, p) for p in range(3)] if t + 1 < SECTIONS else []
        plan["grads", t] = [on(halves_start, t)]
    plan["image", 6] = [on(halves_end, 3), on(parts_start, 3)]
    plan["image", 5] = [on(parts_end, 3), on(near_start, 3)]
    plan["norm", 4] = [on(halves_end, 2), on(parts_start, 2)]
    plan["image", 2] = [on(halves_end, 1), on(parts_start, 1)]
    plan["image", 3] = [on(near_end, 3)]
    plan["half", 0] = [on(parts_end, 2), on(near_start, 2)]
    plan["half", 1] = [on(parts_end, 1), on(near_start, 1)]
    plan["image", 1] = [on(near_end, 2)]
    plan["norm", 0] = [on(halves_end, 0), on(around_start, 0)]
    plan["conv", 1] = [vectors_start, on(near_end, 1)]
    done = []

    def at_point(name, s):
        for act in plan.get((name, s), []):
            act()
        done.append((name, s))

    layers(
        n, at_point,
        x_ref, cot_ref, routes_ref, vec_ref, win_ref, wout_ref, fin_ref, gin_ref, gvec_part, grad_ref, *scratch,
    )
    assert all(key in done or not plan[key] for key in plan)
    vectors_mate()
    vectors_near()
    around_end(0)
    vectors_end()

    for parity in range(2):
        blocks = pl.ds(0, blocks_of(parity))
        half = result.at[blocks, core]

        @pl.when(lax.rem(me, 2) == parity)
        def _():
            for k, q in around:
                from_me, from_place = xor(me, k), xor(place, q)
                rows, lanes = share_in_half(from_me, from_place)
                spot = result.at[blocks, core, rows, lanes]
                remote(spot, spot, r_send.at[0, 0], r_recv.at[from_me, from_place], mate).wait_recv()

        copy = remote(half, half, m_send.at[parity], m_recv.at[parity], mate)
        go(copy, lax.rem(me, 2) == parity)

    def finish(c):
        for b in range(3):
            rows = pl.ds(pl.multiple_of(c * HALF, HALF), HALF)
            ga_ref[0, rows, b * D : (b + 1) * D] = result[b, c].astype(F32) * (1.0 / images)
            gb_ref[0, pl.ds(pl.multiple_of(b * D + c * HALF, HALF), HALF)] = result[3 + b, c].astype(F32) * (1.0 / images)

    finish(core)
    for parity in range(2):
        half = result.at[pl.ds(0, blocks_of(parity)), 1 - core]
        pl.when(lax.rem(me, 2) == parity)(
            lambda half=half, parity=parity: remote(half, half, m_send.at[parity], m_recv.at[parity], mate).wait_recv()
        )
    finish(1 - core)

    @pl.when(lax.rem(me, 2) == 0)
    def _():
        gb_ref[0, D:HID] = jnp.zeros((HID - D, D), F32)

    for copy, condition in waiting:
        when(condition, lambda copy=copy: copy.wait_send())


def per_device(inputs, cotangent, routes, vectors, in_weight, out_weight):
    micro, n = inputs.shape[:2]
    dp = lax.axis_size("dp")
    near, piece_rows, piece_lanes, far_steps = shares_of(dp)
    images = micro * n * dp
    vmem = pl.BlockSpec(memory_space=pltpu.VMEM)
    hbm = pl.BlockSpec(memory_space=pl.ANY)
    dma = pltpu.SemaphoreType.DMA
    by_token = jax.ShapeDtypeStruct((1, PATCHES, n, D), BF)
    some = max(far_steps, 1)

    def grad_buffer(*shape):
        return pltpu.VMEM((SECTIONS,) + shape, BF)

    fin, gin, gvec, ga, gb = pl.pallas_call(
        functools.partial(whole_kernel, n, dp, images),
        out_shape=(
            by_token,
            by_token,
            jax.ShapeDtypeStruct((1, VEC_ROWS, D), F32),
            jax.ShapeDtypeStruct((1, D, HID), F32),
            jax.ShapeDtypeStruct((1, HID, D), F32),
        ),
        in_specs=[hbm] * 6,
        out_specs=(vmem,) * 5,
        scratch_shapes=[
            pltpu.VMEM((PATCHES, n, D), BF),
            pltpu.VMEM((PATCHES, n, D), BF),
            pltpu.VMEM((2, n, TOPK, REGIONS), jnp.int32),
            pltpu.VMEM((SECTIONS, VEC_ROWS, D), F32),
            pltpu.VMEM((SECTIONS, D, HID), BF),
            pltpu.VMEM((SECTIONS, HID, D), BF),
            pltpu.VMEM((SECTIONS, VEC_ROWS, D), F32),
            pltpu.VMEM((6, BLOCK, BLOCK), F32),
            grad_buffer(6, HALF, BLOCK),
            grad_buffer(6, HALF, BLOCK),
            grad_buffer(6, HALF, BLOCK),
            grad_buffer(6, HALF, BLOCK),
            grad_buffer(3, 6, PART, BLOCK),
            grad_buffer(6, PART, BLOCK),
            grad_buffer(SECTIONS * near, 6, piece_rows, piece_lanes),
            grad_buffer(far_steps + 1, 6, piece_rows, piece_lanes),
            grad_buffer(some, 6, piece_rows, piece_lanes),
            pltpu.VMEM((6, 2, HALF, BLOCK), BF),
            pltpu.VMEM((3, VEC_ROWS, D), F32),
            pltpu.VMEM((3 + far_steps, VEC_ROWS, D), F32),
            pltpu.VMEM((VEC_ROWS, D), F32),
            pltpu.VMEM((near, VEC_ROWS, D), F32),
            pltpu.VMEM((some, VEC_ROWS, D), F32),
            dma((7,)),
            dma((3, 3)), dma((3, SECTIONS)),
            dma((3, SECTIONS)), dma((3, SECTIONS)),
            dma((3,)), dma((3,)),
            dma((SECTIONS,)), dma((SECTIONS,)),
            dma((SECTIONS, 3)), dma((SECTIONS, 3)),
            dma((SECTIONS, SECTIONS * near)), dma((SECTIONS, SECTIONS * near)),
            dma((SECTIONS, some)), dma((SECTIONS, some)),
            dma((SECTIONS, near)), dma((SECTIONS, near)),
            dma((2,)), dma((2,)),
            dma((3,)), dma((3,)),
            dma((1,)), dma((1,)),
            dma((near,)), dma((near,)),
            dma((some,)), dma((some,)),
        ]
        + layer_scratch(n),
        compiler_params=pltpu.CompilerParams(
            vmem_limit_bytes=60 * 1024 * 1024, collective_id=0, has_side_effects=True
        ),
        name="two_layers",
    )(
        jnp.transpose(inputs, (0, 2, 1, 3)),
        jnp.transpose(cotangent, (0, 2, 1, 3)),
        jnp.swapaxes(routes, 3, 4),
        vectors,
        in_weight,
        out_weight,
    )
    return jnp.transpose(fin, (0, 2, 1, 3)), jnp.transpose(gin, (0, 2, 1, 3)), gvec, ga, gb


def solution(mesh):
    in_specs = (
        P(None, "dp", None, None),
        P(None, "dp", None, None),
        P(None, None, "dp", None, None),
        P("section", None, None),
        P("section", None, None),
        P("section", None, None),
    )
    out_specs = (
        P("section", "dp", None, None),
        P("section", "dp", None, None),
        P("section", None, None),
        P("section", None, None),
        P("section", None, None),
    )
    return jax.shard_map(
        per_device, mesh=mesh, in_specs=in_specs, out_specs=out_specs, check_vma=False
    )
```

```python
import functools

import jax
import jax.numpy as jnp
from jax import lax
from jax.experimental import pallas as pl
from jax.experimental.pallas import tpu as pltpu
from jax.sharding import PartitionSpec as P

D = 256
HEADS = 8
HEAD_DIM = 32
HID = 768
SIDE = 14
WIN = 7
TOPK = 4
SECTIONS = 4
VEC_ROWS = 16
PATCHES = 196
REGIONS = 49
BLOCK = 256
EPSILON = 1e-06

PITCH = 16
LIVE = SIDE * PITCH
ROWS = 256
HALO = 24
CHUNK = 32
LANES = 128
NEGATIVE = -1e30
LOG2E = 1.4426950408889634
SCALE = HEAD_DIM ** (-0.5)

BF = jnp.bfloat16
F32 = jnp.float32


def dot(a, b, ca=1, cb=0):
    return lax.dot_general(
        a, b, (((ca,), (cb,)), ((), ())), preferred_element_type=jnp.float32
    )


def iota(shape, dim):
    return lax.broadcasted_iota(jnp.int32, shape, dim)


def one_hot(cond):
    return jnp.where(cond, 1.0, 0.0).astype(BF)


def rows_of(i, count=LIVE):
    return pl.ds(pl.multiple_of(i * ROWS, ROWS), count)


def col_sum(x):
    return jnp.sum(x, axis=0, keepdims=True)


def ln_stats(x):
    average = jnp.mean(x, axis=-1, keepdims=True)
    centred = x - average
    spread = jnp.mean(centred * centred, axis=-1, keepdims=True)
    inverse = lax.rsqrt(spread + EPSILON)
    return centred * inverse, inverse


def gelu_pair(x):
    a = jnp.abs(x)
    t = 1.0 / (1.0 + a * (0.3275911 * 0.7071067811865476))
    e = jnp.exp2(x * x * (-0.5 * LOG2E))
    w = t * (0.5 * 1.061405429) + (0.5 * -1.453152027)
    w = w * t + (0.5 * 1.421413741)
    w = w * t + (0.5 * -0.284496736)
    w = w * t + (0.5 * 0.254829592)
    w = w * t * e
    phi = jnp.where(x >= 0, 1.0 - w, w)
    return x * phi, phi + x * e * 0.3989422804014327


def region_one_hot(shape, token_dim):
    token = iota(shape, token_dim)
    region = iota(shape, 1 - token_dim)
    r, c = token >> 4, token & (PITCH - 1)
    own = (r >> 1) * WIN + (c >> 1)
    return one_hot((own == region) & (c < SIDE) & (r < SIDE))


def weight_grads(scratch, s, first, count, half):
    nm, at, act, g, dproj = (scratch[LAYER_SCRATCH.index(name)] for name in ("nm", "at", "act", "g", "dproj"))
    results = []
    ins = min(first + count, 3) - first
    if ins > 0:
        lanes = pl.ds(pl.multiple_of(half * LANES, LANES), LANES)
        wide = dot(nm[s, :, lanes], dproj[:, first * D : (first + ins) * D], 0, 0)
        results += [wide[:, b * D : (b + 1) * D] for b in range(ins)]
    for b in range(max(first, 3) - 3, first + count - 3):
        lanes = pl.ds(pl.multiple_of(b * D + half * LANES, LANES), LANES)
        left = act[s // 2, :, lanes] if s % 2 == 1 else at[s // 2, :, lanes]
        results.append(dot(left, g[...], 0, 0))
    return results


LAYER_SCRATCH = (
    "hs", "zh", "inv", "nm", "pr", "pt", "at", "act", "gp", "bias", "mixed", "g", "dproj", "cv", "cvl", "cvr",
    "dom", "qm", "dsb", "tmp", "dqt", "km", "wide",
)


def layers(
    n, at_point,
    x_ref, cot_ref, routes_ref, vec_ref, win_ref, wout_ref, fin_ref, gin_ref, gvec_ref,
    hs, zh, inv, nm, pr, pt, at, act, gp, bias, mixed, g, dproj, cv, cvl, cvr, dom, qm, dsb, tmp, dqt, km, wide,
):
    pairs = PATCHES * n

    def eye():
        return one_hot(iota((ROWS, ROWS), 0) == iota((ROWS, ROWS), 1))

    def transposed(x):
        return dot(eye(), x, 1, 1)

    def spread(i):
        t, p = iota((ROWS, pairs), 0), iota((ROWS, pairs), 1)
        r, c = t >> 4, t & (PITCH - 1)
        return one_hot((p == (r * SIDE + c) * n + i) & (c < SIDE) & (r < SIDE))

    def gather():
        p, t = iota((pairs, n * ROWS), 0), iota((pairs, n * ROWS), 1)
        r, c, i = (t & (ROWS - 1)) >> 4, t & (PITCH - 1), t >> 8
        return one_hot((p == (r * SIDE + c) * n + i) & (c < SIDE) & (r < SIDE))

    def chunks():
        return [slice(c, c + CHUNK) for c in range(0, LIVE, CHUNK)]

    def rows_at(i, c, count):
        return pl.ds(pl.multiple_of(i * ROWS + c, PITCH), count)

    def tail(i):
        return pl.ds(i * ROWS + LIVE, ROWS - LIVE)

    none = jnp.zeros((ROWS - LIVE, D), BF)
    none_wide = jnp.zeros((ROWS - LIVE, HID), BF)
    halo = jnp.zeros((HALO, D), F32)
    for buffer in (cv, cvl, cvr):
        buffer[0:HALO] = halo
        buffer[HALO + LIVE : HALO + LIVE + HALO] = halo
    for i in range(n):
        for s in range(SECTIONS):
            nm[s, tail(i)] = none
            hs[s, tail(i)] = none
        for a in range(2):
            pr[a, tail(i)] = none_wide
            act[a, tail(i)] = none_wide
            at[a, tail(i)] = none
        wide[tail(i)] = none
        dproj[tail(i)] = none_wide
    gvec_ref[...] = jnp.zeros_like(gvec_ref)

    at_point("inputs", 0)
    x_pairs = x_ref[...].reshape(pairs, D)
    cot_pairs = cot_ref[...].reshape(pairs, D)
    for i in range(n):
        spread_i = spread(i)
        hs[0, pl.ds(i * ROWS, ROWS)] = dot(spread_i, x_pairs).astype(BF)
        g[pl.ds(i * ROWS, ROWS)] = dot(spread_i, cot_pairs).astype(BF)

    def conv_load(r0, count, x):
        cv[pl.ds(HALO + r0, count)] = x

    def conv_shift():
        for rows in chunks():
            cvl[HALO + rows.start : HALO + rows.stop] = cv[HALO + rows.start - 1 : HALO + rows.stop - 1]
            cvr[HALO + rows.start : HALO + rows.stop] = cv[HALO + rows.start + 1 : HALO + rows.stop + 1]

    def conv_at(r, u, v):
        start = HALO + (r + u) * PITCH
        return (cvl, cv, cvr)[v + 1][start : start + PITCH]

    def attention_start(s):
        vec = vec_ref.at[s]

        def image(i, carry):
            for rows in chunks():
                conv_load(rows.start, CHUNK, hs[s, rows_at(i, rows.start, CHUNK)].astype(F32))
            conv_shift()
            for r in range(SIDE):
                total = conv_at(r, 0, 0) + vec[15:16]
                for u in (-1, 0, 1):
                    for v in (-1, 0, 1):
                        j = 6 + 3 * (u + 1) + v + 1
                        total = total + conv_at(r, u, v) * vec[j : j + 1]
                here = rows_at(i, r * PITCH, PITCH)
                mixed[here] = total
                hat, inverse = ln_stats(total)
                zh[s, here] = hat
                inv[s, here] = inverse
                nm[s, here] = (hat * vec[0:1] + vec[1:2]).astype(BF)
            return carry

        lax.fori_loop(0, n, image, 0)

    def route_bias():
        key_region = region_one_hot((LIVE, REGIONS), 0)
        query_region = region_one_hot((REGIONS, ROWS), 1)
        for i in range(n):
            for a in range(2):
                picks = routes_ref[a, i]
                region = iota((REGIONS, REGIONS), 0)
                routed = jnp.zeros((REGIONS, REGIONS), F32)
                for k in range(TOPK):
                    routed = routed + jnp.where(picks[k : k + 1] == region, 1.0, 0.0)
                by_region = dot(key_region, routed.astype(BF)).astype(BF)
                bias[a, i] = (1.0 - dot(by_region, query_region)) * NEGATIVE

    def half_of(h):
        return slice((h // 4) * LANES, (h // 4 + 1) * LANES)

    def own_lanes(h, count):
        return (iota((count, LANES), 1) >> 5) == h % 4

    def attention_forward(s):
        a = s // 2
        vec = vec_ref.at[s]

        def image(i, carry):
            rows = rows_of(i)
            whole = rows_of(i, ROWS)
            pr[a, rows] = dot(nm[s, rows], win_ref[s]).astype(BF)
            tmp[...] = transposed(pr[a, whole, 2 * D : 3 * D]).astype(BF)
            for h in range(HEADS):
                lanes = half_of(h)
                keys = jnp.where(own_lanes(h, LIVE), pr[a, rows, slice(D + lanes.start, D + lanes.stop)], jnp.zeros((), BF))
                scores = dot(keys, pr[a, whole, lanes], 1, 1) * (SCALE * LOG2E) + bias[a, i]
                expo = jnp.exp2(scores - jnp.max(scores, axis=0, keepdims=True))
                pt[a, i, :, h * ROWS : (h + 1) * ROWS] = (expo * (1.0 / col_sum(expo))).astype(BF)
            pl.when(i == 0)(lambda: at_point("scores", s))
            for h in range(HEADS):
                own = slice(h * HEAD_DIM, (h + 1) * HEAD_DIM)
                dqt[own] = dot(tmp[own, 0:LIVE], pt[a, i, :, h * ROWS : (h + 1) * ROWS])
            attended = transposed(dqt[...].astype(BF)).astype(BF)
            at[a, whole] = attended
            pl.when(i == 0)(lambda: at_point("out", s))
            out = mixed[rows] + dot(attended[:LIVE], wout_ref[s, 0:D]) + vec[2:3]
            hs[s + 1, rows] = out.astype(BF)
            return carry

        lax.fori_loop(0, n, image, 0)

    def dense_forward(s):
        a = s // 2
        vec = vec_ref.at[s]
        token = iota((CHUNK, D), 0)

        def image(i, carry):
            rows = rows_of(i)
            for part in chunks():
                here = rows_at(i, part.start, CHUNK)
                hat, inverse = ln_stats(hs[s, here].astype(F32))
                zh[s, here] = hat
                inv[s, here] = inverse
                nm[s, here] = (hat * vec[0:1] + vec[1:2]).astype(BF)
            for j in range(3):
                lanes = slice(j * D, (j + 1) * D)
                hidden = dot(nm[s, rows], win_ref[s, :, lanes]) + vec[3 + j : 4 + j]
                value, slope = gelu_pair(hidden)
                act[a, rows, lanes] = value.astype(BF)
                gp[a, rows, lanes] = slope
            pl.when(i == 0)(lambda: at_point("out", s))
            out = hs[s, rows].astype(F32) + dot(act[a, rows], wout_ref[s]) + vec[2:3]
            if s + 1 < SECTIONS:
                live = (iota((LIVE, D), 0) & (PITCH - 1)) < SIDE
                hs[s + 1, rows] = jnp.where(live, out, 0.0).astype(BF)
            else:
                wide[rows] = out.astype(BF)
            return carry

        lax.fori_loop(0, n, image, 0)

    def norm_backward(s, here, d_normed, sums):
        vec = vec_ref.at[s]
        hat = zh[s, here]
        product = d_normed * hat
        scaled = d_normed * vec[0:1]
        first = jnp.mean(scaled, axis=-1, keepdims=True)
        second = jnp.mean(product * vec[0:1], axis=-1, keepdims=True)
        sums[0] = sums[0] + fold(product)
        sums[1] = sums[1] + fold(d_normed)
        return inv[s, here] * (scaled - first - hat * second)

    def fold(x):
        return jnp.sum(x.reshape(x.shape[0] // 8, 8, x.shape[1]), axis=0)

    def empty():
        return jnp.zeros((8, D), F32)

    def add_row(s, row, total):
        gvec_ref[s, row : row + 1] += col_sum(total)

    def dense_backward(s):
        a = s // 2
        at_point("first grads", s)
        for i in range(n):
            rows = rows_of(i)
            for j in range(3):
                lanes = slice(j * D, (j + 1) * D)
                d_active = dot(g[rows], wout_ref[s, lanes], 1, 1)
                d_hidden = (d_active * gp[a, rows, lanes]).astype(BF)
                dproj[rows, lanes] = d_hidden
                add_row(s, 3 + j, fold(d_hidden.astype(F32)))
        at_point("grads", s)
        for i in range(n):
            rows = rows_of(i)
            d_normed = dot(dproj[rows], win_ref[s], 1, 1)
            sums = [empty(), empty(), empty()]
            for part in chunks():
                here = rows_at(i, part.start, CHUNK)
                grad = g[here].astype(F32)
                sums[2] = sums[2] + fold(grad)
                out = grad + norm_backward(s, here, d_normed[part], sums)
                g[here] = out.astype(BF)
            for row in range(3):
                add_row(s, row, sums[row])
            at_point("image", 2 * s + i)

    def attention_backward(s):
        a = s // 2
        vec = vec_ref.at[s]
        nothing = jnp.zeros((), BF)
        for i in range(n):
            rows = rows_of(i)
            whole = rows_of(i, ROWS)
            km[whole] = dot(g[whole], wout_ref[s, 0:D], 1, 1).astype(BF)
            for h in range(HEADS):
                dom[h * ROWS : (h + 1) * ROWS] = jnp.where(own_lanes(h, ROWS), km[whole, half_of(h)], nothing)
            for half in range(2):
                lanes = slice(2 * D + half * LANES, 2 * D + (half + 1) * LANES)
                four = slice(half * 4 * ROWS, (half + 1) * 4 * ROWS)
                dproj[rows, lanes] = dot(pt[a, i, :, four], dom[four]).astype(BF)
        at_point("first grads", s)
        for i in range(n):
            rows = rows_of(i)
            whole = rows_of(i, ROWS)
            tmp[...] = transposed(pr[a, whole, D : 2 * D]).astype(BF)
            for h in range(HEADS):
                qm[h * ROWS : (h + 1) * ROWS] = jnp.where(own_lanes(h, ROWS), pr[a, whole, half_of(h)], nothing)
            for h in range(HEADS):
                lanes = half_of(h)
                row = slice(h * ROWS, (h + 1) * ROWS)
                values = jnp.where(own_lanes(h, LIVE), pr[a, rows, slice(2 * D + lanes.start, 2 * D + lanes.stop)], nothing)
                d_weights = dot(values, km[whole, lanes], 1, 1)
                weights = pt[a, i, :, row].astype(F32)
                dsb[:, row] = (weights * (d_weights - col_sum(weights * d_weights))).astype(BF)
                if h == 3:
                    at_point("half", 2 * s + i)
            for h in range(HEADS):
                own = slice(h * HEAD_DIM, (h + 1) * HEAD_DIM)
                dqt[own] = dot(tmp[own, 0:LIVE], dsb[:, h * ROWS : (h + 1) * ROWS])
            for half in range(2):
                lanes = slice(D + half * LANES, D + (half + 1) * LANES)
                four = slice(half * 4 * ROWS, (half + 1) * 4 * ROWS)
                dproj[rows, lanes] = (dot(dsb[:, four], qm[four]) * SCALE).astype(BF)
            dproj[rows, 0:D] = (transposed(dqt[...].astype(BF))[:LIVE] * SCALE).astype(BF)
            at_point("image", 2 * s + i)
        at_point("grads", s)
        for i in range(n):
            rows = rows_of(i)
            d_normed = dot(dproj[rows], win_ref[s], 1, 1)
            sums = [empty(), empty(), empty(), empty()]
            for part in chunks():
                here = rows_at(i, part.start, CHUNK)
                grad = g[here].astype(F32)
                sums[2] = sums[2] + fold(grad)
                d_mixed = grad + norm_backward(s, here, d_normed[part], sums)
                sums[3] = sums[3] + fold(d_mixed)
                conv_load(part.start, CHUNK, d_mixed)
            for row, total in zip((0, 1, 2, 15), sums):
                add_row(s, row, total)
            at_point("norm", 2 * s + i)
            conv_shift()
            taps = [empty() for _ in range(9)]
            for r in range(SIDE):
                here = rows_at(i, r * PITCH, PITCH)
                start = hs[s, here].astype(F32)
                total = conv_at(r, 0, 0)
                for u in (-1, 0, 1):
                    for v in (-1, 0, 1):
                        j = 3 * (u + 1) + v + 1
                        moved = conv_at(r, -u, -v)
                        total = total + moved * vec[6 + j : 7 + j]
                        taps[j] = taps[j] + fold(moved * start)
                g[here] = jnp.where(iota((PITCH, D), 0) < SIDE, total, 0.0).astype(BF)
            for j in range(9):
                add_row(s, 6 + j, taps[j])
            at_point("conv", 2 * s + i)

    at_point("vectors", 0)
    attention_start(0)
    route_bias()
    at_point("prepared", 0)
    for s in range(SECTIONS):
        at_point("weights", s)
        if s == 2:
            attention_start(s)
        (attention_forward, dense_forward)[s % 2](s)
    fin_ref[...] = dot(gather(), wide[...]).astype(BF).reshape(PATCHES, n, D)
    for s in reversed(range(SECTIONS)):
        (attention_backward, dense_backward)[s % 2](s)
    gin_ref[...] = dot(gather(), g[...]).astype(BF).reshape(PATCHES, n, D)


def layer_scratch(n):
    total = n * ROWS
    return [
        pltpu.VMEM((SECTIONS, total, D), BF),
        pltpu.VMEM((SECTIONS, total, D), F32),
        pltpu.VMEM((SECTIONS, total, 1), F32),
        pltpu.VMEM((SECTIONS, total, D), BF),
        pltpu.VMEM((2, total, HID), BF),
        pltpu.VMEM((2, n, LIVE, HEADS * ROWS), BF),
        pltpu.VMEM((2, total, D), BF),
        pltpu.VMEM((2, total, HID), BF),
        pltpu.VMEM((2, total, HID), F32),
        pltpu.VMEM((2, n, LIVE, ROWS), F32),
        pltpu.VMEM((total, D), F32),
        pltpu.VMEM((total, D), BF),
        pltpu.VMEM((total, HID), BF),
        pltpu.VMEM((LIVE + 2 * HALO, D), F32),
        pltpu.VMEM((LIVE + 2 * HALO, D), F32),
        pltpu.VMEM((LIVE + 2 * HALO, D), F32),
        pltpu.VMEM((HEADS * ROWS, LANES), BF),
        pltpu.VMEM((HEADS * ROWS, LANES), BF),
        pltpu.VMEM((LIVE, HEADS * ROWS), BF),
        pltpu.VMEM((D, ROWS), BF),
        pltpu.VMEM((D, ROWS), F32),
        pltpu.VMEM((total, D), BF),
        pltpu.VMEM((total, D), BF),
    ]


def compute_kernel(n, *refs):
    x_ref, cot_ref, routes_ref, vec_ref, win_ref, wout_ref, fin_ref, gin_ref, gvec_ref, ga_ref, gb_ref = refs[:11]

    def at_point(name, s):
        if name != "grads":
            return
        count = 6 if s % 2 == 1 else 4
        for half in range(2):
            for b, value in enumerate(weight_grads(refs[11:], s, 0, count, half)):
                rows = slice(half * LANES, (half + 1) * LANES)
                if b < 3:
                    ga_ref[s, rows, b * D : (b + 1) * D] = value
                else:
                    gb_ref[s, (b - 3) * D + half * LANES : (b - 3) * D + (half + 1) * LANES] = value
        if s % 2 == 0:
            gb_ref[s, D:HID] = jnp.zeros((HID - D, D), F32)

    layers(n, at_point, x_ref, cot_ref, routes_ref, vec_ref, win_ref, wout_ref, fin_ref.at[0], gin_ref.at[0], gvec_ref, *refs[11:])


def compute(x, cot, routes, vec, win, wout):
    n = x.shape[0]
    vmem = pl.BlockSpec(memory_space=pltpu.VMEM)
    by_token = jax.ShapeDtypeStruct((1, PATCHES, n, D), BF)
    fin, gin, gvec, ga, gb = pl.pallas_call(
        functools.partial(compute_kernel, n),
        out_shape=(
            by_token,
            by_token,
            jax.ShapeDtypeStruct((SECTIONS, VEC_ROWS, D), F32),
            jax.ShapeDtypeStruct((SECTIONS, D, HID), F32),
            jax.ShapeDtypeStruct((SECTIONS, HID, D), F32),
        ),
        in_specs=[vmem] * 6,
        out_specs=(vmem,) * 5,
        scratch_shapes=layer_scratch(n),
        compiler_params=pltpu.CompilerParams(vmem_limit_bytes=56 * 1024 * 1024),
        name="layers_alone",
    )(jnp.transpose(x, (1, 0, 2)), jnp.transpose(cot, (1, 0, 2)), jnp.swapaxes(routes, 2, 3), vec, win, wout)
    return jnp.transpose(fin, (0, 2, 1, 3)), jnp.transpose(gin, (0, 2, 1, 3)), gvec, ga, gb


MESH = pl.DeviceIdType.MESH
HALF = BLOCK // 2
PART = HALF // SECTIONS


def blocks_of(t):
    return 6 if t % 2 == 1 else 4


GROUPS = ((0, 0, 2), (1, 0, 6), (2, 0, 4), (3, 0, 6), (0, 2, 2))


def shares_of(dp):
    chips = dp // 2
    near = min(chips, 4)
    split = min(near, 2)
    return near, PART // split, BLOCK // (near // split), (chips // near).bit_length() - 1


def piece_slices(dp, piece):
    near, piece_rows, piece_lanes, _ = shares_of(dp)
    k, q = piece // near, piece % near
    rows = k * PART + q % (PART // piece_rows) * piece_rows
    lanes = q // (PART // piece_rows) * piece_lanes
    return slice(rows, rows + piece_rows), slice(lanes, lanes + piece_lanes)


def results_kernel(dp, images, fin_in, gin_in, gvec_in, result, fin_ref, gin_ref, gvec_ref, ga_ref, gb_ref, ga, gb, sems):
    copies = [
        pltpu.make_async_copy(fin_in, fin_ref.at[0], sems.at[0]),
        pltpu.make_async_copy(gin_in, gin_ref.at[0], sems.at[1]),
        pltpu.make_async_copy(ga, ga_ref.at[0], sems.at[2]),
        pltpu.make_async_copy(gb, gb_ref.at[0], sems.at[3]),
    ]
    copies[0].start()
    copies[1].start()
    gvec_ref[0] = gvec_in[...] * (1.0 / images)
    for target, first in ((ga, 0), (gb, 3)):
        for c in range(2):
            for piece in range(result.shape[1]):
                rows, lanes = piece_slices(dp, piece)
                for b in range(3):
                    value = result[c, piece, first + b].astype(F32) * (1.0 / images)
                    start = c * HALF + rows.start
                    if first == 0:
                        target[start : start + rows.stop - rows.start, b * D + lanes.start : b * D + lanes.stop] = value
                    else:
                        target[b * D + start : b * D + start + rows.stop - rows.start, lanes] = value
        if first == 0:
            copies[2].start()

    @pl.when(lax.rem(lax.axis_index("section"), 2) == 0)
    def _():
        gb[D:HID] = jnp.zeros((HID - D, D), F32)

    copies[3].start()
    for copy in copies:
        copy.wait()


def whole_kernel(
    n, dp, images,
    inputs_ref, cot_in_ref, routes_in_ref, vec_own, win_own, wout_own,
    fin_ref, gin_ref, gvec_ref, result,
    x_ref, cot_ref, routes_ref, vec_ref, win_ref, wout_ref, gvec_part,
    own_half, send_half, got_half, half_sum, got_part, part_sum, got_near, share, got_far, vec_got, vec_sum, vec_mate, vec_near, vec_far,
    in_sem, w_send, w_recv, f_send, f_recv, v_send, v_recv, h_send, h_recv, p_send, p_recv, n_send, n_recv, d_send, d_recv,
    r_send, r_recv, m_send, m_recv, gv_send, gv_recv, gm_send, gm_recv, gn_send, gn_recv, gd_send, gd_recv,
    *scratch,
):
    me, j = lax.axis_index("section"), lax.axis_index("dp")
    core = lax.rem(j, 2)
    chip = j // 2
    near, piece_rows, piece_lanes, far_steps = shares_of(dp)
    place = lax.rem(chip, near)
    xor = lax.bitwise_xor

    def device(k, q, other=0):
        return (xor(me, k), xor(j, 2 * q + other))

    mate = device(0, 0, 1)
    sections = [device(k, 0) for k in range(1, SECTIONS)]
    around = [(k, q) for k in range(SECTIONS) for q in range(near) if (k, q) != (0, 0)]
    far = [(me, xor(j, 2 * near << b)) for b in range(far_steps)]
    waiting = []

    def remote(src, dst, send, recv, to):
        return pltpu.make_async_remote_copy(src, dst, send, recv, device_id=to, device_id_type=MESH)

    def when(condition, act):
        if condition is None:
            act()
        else:
            pl.when(condition)(act)

    def go(copy, condition=None):
        when(condition, lambda: copy.start())
        waiting.append((copy, condition))

    loads = [
        pltpu.make_async_copy(inputs_ref.at[me], x_ref, in_sem.at[0]),
        pltpu.make_async_copy(cot_in_ref.at[me], cot_ref, in_sem.at[1]),
        pltpu.make_async_copy(routes_in_ref.at[0, me], routes_ref.at[0], in_sem.at[2]),
        pltpu.make_async_copy(routes_in_ref.at[1, me], routes_ref.at[1], in_sem.at[3]),
        pltpu.make_async_copy(vec_own.at[0], vec_ref.at[me], in_sem.at[4]),
        pltpu.make_async_copy(win_own.at[0], win_ref.at[me], in_sem.at[5]),
        pltpu.make_async_copy(wout_own.at[0], wout_ref.at[me], in_sem.at[6]),
    ]
    for copy in loads:
        copy.start()

    barrier = pltpu.get_barrier_semaphore()
    everyone = [device(k, q) for k, q in around] + [mate] + far
    for to in everyone:
        pl.semaphore_signal(barrier, inc=1, device_id=to, device_id_type=MESH)
    pl.semaphore_wait(barrier, len(everyone))

    own_rows = pl.ds(pl.multiple_of(core * HALF, HALF), HALF)
    tail_rows = pl.ds(pl.multiple_of(D + core * D, D), D)
    pieces = [(win_own, win_ref, own_rows), (wout_own, wout_ref, own_rows), (wout_own, wout_ref, tail_rows)]

    def spot(p, t):
        return pieces[p][1].at[t, pieces[p][2]]

    def odd(t):
        return lax.rem(t, 2) == 1

    vec_copies = [remote(vec_own.at[0], vec_ref.at[me], v_send.at[k], v_recv.at[k], to) for k, to in enumerate(sections)]
    out_copies = [
        [
            remote(source.at[0, rows], target.at[me, rows], w_send.at[p, k - 1], w_recv.at[p, me], device(k, 0))
            for k in (1, 2)
        ]
        for p, (source, target, rows) in enumerate(pieces)
    ]
    relayed, relay_to = xor(me, 1 + core), xor(me, 2 - core)
    relays = [remote(spot(p, relayed), spot(p, relayed), w_send.at[p, 2], w_recv.at[p, relayed], (relay_to, j)) for p in range(3)]
    arrivals, handings, takings = {}, {}, {}
    for p in range(3):
        for k in (1, 2, 3):
            t = xor(me, k)
            arrivals[p, k] = remote(spot(p, t), spot(p, t), w_send.at[p, 0], w_recv.at[p, t], mate)
            handings[p, k] = remote(spot(p, t), spot(p, t), f_send.at[p, t], f_recv.at[p, t], mate)
        for t in range(SECTIONS):
            if p < 2 or t % 2 == 1:
                takings[p, t] = remote(spot(p, t), spot(p, t), f_send.at[p, t], f_recv.at[p, t], mate)
    foreign = [me != t for t in range(SECTIONS)]

    def send_weights(p):
        for copy in out_copies[p]:
            go(copy, odd(me) if p == 2 else None)

    def pass_on(p, ks):
        for k in ks:
            condition = odd(xor(me, k)) if p == 2 else None
            when(condition, lambda: arrivals[p, k].wait_recv())
        if ks != (3,):
            go(relays[p], odd(relayed) if p == 2 else None)
        for k in ks:
            go(handings[p, k], odd(xor(me, k)) if p == 2 else None)

    def take_weights(t, p):
        if p < 2 or t % 2 == 1:
            pl.when(foreign[t])(lambda: takings[p, t].wait_recv())

    for copy in vec_copies:
        go(copy)
    send_weights(0)


    def piece_of(k, q):
        return k * near + q

    def quarter(k):
        return pl.ds(pl.multiple_of(k * near, near), near)

    mine = piece_of(me, place)
    steps = {}

    def halves_start(t):
        section, first, count = GROUPS[t]
        for b, value in enumerate(weight_grads(scratch, section, first, count, 1 - core)):
            send_half[t][b] = value.astype(BF)
        copy = remote(send_half[t], got_half[t], h_send.at[t], h_recv.at[t], mate)
        go(copy)
        for b, value in enumerate(weight_grads(scratch, section, first, count, core)):
            own_half[t][b] = value.astype(BF)
        steps[t] = [copy]

    def halves_end(t):
        steps[t][0].wait_recv()
        for b in range(GROUPS[t][2]):
            total = own_half[t][b] + got_half[t][b]
            for piece in range(SECTIONS * near):
                rows, lanes = piece_slices(dp, piece)
                half_sum[t][piece, b] = total[rows, lanes]

    def parts_start(t):
        steps[t] = [
            remote(half_sum[t].at[quarter(to[0])], got_part[t].at[k], p_send.at[t, k], p_recv.at[t, k], to)
            for k, to in enumerate(sections)
        ]
        for copy in steps[t]:
            go(copy)

    def parts_end(t):
        for copy in steps[t]:
            copy.wait_recv()
        for q in range(near):
            for b in range(GROUPS[t][2]):
                total = half_sum[t][piece_of(me, q), b].astype(F32)
                for k in range(SECTIONS - 1):
                    total = total + got_part[t][k, q, b].astype(F32)
                part_sum[t][q, b] = total.astype(BF)

    def near_start(t):
        steps[t] = []
        for q in range(1, near):
            to_place = xor(place, q)
            source = part_sum[t].at[to_place]
            steps[t].append(remote(source, got_near[t].at[q], n_send.at[t, q], n_recv.at[t, q], device(0, q)))
        for copy in steps[t]:
            go(copy)

    def share_end(t, own, slots):
        for copy in steps[t]:
            copy.wait_recv()
        for b in range(GROUPS[t][2]):
            total = own(b).astype(F32)
            for slot in slots:
                total = total + got_near[t][slot, b].astype(F32)
            share[t][0, b] = total.astype(BF)
        for step in range(far_steps):
            copy = remote(share[t].at[step], got_far[t].at[step], d_send.at[t, step], d_recv.at[t, step], far[step])
            go(copy)
            copy.wait_recv()
            for b in range(GROUPS[t][2]):
                share[t][step + 1, b] = (share[t][step, b].astype(F32) + got_far[t][step, b].astype(F32)).astype(BF)
        deliver(t)

    def near_end(t):
        share_end(t, lambda b: part_sum[t][place, b], range(1, near))

    def deliver(t):
        section, first, count = GROUPS[t]
        last = share[t].at[far_steps]
        spot = result.at[core, mine, pl.ds(first, count)]
        for q in range(near):
            to = (section, xor(j, 2 * q))
            go(remote(last, spot, r_send.at[t, q], r_recv.at[t // 4, me, place], to), None if q > 0 else me != section)

        @pl.when(me == section)
        def _():
            for b in range(count):
                result[core, mine, first + b] = share[t][far_steps, b]

    copies = {}

    def vectors_start():
        copies["sections"] = [
            remote(gvec_part.at[to[0]], vec_got.at[k], gv_send.at[k], gv_recv.at[k], to) for k, to in enumerate(sections)
        ]
        for copy in copies["sections"]:
            go(copy)

    def vectors_mate():
        for copy in copies["sections"]:
            copy.wait_recv()
        vec_sum[0] = gvec_part[me] + vec_got[0] + vec_got[1] + vec_got[2]
        copies["mate"] = remote(vec_sum.at[0], vec_mate, gm_send.at[0], gm_recv.at[0], mate)
        go(copies["mate"])

    def vectors_near():
        copies["mate"].wait_recv()
        vec_sum[1] = vec_sum[0] + vec_mate[...]
        copies["near"] = [remote(vec_sum.at[1], vec_near.at[q], gn_send.at[q], gn_recv.at[q], device(0, q)) for q in range(1, near)]
        for copy in copies["near"]:
            go(copy)

    def vectors_end():
        for copy in copies["near"]:
            copy.wait_recv()
        vec_near[0] = vec_sum[1]
        total = vec_near[place]
        for q in range(1, near):
            total = total + vec_near[xor(place, q)]
        vec_sum[2] = total
        for step in range(far_steps):
            copy = remote(vec_sum.at[2 + step], vec_far.at[step], gd_send.at[step], gd_recv.at[step], far[step])
            go(copy)
            copy.wait_recv()
            vec_sum[3 + step] = vec_sum[2 + step] + vec_far[step]
        gvec_ref[...] = vec_sum[2 + far_steps]

    def on(act, *rest):
        return lambda: act(*rest)

    def inputs_here():
        for copy in loads[:4]:
            copy.wait()

    def vectors_here():
        for copy in vec_copies:
            copy.wait_recv()
        for copy in loads[4:]:
            copy.wait()

    plan = {
        ("inputs", 0): [inputs_here],
        ("vectors", 0): [vectors_here],
        ("prepared", 0): [
            on(send_weights, 1),
            on(send_weights, 2),
            on(pass_on, 0, (1, 2)),
            on(pass_on, 1, (1, 2)),
            on(pass_on, 2, (1, 2)),
            on(pass_on, 0, (3,)),
        ],
        ("weights", 1): [on(pass_on, 2, (3,))],
    }
    for t in range(SECTIONS):
        plan["weights", t] = plan.get(("weights", t), []) + [on(take_weights, t, 0)]
        plan["out", t] = [on(take_weights, t, 1), on(take_weights, t, 2)]
        plan["grads", t] = [on(halves_start, t)]
    plan["scores", 0] = [on(pass_on, 1, (3,))]
    plan["first grads", 0] = [on(halves_start, 4)]
    plan["first grads", 2] = [on(halves_end, 3), on(parts_start, 3)]
    plan["conv", 4] = [on(halves_end, 2), on(parts_start, 2)]
    plan["image", 3] = [on(halves_end, 1), on(parts_start, 1)]
    plan["half", 0] = [on(parts_end, 3), on(near_start, 3), on(halves_end, 4), on(parts_start, 4)]
    plan["half", 1] = [on(parts_end, 2), on(near_start, 2)]
    plan["norm", 1] = [on(halves_end, 0), on(parts_start, 0)]
    plan["conv", 1] = [vectors_start, on(near_end, 3)]
    done = []

    def at_point(name, s):
        for act in plan.get((name, s), []):
            act()
        done.append((name, s))

    layers(
        n, at_point,
        x_ref, cot_ref, routes_ref, vec_ref, win_ref, wout_ref, fin_ref, gin_ref, gvec_part, *scratch,
    )
    assert all(key in done or not plan[key] for key in plan)
    for t in (1, 4):
        parts_end(t)
        near_start(t)
    near_end(2)
    parts_end(0)
    near_start(0)
    vectors_mate()
    near_end(1)
    vectors_near()
    near_end(4)
    near_end(0)
    vectors_end()

    for section in range(SECTIONS):
        half = result.at[core, :, pl.ds(0, blocks_of(section))]

        @pl.when(me == section)
        def _():
            for t, (owner, first, count) in enumerate(GROUPS):
                if owner == section:
                    for k, q in around:
                        from_me, from_place = xor(me, k), xor(place, q)
                        spot = result.at[core, piece_of(from_me, from_place), pl.ds(first, count)]
                        remote(spot, spot, r_send.at[0, 0], r_recv.at[t // 4, from_me, from_place], mate).wait_recv()

        go(remote(half, half, m_send.at[section], m_recv.at[section], mate), me == section)

    for section in range(SECTIONS):
        half = result.at[1 - core, :, pl.ds(0, blocks_of(section))]
        copy = remote(half, half, m_send.at[section], m_recv.at[section], mate)
        pl.when(me == section)(lambda copy=copy: copy.wait_recv())

    for copy, condition in waiting:
        when(condition, lambda copy=copy: copy.wait_send())


def per_device(inputs, cotangent, routes, vectors, in_weight, out_weight):
    micro, n = inputs.shape[:2]
    dp = lax.axis_size("dp")
    near, piece_rows, piece_lanes, far_steps = shares_of(dp)
    images = micro * n * dp
    vmem = pl.BlockSpec(memory_space=pltpu.VMEM)
    hbm = pl.BlockSpec(memory_space=pltpu.HBM)
    dma = pltpu.SemaphoreType.DMA
    some, groups = max(far_steps, 1), len(GROUPS)

    def grad_buffer(*shape):
        return [pltpu.VMEM(tuple(count if size == "blocks" else size for size in shape), BF) for _, _, count in GROUPS]

    made = pl.pallas_call(
        functools.partial(whole_kernel, n, dp, images),
        out_shape=(
            jax.ShapeDtypeStruct((PATCHES, n, D), BF),
            jax.ShapeDtypeStruct((PATCHES, n, D), BF),
            jax.ShapeDtypeStruct((VEC_ROWS, D), F32),
            jax.ShapeDtypeStruct((2, SECTIONS * near, 6, piece_rows, piece_lanes), BF),
        ),
        in_specs=[hbm] * 6,
        out_specs=(vmem,) * 4,
        scratch_shapes=[
            pltpu.VMEM((PATCHES, n, D), BF),
            pltpu.VMEM((PATCHES, n, D), BF),
            pltpu.VMEM((2, n, TOPK, REGIONS), jnp.int32),
            pltpu.VMEM((SECTIONS, VEC_ROWS, D), F32),
            pltpu.VMEM((SECTIONS, D, HID), BF),
            pltpu.VMEM((SECTIONS, HID, D), BF),
            pltpu.VMEM((SECTIONS, VEC_ROWS, D), F32),
            grad_buffer("blocks", HALF, BLOCK),
            grad_buffer("blocks", HALF, BLOCK),
            grad_buffer("blocks", HALF, BLOCK),
            grad_buffer(SECTIONS * near, "blocks", piece_rows, piece_lanes),
            grad_buffer(3, near, "blocks", piece_rows, piece_lanes),
            grad_buffer(near, "blocks", piece_rows, piece_lanes),
            grad_buffer(near, "blocks", piece_rows, piece_lanes),
            grad_buffer(far_steps + 1, "blocks", piece_rows, piece_lanes),
            grad_buffer(some, "blocks", piece_rows, piece_lanes),
            pltpu.VMEM((3, VEC_ROWS, D), F32),
            pltpu.VMEM((3 + far_steps, VEC_ROWS, D), F32),
            pltpu.VMEM((VEC_ROWS, D), F32),
            pltpu.VMEM((near, VEC_ROWS, D), F32),
            pltpu.VMEM((some, VEC_ROWS, D), F32),
            dma((7,)),
            dma((3, 3)), dma((3, SECTIONS)),
            dma((3, SECTIONS)), dma((3, SECTIONS)),
            dma((3,)), dma((3,)),
            dma((groups,)), dma((groups,)),
            dma((groups, 3)), dma((groups, 3)),
            dma((groups, near)), dma((groups, near)),
            dma((groups, some)), dma((groups, some)),
            dma((groups, near)), dma((2, SECTIONS, near)),
            dma((SECTIONS,)), dma((SECTIONS,)),
            dma((3,)), dma((3,)),
            dma((1,)), dma((1,)),
            dma((near,)), dma((near,)),
            dma((some,)), dma((some,)),
        ]
        + layer_scratch(n),
        compiler_params=pltpu.CompilerParams(
            vmem_limit_bytes=60 * 1024 * 1024, collective_id=0, has_side_effects=True
        ),
        name="two_layers",
    )(
        jnp.transpose(inputs, (0, 2, 1, 3)),
        jnp.transpose(cotangent, (0, 2, 1, 3)),
        jnp.swapaxes(routes, 3, 4),
        vectors,
        in_weight,
        out_weight,
    )
    by_token = jax.ShapeDtypeStruct((1, PATCHES, n, D), BF)
    fin, gin, gvec, ga, gb = pl.pallas_call(
        functools.partial(results_kernel, dp, images),
        out_shape=(
            by_token,
            by_token,
            jax.ShapeDtypeStruct((1, VEC_ROWS, D), F32),
            jax.ShapeDtypeStruct((1, D, HID), F32),
            jax.ShapeDtypeStruct((1, HID, D), F32),
        ),
        in_specs=[vmem] * 4,
        out_specs=(hbm, hbm, vmem, hbm, hbm),
        scratch_shapes=[pltpu.VMEM((D, HID), F32), pltpu.VMEM((HID, D), F32), dma((4,))],
        compiler_params=pltpu.CompilerParams(vmem_limit_bytes=60 * 1024 * 1024),
        name="results",
    )(*made)
    return jnp.transpose(fin, (0, 2, 1, 3)), jnp.transpose(gin, (0, 2, 1, 3)), gvec, ga, gb


def solution(mesh):
    in_specs = (
        P(None, "dp", None, None),
        P(None, "dp", None, None),
        P(None, None, "dp", None, None),
        P("section", None, None),
        P("section", None, None),
        P("section", None, None),
    )
    out_specs = (
        P("section", "dp", None, None),
        P("section", "dp", None, None),
        P("section", None, None),
        P("section", None, None),
        P("section", None, None),
    )
    return jax.shard_map(
        per_device, mesh=mesh, in_specs=in_specs, out_specs=out_specs, check_vma=False
    )
```

```python
import functools

import jax
import jax.numpy as jnp
from jax import lax
from jax.experimental import pallas as pl
from jax.experimental.pallas import tpu as pltpu
from jax.sharding import PartitionSpec as P

D = 256
HEADS = 8
HEAD_DIM = 32
HID = 768
SIDE = 14
WIN = 7
TOPK = 4
SECTIONS = 4
VEC_ROWS = 16
PATCHES = 196
REGIONS = 49
BLOCK = 256
EPSILON = 1e-06

PITCH = 16
LIVE = SIDE * PITCH
ROWS = 256
HALO = 24
CHUNK = 32
LANES = 128
NEGATIVE = -1e30
LOG2E = 1.4426950408889634
SCALE = HEAD_DIM ** (-0.5)

BF = jnp.bfloat16
F32 = jnp.float32


def dot(a, b, ca=1, cb=0):
    return lax.dot_general(
        a, b, (((ca,), (cb,)), ((), ())), preferred_element_type=jnp.float32
    )


def iota(shape, dim):
    return lax.broadcasted_iota(jnp.int32, shape, dim)


def one_hot(cond):
    return jnp.where(cond, 1.0, 0.0).astype(BF)


def rows_of(i, count=LIVE):
    return pl.ds(pl.multiple_of(i * ROWS, ROWS), count)


def col_sum(x):
    return jnp.sum(x, axis=0, keepdims=True)


def ln_stats(x):
    average = jnp.mean(x, axis=-1, keepdims=True)
    centred = x - average
    spread = jnp.mean(centred * centred, axis=-1, keepdims=True)
    inverse = lax.rsqrt(spread + EPSILON)
    return centred * inverse, inverse


def gelu_pair(x):
    a = jnp.abs(x)
    t = 1.0 / (1.0 + a * (0.3275911 * 0.7071067811865476))
    e = jnp.exp2(x * x * (-0.5 * LOG2E))
    w = t * (0.5 * 1.061405429) + (0.5 * -1.453152027)
    w = w * t + (0.5 * 1.421413741)
    w = w * t + (0.5 * -0.284496736)
    w = w * t + (0.5 * 0.254829592)
    w = w * t * e
    phi = jnp.where(x >= 0, 1.0 - w, w)
    return x * phi, phi + x * e * 0.3989422804014327


def region_one_hot(shape, token_dim):
    token = iota(shape, token_dim)
    region = iota(shape, 1 - token_dim)
    r, c = token >> 4, token & (PITCH - 1)
    own = (r >> 1) * WIN + (c >> 1)
    return one_hot((own == region) & (c < SIDE) & (r < SIDE))


def weight_grads(scratch, s, first, count, half):
    nmt, att, actt, g, dproj = (scratch[LAYER_SCRATCH.index(name)] for name in ("nmt", "att", "actt", "g", "dproj"))
    results = []
    ins = min(first + count, 3) - first
    if ins > 0:
        rows = pl.ds(pl.multiple_of(half * LANES, LANES), LANES)
        wide = dot(nmt[s, rows], dproj[:, first * D : (first + ins) * D])
        results += [wide[:, b * D : (b + 1) * D] for b in range(ins)]
    for b in range(max(first, 3) - 3, first + count - 3):
        rows = pl.ds(pl.multiple_of(b * D + half * LANES, LANES), LANES)
        results.append(dot((actt if s % 2 == 1 else att)[s // 2, rows], g[...]))
    return results


LAYER_SCRATCH = (
    "hs", "zh", "inv", "nm", "nmt", "pr", "pt", "att", "act", "actt", "gp", "bias", "mixed", "g", "dproj", "cv", "cvl", "cvr",
    "dom", "qm", "dsb", "tmp", "dqt", "km", "wide",
)


def layers(
    n, at_point,
    x_ref, cot_ref, routes_ref, vec_ref, win_ref, wout_ref, fin_ref, gin_ref, gvec_ref,
    hs, zh, inv, nm, nmt, pr, pt, att, act, actt, gp, bias, mixed, g, dproj, cv, cvl, cvr, dom, qm, dsb, tmp, dqt, km, wide,
):
    pairs = PATCHES * n

    def eye():
        return one_hot(iota((ROWS, ROWS), 0) == iota((ROWS, ROWS), 1))

    def transposed(x):
        return dot(eye(), x, 1, 1)

    def spread(i):
        t, p = iota((ROWS, pairs), 0), iota((ROWS, pairs), 1)
        r, c = t >> 4, t & (PITCH - 1)
        return one_hot((p == (r * SIDE + c) * n + i) & (c < SIDE) & (r < SIDE))

    def gather():
        p, t = iota((pairs, n * ROWS), 0), iota((pairs, n * ROWS), 1)
        r, c, i = (t & (ROWS - 1)) >> 4, t & (PITCH - 1), t >> 8
        return one_hot((p == (r * SIDE + c) * n + i) & (c < SIDE) & (r < SIDE))

    def chunks():
        return [slice(c, c + CHUNK) for c in range(0, LIVE, CHUNK)]

    def rows_at(i, c, count):
        return pl.ds(pl.multiple_of(i * ROWS + c, PITCH), count)

    def tail(i):
        return pl.ds(i * ROWS + LIVE, ROWS - LIVE)

    none = jnp.zeros((ROWS - LIVE, D), BF)
    none_wide = jnp.zeros((ROWS - LIVE, HID), BF)
    halo = jnp.zeros((HALO, D), F32)
    for buffer in (cv, cvl, cvr):
        buffer[0:HALO] = halo
        buffer[HALO + LIVE : HALO + LIVE + HALO] = halo
    for i in range(n):
        for s in range(SECTIONS):
            nm[s, tail(i)] = none
            hs[s, tail(i)] = none
        for a in range(2):
            pr[a, tail(i)] = none_wide
            act[a, tail(i)] = none_wide
        wide[tail(i)] = none
        dproj[tail(i)] = none_wide
    gvec_ref[...] = jnp.zeros_like(gvec_ref)

    at_point("inputs", 0)
    x_pairs = x_ref[...].reshape(pairs, D)
    cot_pairs = cot_ref[...].reshape(pairs, D)
    for i in range(n):
        spread_i = spread(i)
        hs[0, pl.ds(i * ROWS, ROWS)] = dot(spread_i, x_pairs).astype(BF)
        g[pl.ds(i * ROWS, ROWS)] = dot(spread_i, cot_pairs).astype(BF)

    def conv_load(r0, count, x):
        cv[pl.ds(HALO + r0, count)] = x

    def conv_shift():
        for rows in chunks():
            cvl[HALO + rows.start : HALO + rows.stop] = cv[HALO + rows.start - 1 : HALO + rows.stop - 1]
            cvr[HALO + rows.start : HALO + rows.stop] = cv[HALO + rows.start + 1 : HALO + rows.stop + 1]

    def conv_at(r, u, v):
        start = HALO + (r + u) * PITCH
        return (cvl, cv, cvr)[v + 1][start : start + PITCH]

    def columns(i):
        return slice(i * ROWS, (i + 1) * ROWS)

    def attention_start(s):
        vec = vec_ref.at[s]
        for i in range(n):
            for rows in chunks():
                conv_load(rows.start, CHUNK, hs[s, rows_at(i, rows.start, CHUNK)].astype(F32))
            conv_shift()
            for r in range(SIDE):
                total = conv_at(r, 0, 0) + vec[15:16]
                for u in (-1, 0, 1):
                    for v in (-1, 0, 1):
                        j = 6 + 3 * (u + 1) + v + 1
                        total = total + conv_at(r, u, v) * vec[j : j + 1]
                here = rows_at(i, r * PITCH, PITCH)
                mixed[here] = total
                hat, inverse = ln_stats(total)
                zh[s, here] = hat
                inv[s, here] = inverse
                nm[s, here] = (hat * vec[0:1] + vec[1:2]).astype(BF)
        for i in range(n):
            nmt[s, :, columns(i)] = transposed(nm[s, rows_of(i, ROWS)]).astype(BF)

    def route_bias():
        key_region = region_one_hot((LIVE, REGIONS), 0)
        query_region = region_one_hot((REGIONS, ROWS), 1)
        for i in range(n):
            for a in range(2):
                picks = routes_ref[a, i]
                region = iota((REGIONS, REGIONS), 0)
                routed = jnp.zeros((REGIONS, REGIONS), F32)
                for k in range(TOPK):
                    routed = routed + jnp.where(picks[k : k + 1] == region, 1.0, 0.0)
                by_region = dot(key_region, routed.astype(BF)).astype(BF)
                bias[a, i] = (1.0 - dot(by_region, query_region)) * NEGATIVE

    def half_of(h):
        return slice((h // 4) * LANES, (h // 4 + 1) * LANES)

    def own_lanes(h, count):
        return (iota((count, LANES), 1) >> 5) == h % 4

    def attention_forward(s):
        a = s // 2
        vec = vec_ref.at[s]
        at_point("weights", s)
        for i in range(n):
            rows = rows_of(i)
            pr[a, rows, 0 : 2 * D] = dot(nm[s, rows], win_ref[s, :, 0 : 2 * D]).astype(BF)
        for i in range(n):
            rows, whole = rows_of(i), rows_of(i, ROWS)
            for h in range(HEADS):
                lanes = half_of(h)
                keys = jnp.where(own_lanes(h, LIVE), pr[a, rows, slice(D + lanes.start, D + lanes.stop)], jnp.zeros((), BF))
                scores = dot(keys, pr[a, whole, lanes], 1, 1) * (SCALE * LOG2E) + bias[a, i]
                expo = jnp.exp2(scores - jnp.max(scores, axis=0, keepdims=True))
                pt[a, i, :, h * ROWS : (h + 1) * ROWS] = (expo * (1.0 / col_sum(expo))).astype(BF)
        at_point("scores", s)
        at_point("values", s)
        for i in range(n):
            rows, whole = rows_of(i), rows_of(i, ROWS)
            pr[a, rows, 2 * D : 3 * D] = dot(nm[s, rows], win_ref[s, :, 2 * D : 3 * D]).astype(BF)
            tmp[i] = transposed(pr[a, whole, 2 * D : 3 * D]).astype(BF)
        for i in range(n):
            for h in range(HEADS):
                own = slice(h * HEAD_DIM, (h + 1) * HEAD_DIM)
                att[a, own, columns(i)] = dot(tmp[i, own, 0:LIVE], pt[a, i, :, h * ROWS : (h + 1) * ROWS]).astype(BF)
        at_point("out", s)
        for i in range(n):
            attended = transposed(att[a, :, columns(i)]).astype(BF)
            out = mixed[rows_of(i)] + dot(attended[:LIVE], wout_ref[s, 0:D]) + vec[2:3]
            hs[s + 1, rows_of(i)] = out.astype(BF)

    def dense_forward(s):
        a = s // 2
        vec = vec_ref.at[s]
        for i in range(n):
            for part in chunks():
                here = rows_at(i, part.start, CHUNK)
                hat, inverse = ln_stats(hs[s, here].astype(F32))
                zh[s, here] = hat
                inv[s, here] = inverse
                nm[s, here] = (hat * vec[0:1] + vec[1:2]).astype(BF)
        for i in range(n):
            nmt[s, :, columns(i)] = transposed(nm[s, rows_of(i, ROWS)]).astype(BF)
        at_point("weights", s)
        at_point("values", s)
        for j in range(3):
            lanes = slice(j * D, (j + 1) * D)
            for i in range(n):
                rows = rows_of(i)
                hidden = dot(nm[s, rows], win_ref[s, :, lanes]) + vec[3 + j : 4 + j]
                value, slope = gelu_pair(hidden)
                act[a, rows, lanes] = value.astype(BF)
                gp[a, rows, lanes] = slope
        at_point("out", s)
        for i in range(n):
            rows = rows_of(i)
            out = hs[s, rows].astype(F32) + dot(act[a, rows], wout_ref[s]) + vec[2:3]
            if s + 1 < SECTIONS:
                live = (iota((LIVE, D), 0) & (PITCH - 1)) < SIDE
                hs[s + 1, rows] = jnp.where(live, out, 0.0).astype(BF)
            else:
                wide[rows] = out.astype(BF)
        for j in range(3):
            lanes = slice(j * D, (j + 1) * D)
            for i in range(n):
                actt[a, lanes, columns(i)] = transposed(act[a, rows_of(i, ROWS), lanes]).astype(BF)

    def norm_backward(s, here, d_normed, sums):
        vec = vec_ref.at[s]
        hat = zh[s, here]
        product = d_normed * hat
        scaled = d_normed * vec[0:1]
        first = jnp.mean(scaled, axis=-1, keepdims=True)
        second = jnp.mean(product * vec[0:1], axis=-1, keepdims=True)
        sums[0] = sums[0] + fold(product)
        sums[1] = sums[1] + fold(d_normed)
        return inv[s, here] * (scaled - first - hat * second)

    def fold(x):
        return jnp.sum(x.reshape(x.shape[0] // 8, 8, x.shape[1]), axis=0)

    def empty():
        return jnp.zeros((8, D), F32)

    def add_row(s, row, total):
        gvec_ref[s, row : row + 1] += col_sum(total)

    def dense_backward(s):
        a = s // 2
        at_point("first grads", s)
        for i in range(n):
            rows = rows_of(i)
            for j in range(3):
                lanes = slice(j * D, (j + 1) * D)
                d_active = dot(g[rows], wout_ref[s, lanes], 1, 1)
                d_hidden = (d_active * gp[a, rows, lanes]).astype(BF)
                dproj[rows, lanes] = d_hidden
                add_row(s, 3 + j, fold(d_hidden.astype(F32)))
        at_point("grads", s)
        for i in range(n):
            rows = rows_of(i)
            d_normed = dot(dproj[rows], win_ref[s], 1, 1)
            sums = [empty(), empty(), empty()]
            for part in chunks():
                here = rows_at(i, part.start, CHUNK)
                grad = g[here].astype(F32)
                sums[2] = sums[2] + fold(grad)
                out = grad + norm_backward(s, here, d_normed[part], sums)
                g[here] = out.astype(BF)
            for row in range(3):
                add_row(s, row, sums[row])
            at_point("image", 2 * s + i)

    def attention_backward(s):
        a = s // 2
        vec = vec_ref.at[s]
        nothing = jnp.zeros((), BF)
        for i in range(n):
            rows = rows_of(i)
            whole = rows_of(i, ROWS)
            km[whole] = dot(g[whole], wout_ref[s, 0:D], 1, 1).astype(BF)
            for h in range(HEADS):
                dom[h * ROWS : (h + 1) * ROWS] = jnp.where(own_lanes(h, ROWS), km[whole, half_of(h)], nothing)
            for half in range(2):
                lanes = slice(2 * D + half * LANES, 2 * D + (half + 1) * LANES)
                four = slice(half * 4 * ROWS, (half + 1) * 4 * ROWS)
                dproj[rows, lanes] = dot(pt[a, i, :, four], dom[four]).astype(BF)
        at_point("first grads", s)
        for i in range(n):
            rows = rows_of(i)
            whole = rows_of(i, ROWS)
            tmp[i] = transposed(pr[a, whole, D : 2 * D]).astype(BF)
            for h in range(HEADS):
                qm[h * ROWS : (h + 1) * ROWS] = jnp.where(own_lanes(h, ROWS), pr[a, whole, half_of(h)], nothing)
            for h in range(HEADS):
                lanes = half_of(h)
                row = slice(h * ROWS, (h + 1) * ROWS)
                values = jnp.where(own_lanes(h, LIVE), pr[a, rows, slice(2 * D + lanes.start, 2 * D + lanes.stop)], nothing)
                d_weights = dot(values, km[whole, lanes], 1, 1)
                weights = pt[a, i, :, row].astype(F32)
                dsb[:, row] = (weights * (d_weights - col_sum(weights * d_weights))).astype(BF)
                if h == 3:
                    at_point("half", 2 * s + i)
            for h in range(HEADS):
                own = slice(h * HEAD_DIM, (h + 1) * HEAD_DIM)
                dqt[own] = dot(tmp[i, own, 0:LIVE], dsb[:, h * ROWS : (h + 1) * ROWS])
            for half in range(2):
                lanes = slice(D + half * LANES, D + (half + 1) * LANES)
                four = slice(half * 4 * ROWS, (half + 1) * 4 * ROWS)
                dproj[rows, lanes] = (dot(dsb[:, four], qm[four]) * SCALE).astype(BF)
            dproj[rows, 0:D] = (transposed(dqt[...].astype(BF))[:LIVE] * SCALE).astype(BF)
            at_point("image", 2 * s + i)
        at_point("grads", s)
        for i in range(n):
            rows = rows_of(i)
            d_normed = dot(dproj[rows], win_ref[s], 1, 1)
            sums = [empty(), empty(), empty(), empty()]
            for part in chunks():
                here = rows_at(i, part.start, CHUNK)
                grad = g[here].astype(F32)
                sums[2] = sums[2] + fold(grad)
                d_mixed = grad + norm_backward(s, here, d_normed[part], sums)
                sums[3] = sums[3] + fold(d_mixed)
                conv_load(part.start, CHUNK, d_mixed)
            for row, total in zip((0, 1, 2, 15), sums):
                add_row(s, row, total)
            at_point("norm", 2 * s + i)
            conv_shift()
            taps = [empty() for _ in range(9)]
            for r in range(SIDE):
                here = rows_at(i, r * PITCH, PITCH)
                start = hs[s, here].astype(F32)
                total = conv_at(r, 0, 0)
                for u in (-1, 0, 1):
                    for v in (-1, 0, 1):
                        j = 3 * (u + 1) + v + 1
                        moved = conv_at(r, -u, -v)
                        total = total + moved * vec[6 + j : 7 + j]
                        taps[j] = taps[j] + fold(moved * start)
                g[here] = jnp.where(iota((PITCH, D), 0) < SIDE, total, 0.0).astype(BF)
            for j in range(9):
                add_row(s, 6 + j, taps[j])
            at_point("conv", 2 * s + i)

    route_bias()
    at_point("routed", 0)
    attention_start(0)
    at_point("prepared", 0)
    for s in range(SECTIONS):
        if s == 2:
            attention_start(s)
        (attention_forward, dense_forward)[s % 2](s)
    fin_ref[...] = dot(gather(), wide[...]).astype(BF).reshape(PATCHES, n, D)
    for s in reversed(range(SECTIONS)):
        (attention_backward, dense_backward)[s % 2](s)
    gin_ref[...] = dot(gather(), g[...]).astype(BF).reshape(PATCHES, n, D)


def layer_scratch(n):
    total = n * ROWS
    return [
        pltpu.VMEM((SECTIONS, total, D), BF),
        pltpu.VMEM((SECTIONS, total, D), F32),
        pltpu.VMEM((SECTIONS, total, 1), F32),
        pltpu.VMEM((SECTIONS, total, D), BF),
        pltpu.VMEM((SECTIONS, D, total), BF),
        pltpu.VMEM((2, total, HID), BF),
        pltpu.VMEM((2, n, LIVE, HEADS * ROWS), BF),
        pltpu.VMEM((2, D, total), BF),
        pltpu.VMEM((2, total, HID), BF),
        pltpu.VMEM((2, HID, total), BF),
        pltpu.VMEM((2, total, HID), F32),
        pltpu.VMEM((2, n, LIVE, ROWS), F32),
        pltpu.VMEM((total, D), F32),
        pltpu.VMEM((total, D), BF),
        pltpu.VMEM((total, HID), BF),
        pltpu.VMEM((LIVE + 2 * HALO, D), F32),
        pltpu.VMEM((LIVE + 2 * HALO, D), F32),
        pltpu.VMEM((LIVE + 2 * HALO, D), F32),
        pltpu.VMEM((HEADS * ROWS, LANES), BF),
        pltpu.VMEM((HEADS * ROWS, LANES), BF),
        pltpu.VMEM((LIVE, HEADS * ROWS), BF),
        pltpu.VMEM((n, D, ROWS), BF),
        pltpu.VMEM((D, ROWS), F32),
        pltpu.VMEM((total, D), BF),
        pltpu.VMEM((total, D), BF),
    ]


def compute_kernel(n, *refs):
    x_ref, cot_ref, routes_ref, vec_ref, win_ref, wout_ref, fin_ref, gin_ref, gvec_ref, ga_ref, gb_ref = refs[:11]

    def at_point(name, s):
        if name != "grads":
            return
        count = 6 if s % 2 == 1 else 4
        for half in range(2):
            for b, value in enumerate(weight_grads(refs[11:], s, 0, count, half)):
                rows = slice(half * LANES, (half + 1) * LANES)
                if b < 3:
                    ga_ref[s, rows, b * D : (b + 1) * D] = value
                else:
                    gb_ref[s, (b - 3) * D + half * LANES : (b - 3) * D + (half + 1) * LANES] = value
        if s % 2 == 0:
            gb_ref[s, D:HID] = jnp.zeros((HID - D, D), F32)

    layers(n, at_point, x_ref, cot_ref, routes_ref, vec_ref, win_ref, wout_ref, fin_ref.at[0], gin_ref.at[0], gvec_ref, *refs[11:])


def compute(x, cot, routes, vec, win, wout):
    n = x.shape[0]
    vmem = pl.BlockSpec(memory_space=pltpu.VMEM)
    by_token = jax.ShapeDtypeStruct((1, PATCHES, n, D), BF)
    fin, gin, gvec, ga, gb = pl.pallas_call(
        functools.partial(compute_kernel, n),
        out_shape=(
            by_token,
            by_token,
            jax.ShapeDtypeStruct((SECTIONS, VEC_ROWS, D), F32),
            jax.ShapeDtypeStruct((SECTIONS, D, HID), F32),
            jax.ShapeDtypeStruct((SECTIONS, HID, D), F32),
        ),
        in_specs=[vmem] * 6,
        out_specs=(vmem,) * 5,
        scratch_shapes=layer_scratch(n),
        compiler_params=pltpu.CompilerParams(vmem_limit_bytes=56 * 1024 * 1024),
        name="layers_alone",
    )(jnp.transpose(x, (1, 0, 2)), jnp.transpose(cot, (1, 0, 2)), jnp.swapaxes(routes, 2, 3), vec, win, wout)
    return jnp.transpose(fin, (0, 2, 1, 3)), jnp.transpose(gin, (0, 2, 1, 3)), gvec, ga, gb


MESH = pl.DeviceIdType.MESH
HALF = BLOCK // 2
PART = HALF // SECTIONS


def blocks_of(t):
    return 6 if t % 2 == 1 else 4


GROUPS = ((0, 0, 2), (1, 0, 6), (2, 0, 4), (3, 0, 6), (0, 2, 2))


def shares_of(dp):
    chips = dp // 2
    near = min(chips, 4)
    split = min(near, 2)
    return near, PART // split, BLOCK // (near // split), (chips // near).bit_length() - 1


def piece_slices(dp, piece):
    near, piece_rows, piece_lanes, _ = shares_of(dp)
    k, q = piece // near, piece % near
    rows = k * PART + q % (PART // piece_rows) * piece_rows
    lanes = q // (PART // piece_rows) * piece_lanes
    return slice(rows, rows + piece_rows), slice(lanes, lanes + piece_lanes)


def results_kernel(dp, images, fin_in, gin_in, gvec_in, result, fin_ref, gin_ref, gvec_ref, ga_ref, gb_ref, ga, gb, sems):
    copies = [
        pltpu.make_async_copy(fin_in, fin_ref.at[0], sems.at[0]),
        pltpu.make_async_copy(gin_in, gin_ref.at[0], sems.at[1]),
        pltpu.make_async_copy(ga, ga_ref.at[0], sems.at[2]),
        pltpu.make_async_copy(gb, gb_ref.at[0], sems.at[3]),
    ]
    copies[0].start()
    copies[1].start()
    gvec_ref[0] = gvec_in[...] * (1.0 / images)
    for target, first in ((ga, 0), (gb, 3)):
        for c in range(2):
            for piece in range(result.shape[1]):
                rows, lanes = piece_slices(dp, piece)
                for b in range(3):
                    value = result[c, piece, first + b].astype(F32) * (1.0 / images)
                    start = c * HALF + rows.start
                    if first == 0:
                        target[start : start + rows.stop - rows.start, b * D + lanes.start : b * D + lanes.stop] = value
                    else:
                        target[b * D + start : b * D + start + rows.stop - rows.start, lanes] = value
        if first == 0:
            copies[2].start()

    @pl.when(lax.rem(lax.axis_index("section"), 2) == 0)
    def _():
        gb[D:HID] = jnp.zeros((HID - D, D), F32)

    copies[3].start()
    for copy in copies:
        copy.wait()


def whole_kernel(
    n, dp, images,
    inputs_ref, cot_in_ref, routes_in_ref, vec_own, win_own, wout_own,
    fin_ref, gin_ref, gvec_ref, result,
    x_ref, cot_ref, routes_ref, vec_ref, win_ref, wout_ref, gvec_part,
    own_half, send_half, got_half, half_sum, got_part, part_sum, got_near, share, got_far, vec_got, vec_sum, vec_mate, vec_near, vec_far,
    in_sem, w_send, w_recv, f_send, f_recv, v_send, v_recv, h_send, h_recv, p_send, p_recv, n_send, n_recv, d_send, d_recv,
    r_send, r_recv, m_send, m_recv, gv_send, gv_recv, gm_send, gm_recv, gn_send, gn_recv, gd_send, gd_recv,
    *scratch,
):
    me, j = lax.axis_index("section"), lax.axis_index("dp")
    core = lax.rem(j, 2)
    chip = j // 2
    near, piece_rows, piece_lanes, far_steps = shares_of(dp)
    place = lax.rem(chip, near)
    xor = lax.bitwise_xor

    def device(k, q, other=0):
        return (xor(me, k), xor(j, 2 * q + other))

    mate = device(0, 0, 1)
    sections = [device(k, 0) for k in range(1, SECTIONS)]
    around = [(k, q) for k in range(SECTIONS) for q in range(near) if (k, q) != (0, 0)]
    far = [(me, xor(j, 2 * near << b)) for b in range(far_steps)]
    waiting = []

    def remote(src, dst, send, recv, to):
        return pltpu.make_async_remote_copy(src, dst, send, recv, device_id=to, device_id_type=MESH)

    def when(condition, act):
        if condition is None:
            act()
        else:
            pl.when(condition)(act)

    def go(copy, condition=None):
        when(condition, lambda: copy.start())
        waiting.append((copy, condition))

    loads = [
        pltpu.make_async_copy(inputs_ref.at[me], x_ref, in_sem.at[0]),
        pltpu.make_async_copy(cot_in_ref.at[me], cot_ref, in_sem.at[1]),
        pltpu.make_async_copy(routes_in_ref.at[0, me], routes_ref.at[0], in_sem.at[2]),
        pltpu.make_async_copy(routes_in_ref.at[1, me], routes_ref.at[1], in_sem.at[3]),
        pltpu.make_async_copy(vec_own.at[0], vec_ref.at[me], in_sem.at[4]),
        pltpu.make_async_copy(win_own.at[0], win_ref.at[me], in_sem.at[5]),
        pltpu.make_async_copy(wout_own.at[0], wout_ref.at[me], in_sem.at[6]),
    ]
    for copy in loads:
        copy.start()

    barrier = pltpu.get_barrier_semaphore()
    everyone = [device(k, q) for k, q in around] + [mate] + far
    for to in everyone:
        pl.semaphore_signal(barrier, inc=1, device_id=to, device_id_type=MESH)
    pl.semaphore_wait(barrier, len(everyone))

    own_rows = pl.ds(pl.multiple_of(core * HALF, HALF), HALF)
    tail_rows = pl.ds(pl.multiple_of(D + core * D, D), D)
    pieces = [(win_own, win_ref, own_rows), (wout_own, wout_ref, own_rows), (wout_own, wout_ref, tail_rows)]

    def spot(p, t):
        return pieces[p][1].at[t, pieces[p][2]]

    def odd(t):
        return lax.rem(t, 2) == 1

    vec_copies = [remote(vec_own.at[0], vec_ref.at[me], v_send.at[k], v_recv.at[k], to) for k, to in enumerate(sections)]
    out_copies = [
        [
            remote(source.at[0, rows], target.at[me, rows], w_send.at[p, k - 1], w_recv.at[p, me], device(k, 0))
            for k in (1, 2)
        ]
        for p, (source, target, rows) in enumerate(pieces)
    ]
    relayed, relay_to = xor(me, 1 + core), xor(me, 2 - core)
    relays = [remote(spot(p, relayed), spot(p, relayed), w_send.at[p, 2], w_recv.at[p, relayed], (relay_to, j)) for p in range(3)]
    arrivals, handings, takings = {}, {}, {}
    for p in range(3):
        for k in (1, 2, 3):
            t = xor(me, k)
            arrivals[p, k] = remote(spot(p, t), spot(p, t), w_send.at[p, 0], w_recv.at[p, t], mate)
            handings[p, k] = remote(spot(p, t), spot(p, t), f_send.at[p, t], f_recv.at[p, t], mate)
        for t in range(SECTIONS):
            if p < 2 or t % 2 == 1:
                takings[p, t] = remote(spot(p, t), spot(p, t), f_send.at[p, t], f_recv.at[p, t], mate)
    foreign = [me != t for t in range(SECTIONS)]

    def send_weights(p):
        for copy in out_copies[p]:
            go(copy, odd(me) if p == 2 else None)

    def pass_on(p, ks):
        for k in ks:
            condition = odd(xor(me, k)) if p == 2 else None
            when(condition, lambda: arrivals[p, k].wait_recv())
        if ks != (3,):
            go(relays[p], odd(relayed) if p == 2 else None)
        for k in ks:
            go(handings[p, k], odd(xor(me, k)) if p == 2 else None)

    def take_weights(t, p):
        if p < 2 or t % 2 == 1:
            pl.when(foreign[t])(lambda: takings[p, t].wait_recv())

    for copy in vec_copies:
        go(copy)
    send_weights(0)


    def piece_of(k, q):
        return k * near + q

    def quarter(k):
        return pl.ds(pl.multiple_of(k * near, near), near)

    mine = piece_of(me, place)
    steps = {}

    def halves_start(t):
        section, first, count = GROUPS[t]
        for b, value in enumerate(weight_grads(scratch, section, first, count, 1 - core)):
            send_half[t][b] = value.astype(BF)
        copy = remote(send_half[t], got_half[t], h_send.at[t], h_recv.at[t], mate)
        go(copy)
        for b, value in enumerate(weight_grads(scratch, section, first, count, core)):
            own_half[t][b] = value.astype(BF)
        steps[t] = [copy]

    def halves_end(t):
        steps[t][0].wait_recv()
        for b in range(GROUPS[t][2]):
            total = own_half[t][b] + got_half[t][b]
            for piece in range(SECTIONS * near):
                rows, lanes = piece_slices(dp, piece)
                half_sum[t][piece, b] = total[rows, lanes]

    def parts_start(t):
        steps[t] = [
            remote(half_sum[t].at[quarter(to[0])], got_part[t].at[k], p_send.at[t, k], p_recv.at[t, k], to)
            for k, to in enumerate(sections)
        ]
        for copy in steps[t]:
            go(copy)

    def parts_end(t):
        for copy in steps[t]:
            copy.wait_recv()
        for q in range(near):
            for b in range(GROUPS[t][2]):
                total = half_sum[t][piece_of(me, q), b].astype(F32)
                for k in range(SECTIONS - 1):
                    total = total + got_part[t][k, q, b].astype(F32)
                part_sum[t][q, b] = total.astype(BF)

    def near_start(t):
        steps[t] = []
        for q in range(1, near):
            to_place = xor(place, q)
            source = part_sum[t].at[to_place]
            steps[t].append(remote(source, got_near[t].at[q], n_send.at[t, q], n_recv.at[t, q], device(0, q)))
        for copy in steps[t]:
            go(copy)

    def share_end(t, own, slots):
        for copy in steps[t]:
            copy.wait_recv()
        for b in range(GROUPS[t][2]):
            total = own(b).astype(F32)
            for slot in slots:
                total = total + got_near[t][slot, b].astype(F32)
            share[t][0, b] = total.astype(BF)
        for step in range(far_steps):
            copy = remote(share[t].at[step], got_far[t].at[step], d_send.at[t, step], d_recv.at[t, step], far[step])
            go(copy)
            copy.wait_recv()
            for b in range(GROUPS[t][2]):
                share[t][step + 1, b] = (share[t][step, b].astype(F32) + got_far[t][step, b].astype(F32)).astype(BF)
        deliver(t)

    def near_end(t):
        share_end(t, lambda b: part_sum[t][place, b], range(1, near))

    def deliver(t):
        section, first, count = GROUPS[t]
        last = share[t].at[far_steps]
        spot = result.at[core, mine, pl.ds(first, count)]
        for q in range(near):
            to = (section, xor(j, 2 * q))
            go(remote(last, spot, r_send.at[t, q], r_recv.at[t // 4, me, place], to), None if q > 0 else me != section)

        @pl.when(me == section)
        def _():
            for b in range(count):
                result[core, mine, first + b] = share[t][far_steps, b]

    copies = {}

    def vectors_start():
        copies["sections"] = [
            remote(gvec_part.at[to[0]], vec_got.at[k], gv_send.at[k], gv_recv.at[k], to) for k, to in enumerate(sections)
        ]
        for copy in copies["sections"]:
            go(copy)

    def vectors_mate():
        for copy in copies["sections"]:
            copy.wait_recv()
        vec_sum[0] = gvec_part[me] + vec_got[0] + vec_got[1] + vec_got[2]
        copies["mate"] = remote(vec_sum.at[0], vec_mate, gm_send.at[0], gm_recv.at[0], mate)
        go(copies["mate"])

    def vectors_near():
        copies["mate"].wait_recv()
        vec_sum[1] = vec_sum[0] + vec_mate[...]
        copies["near"] = [remote(vec_sum.at[1], vec_near.at[q], gn_send.at[q], gn_recv.at[q], device(0, q)) for q in range(1, near)]
        for copy in copies["near"]:
            go(copy)

    def vectors_end():
        for copy in copies["near"]:
            copy.wait_recv()
        vec_near[0] = vec_sum[1]
        total = vec_near[place]
        for q in range(1, near):
            total = total + vec_near[xor(place, q)]
        vec_sum[2] = total
        for step in range(far_steps):
            copy = remote(vec_sum.at[2 + step], vec_far.at[step], gd_send.at[step], gd_recv.at[step], far[step])
            go(copy)
            copy.wait_recv()
            vec_sum[3 + step] = vec_sum[2 + step] + vec_far[step]
        gvec_ref[...] = vec_sum[2 + far_steps]

    def on(act, *rest):
        return lambda: act(*rest)

    def inputs_here():
        for copy in loads[:4]:
            copy.wait()

    def vectors_here():
        for copy in vec_copies:
            copy.wait_recv()
        for copy in loads[4:]:
            copy.wait()

    plan = {
        ("inputs", 0): [inputs_here],
        ("routed", 0): [on(send_weights, 1), on(send_weights, 2), vectors_here],
        ("prepared", 0): [
            on(pass_on, 0, (1, 2)),
            on(pass_on, 1, (1, 2)),
            on(pass_on, 2, (1, 2)),
            on(pass_on, 0, (3,)),
        ],
        ("weights", 1): [on(pass_on, 2, (3,))],
    }
    for t in range(SECTIONS):
        plan["weights", t] = plan.get(("weights", t), []) + [on(take_weights, t, 0)]
        plan["out", t] = [on(take_weights, t, 1), on(take_weights, t, 2)]
        plan["grads", t] = [on(halves_start, t)]
    plan["scores", 0] = [on(pass_on, 1, (3,))]
    plan["first grads", 0] = [on(halves_start, 4)]
    plan["first grads", 2] = [on(halves_end, 3), on(parts_start, 3)]
    plan["conv", 4] = [on(halves_end, 2), on(parts_start, 2)]
    plan["image", 3] = [on(halves_end, 1), on(parts_start, 1)]
    plan["half", 0] = [on(parts_end, 3), on(near_start, 3), on(halves_end, 4), on(parts_start, 4)]
    plan["half", 1] = [on(parts_end, 2), on(near_start, 2)]
    plan["norm", 1] = [on(halves_end, 0), on(parts_start, 0)]
    plan["conv", 1] = [vectors_start, on(near_end, 3)]
    done = []

    def at_point(name, s):
        for act in plan.get((name, s), []):
            act()
        done.append((name, s))

    layers(
        n, at_point,
        x_ref, cot_ref, routes_ref, vec_ref, win_ref, wout_ref, fin_ref, gin_ref, gvec_part, *scratch,
    )
    assert all(key in done or not plan[key] for key in plan)
    for t in (1, 4):
        parts_end(t)
        near_start(t)
    near_end(2)
    parts_end(0)
    near_start(0)
    vectors_mate()
    near_end(1)
    vectors_near()
    near_end(4)
    near_end(0)
    vectors_end()

    for section in range(SECTIONS):
        half = result.at[core, :, pl.ds(0, blocks_of(section))]

        @pl.when(me == section)
        def _():
            for t, (owner, first, count) in enumerate(GROUPS):
                if owner == section:
                    for k, q in around:
                        from_me, from_place = xor(me, k), xor(place, q)
                        spot = result.at[core, piece_of(from_me, from_place), pl.ds(first, count)]
                        remote(spot, spot, r_send.at[0, 0], r_recv.at[t // 4, from_me, from_place], mate).wait_recv()

        go(remote(half, half, m_send.at[section], m_recv.at[section], mate), me == section)

    for section in range(SECTIONS):
        half = result.at[1 - core, :, pl.ds(0, blocks_of(section))]
        copy = remote(half, half, m_send.at[section], m_recv.at[section], mate)
        pl.when(me == section)(lambda copy=copy: copy.wait_recv())

    for copy, condition in waiting:
        when(condition, lambda copy=copy: copy.wait_send())


def per_device(inputs, cotangent, routes, vectors, in_weight, out_weight):
    micro, n = inputs.shape[:2]
    dp = lax.axis_size("dp")
    near, piece_rows, piece_lanes, far_steps = shares_of(dp)
    images = micro * n * dp
    vmem = pl.BlockSpec(memory_space=pltpu.VMEM)
    hbm = pl.BlockSpec(memory_space=pltpu.HBM)
    dma = pltpu.SemaphoreType.DMA
    some, groups = max(far_steps, 1), len(GROUPS)

    def grad_buffer(*shape):
        return [pltpu.VMEM(tuple(count if size == "blocks" else size for size in shape), BF) for _, _, count in GROUPS]

    made = pl.pallas_call(
        functools.partial(whole_kernel, n, dp, images),
        out_shape=(
            jax.ShapeDtypeStruct((PATCHES, n, D), BF),
            jax.ShapeDtypeStruct((PATCHES, n, D), BF),
            jax.ShapeDtypeStruct((VEC_ROWS, D), F32),
            jax.ShapeDtypeStruct((2, SECTIONS * near, 6, piece_rows, piece_lanes), BF),
        ),
        in_specs=[hbm] * 6,
        out_specs=(vmem,) * 4,
        scratch_shapes=[
            pltpu.VMEM((PATCHES, n, D), BF),
            pltpu.VMEM((PATCHES, n, D), BF),
            pltpu.VMEM((2, n, TOPK, REGIONS), jnp.int32),
            pltpu.VMEM((SECTIONS, VEC_ROWS, D), F32),
            pltpu.VMEM((SECTIONS, D, HID), BF),
            pltpu.VMEM((SECTIONS, HID, D), BF),
            pltpu.VMEM((SECTIONS, VEC_ROWS, D), F32),
            grad_buffer("blocks", HALF, BLOCK),
            grad_buffer("blocks", HALF, BLOCK),
            grad_buffer("blocks", HALF, BLOCK),
            grad_buffer(SECTIONS * near, "blocks", piece_rows, piece_lanes),
            grad_buffer(3, near, "blocks", piece_rows, piece_lanes),
            grad_buffer(near, "blocks", piece_rows, piece_lanes),
            grad_buffer(near, "blocks", piece_rows, piece_lanes),
            grad_buffer(far_steps + 1, "blocks", piece_rows, piece_lanes),
            grad_buffer(some, "blocks", piece_rows, piece_lanes),
            pltpu.VMEM((3, VEC_ROWS, D), F32),
            pltpu.VMEM((3 + far_steps, VEC_ROWS, D), F32),
            pltpu.VMEM((VEC_ROWS, D), F32),
            pltpu.VMEM((near, VEC_ROWS, D), F32),
            pltpu.VMEM((some, VEC_ROWS, D), F32),
            dma((7,)),
            dma((3, 3)), dma((3, SECTIONS)),
            dma((3, SECTIONS)), dma((3, SECTIONS)),
            dma((3,)), dma((3,)),
            dma((groups,)), dma((groups,)),
            dma((groups, 3)), dma((groups, 3)),
            dma((groups, near)), dma((groups, near)),
            dma((groups, some)), dma((groups, some)),
            dma((groups, near)), dma((2, SECTIONS, near)),
            dma((SECTIONS,)), dma((SECTIONS,)),
            dma((3,)), dma((3,)),
            dma((1,)), dma((1,)),
            dma((near,)), dma((near,)),
            dma((some,)), dma((some,)),
        ]
        + layer_scratch(n),
        compiler_params=pltpu.CompilerParams(
            vmem_limit_bytes=60 * 1024 * 1024, collective_id=0, has_side_effects=True
        ),
        name="two_layers",
    )(
        jnp.transpose(inputs, (0, 2, 1, 3)),
        jnp.transpose(cotangent, (0, 2, 1, 3)),
        jnp.swapaxes(routes, 3, 4),
        vectors,
        in_weight,
        out_weight,
    )
    by_token = jax.ShapeDtypeStruct((1, PATCHES, n, D), BF)
    fin, gin, gvec, ga, gb = pl.pallas_call(
        functools.partial(results_kernel, dp, images),
        out_shape=(
            by_token,
            by_token,
            jax.ShapeDtypeStruct((1, VEC_ROWS, D), F32),
            jax.ShapeDtypeStruct((1, D, HID), F32),
            jax.ShapeDtypeStruct((1, HID, D), F32),
        ),
        in_specs=[vmem] * 4,
        out_specs=(hbm, hbm, vmem, hbm, hbm),
        scratch_shapes=[pltpu.VMEM((D, HID), F32), pltpu.VMEM((HID, D), F32), dma((4,))],
        compiler_params=pltpu.CompilerParams(vmem_limit_bytes=60 * 1024 * 1024),
        name="results",
    )(*made)
    return jnp.transpose(fin, (0, 2, 1, 3)), jnp.transpose(gin, (0, 2, 1, 3)), gvec, ga, gb


def solution(mesh):
    in_specs = (
        P(None, "dp", None, None),
        P(None, "dp", None, None),
        P(None, None, "dp", None, None),
        P("section", None, None),
        P("section", None, None),
        P("section", None, None),
    )
    out_specs = (
        P("section", "dp", None, None),
        P("section", "dp", None, None),
        P("section", None, None),
        P("section", None, None),
        P("section", None, None),
    )
    return jax.shard_map(
        per_device, mesh=mesh, in_specs=in_specs, out_specs=out_specs, check_vma=False
    )
```

```python
import functools

import jax
import jax.numpy as jnp
from jax import lax
from jax.experimental import pallas as pl
from jax.experimental.pallas import tpu as pltpu
from jax.sharding import PartitionSpec as P

D = 256
HEADS = 8
HEAD_DIM = 32
HID = 768
SIDE = 14
WIN = 7
TOPK = 4
SECTIONS = 4
VEC_ROWS = 16
PATCHES = 196
REGIONS = 49
BLOCK = 256
EPSILON = 1e-06

PITCH = 16
LIVE = SIDE * PITCH
ROWS = 256
HALO = 24
CHUNK = 32
LANES = 128
NEGATIVE = -1e30
LOG2E = 1.4426950408889634
SCALE = HEAD_DIM ** (-0.5)

BF = jnp.bfloat16
F32 = jnp.float32


def dot(a, b, ca=1, cb=0):
    return lax.dot_general(
        a, b, (((ca,), (cb,)), ((), ())), preferred_element_type=jnp.float32
    )


def iota(shape, dim):
    return lax.broadcasted_iota(jnp.int32, shape, dim)


def one_hot(cond):
    return jnp.where(cond, 1.0, 0.0).astype(BF)


def rows_of(i, count=LIVE):
    return pl.ds(pl.multiple_of(i * ROWS, ROWS), count)


def col_sum(x):
    return jnp.sum(x, axis=0, keepdims=True)


def ln_stats(x):
    average = jnp.mean(x, axis=-1, keepdims=True)
    centred = x - average
    spread = jnp.mean(centred * centred, axis=-1, keepdims=True)
    inverse = lax.rsqrt(spread + EPSILON)
    return centred * inverse, inverse


def gelu_pair(x):
    a = jnp.abs(x)
    t = 1.0 / (1.0 + a * (0.3275911 * 0.7071067811865476))
    e = jnp.exp2(x * x * (-0.5 * LOG2E))
    w = t * (0.5 * 1.061405429) + (0.5 * -1.453152027)
    w = w * t + (0.5 * 1.421413741)
    w = w * t + (0.5 * -0.284496736)
    w = w * t + (0.5 * 0.254829592)
    w = w * t * e
    phi = jnp.where(x >= 0, 1.0 - w, w)
    return x * phi, phi + x * e * 0.3989422804014327


def region_one_hot(shape, token_dim):
    token = iota(shape, token_dim)
    region = iota(shape, 1 - token_dim)
    r, c = token >> 4, token & (PITCH - 1)
    own = (r >> 1) * WIN + (c >> 1)
    return one_hot((own == region) & (c < SIDE) & (r < SIDE))


def weight_grads(scratch, s, first, count, half):
    nmt, att, actt, g, dproj = (scratch[LAYER_SCRATCH.index(name)] for name in ("nmt", "att", "actt", "g", "dproj"))
    results = []
    ins = min(first + count, 3) - first
    if ins > 0:
        rows = pl.ds(pl.multiple_of(half * LANES, LANES), LANES)
        wide = dot(nmt[s, rows], dproj[:, first * D : (first + ins) * D])
        results += [wide[:, b * D : (b + 1) * D] for b in range(ins)]
    for b in range(max(first, 3) - 3, first + count - 3):
        rows = pl.ds(pl.multiple_of(b * D + half * LANES, LANES), LANES)
        results.append(dot((actt if s % 2 == 1 else att)[s // 2, rows], g[...]))
    return results


LAYER_SCRATCH = (
    "hs", "zh", "inv", "nm", "nmt", "pr", "pt", "att", "act", "actt", "gp", "bias", "mixed", "g", "dproj", "cv", "cvl", "cvr",
    "dom", "qm", "dsb", "tmp", "dqt", "km", "wide",
)


def layers(
    n, at_point,
    x_ref, cot_ref, routes_ref, vec_ref, win_ref, wout_ref, fin_ref, gin_ref, gvec_ref,
    hs, zh, inv, nm, nmt, pr, pt, att, act, actt, gp, bias, mixed, g, dproj, cv, cvl, cvr, dom, qm, dsb, tmp, dqt, km, wide,
):
    pairs = PATCHES * n

    def eye():
        return one_hot(iota((ROWS, ROWS), 0) == iota((ROWS, ROWS), 1))

    def transposed(x):
        return dot(eye(), x, 1, 1)

    def spread(i):
        t, p = iota((ROWS, pairs), 0), iota((ROWS, pairs), 1)
        r, c = t >> 4, t & (PITCH - 1)
        return one_hot((p == (r * SIDE + c) * n + i) & (c < SIDE) & (r < SIDE))

    def gather():
        p, t = iota((pairs, n * ROWS), 0), iota((pairs, n * ROWS), 1)
        r, c, i = (t & (ROWS - 1)) >> 4, t & (PITCH - 1), t >> 8
        return one_hot((p == (r * SIDE + c) * n + i) & (c < SIDE) & (r < SIDE))

    def chunks():
        return [slice(c, c + CHUNK) for c in range(0, LIVE, CHUNK)]

    def rows_at(i, c, count):
        return pl.ds(pl.multiple_of(i * ROWS + c, PITCH), count)

    def tail(i):
        return pl.ds(i * ROWS + LIVE, ROWS - LIVE)

    none = jnp.zeros((ROWS - LIVE, D), BF)
    none_wide = jnp.zeros((ROWS - LIVE, HID), BF)
    halo = jnp.zeros((HALO, D), F32)
    for buffer in (cv, cvl, cvr):
        buffer[0:HALO] = halo
        buffer[HALO + LIVE : HALO + LIVE + HALO] = halo
    for i in range(n):
        for s in range(SECTIONS):
            nm[s, tail(i)] = none
            hs[s, tail(i)] = none
        for a in range(2):
            pr[a, tail(i)] = none_wide
            act[a, tail(i)] = none_wide
        wide[tail(i)] = none
        dproj[tail(i)] = none_wide
    gvec_ref[...] = jnp.zeros_like(gvec_ref)

    at_point("inputs", 0)
    x_pairs = x_ref[...].reshape(pairs, D)
    cot_pairs = cot_ref[...].reshape(pairs, D)
    for i in range(n):
        spread_i = spread(i)
        hs[0, pl.ds(i * ROWS, ROWS)] = dot(spread_i, x_pairs).astype(BF)
        g[pl.ds(i * ROWS, ROWS)] = dot(spread_i, cot_pairs).astype(BF)

    def conv_load(r0, count, x):
        cv[pl.ds(HALO + r0, count)] = x

    def conv_shift():
        for rows in chunks():
            cvl[HALO + rows.start : HALO + rows.stop] = cv[HALO + rows.start - 1 : HALO + rows.stop - 1]
            cvr[HALO + rows.start : HALO + rows.stop] = cv[HALO + rows.start + 1 : HALO + rows.stop + 1]

    def conv_at(r, u, v):
        start = HALO + (r + u) * PITCH
        return (cvl, cv, cvr)[v + 1][start : start + PITCH]

    def columns(i):
        return slice(i * ROWS, (i + 1) * ROWS)

    def attention_start(s):
        vec = vec_ref.at[s]
        for i in range(n):
            for rows in chunks():
                conv_load(rows.start, CHUNK, hs[s, rows_at(i, rows.start, CHUNK)].astype(F32))
            conv_shift()
            for r in range(SIDE):
                total = conv_at(r, 0, 0) + vec[15:16]
                for u in (-1, 0, 1):
                    for v in (-1, 0, 1):
                        j = 6 + 3 * (u + 1) + v + 1
                        total = total + conv_at(r, u, v) * vec[j : j + 1]
                here = rows_at(i, r * PITCH, PITCH)
                mixed[here] = total
                hat, inverse = ln_stats(total)
                zh[s, here] = hat
                inv[s, here] = inverse
                nm[s, here] = (hat * vec[0:1] + vec[1:2]).astype(BF)
        for i in range(n):
            nmt[s, :, columns(i)] = transposed(nm[s, rows_of(i, ROWS)]).astype(BF)

    def route_bias():
        key_region = region_one_hot((LIVE, REGIONS), 0)
        query_region = region_one_hot((REGIONS, ROWS), 1)
        for i in range(n):
            for a in range(2):
                picks = routes_ref[a, i]
                region = iota((REGIONS, REGIONS), 0)
                routed = jnp.zeros((REGIONS, REGIONS), F32)
                for k in range(TOPK):
                    routed = routed + jnp.where(picks[k : k + 1] == region, 1.0, 0.0)
                by_region = dot(key_region, routed.astype(BF)).astype(BF)
                bias[a, i] = (1.0 - dot(by_region, query_region)) * NEGATIVE

    def half_of(h):
        return slice((h // 4) * LANES, (h // 4 + 1) * LANES)

    def own_lanes(h, count):
        return (iota((count, LANES), 1) >> 5) == h % 4

    def attention_forward(s):
        a = s // 2
        vec = vec_ref.at[s]
        at_point("weights", s)
        for i in range(n):
            rows = rows_of(i)
            pr[a, rows, 0 : 2 * D] = dot(nm[s, rows], win_ref[s, :, 0 : 2 * D]).astype(BF)
        for i in range(n):
            rows, whole = rows_of(i), rows_of(i, ROWS)
            for h in range(HEADS):
                lanes = half_of(h)
                keys = jnp.where(own_lanes(h, LIVE), pr[a, rows, slice(D + lanes.start, D + lanes.stop)], jnp.zeros((), BF))
                scores = dot(keys, pr[a, whole, lanes], 1, 1) * (SCALE * LOG2E) + bias[a, i]
                expo = jnp.exp2(scores - jnp.max(scores, axis=0, keepdims=True))
                pt[a, i, :, h * ROWS : (h + 1) * ROWS] = (expo * (1.0 / col_sum(expo))).astype(BF)
        at_point("scores", s)
        at_point("values", s)
        for i in range(n):
            rows, whole = rows_of(i), rows_of(i, ROWS)
            pr[a, rows, 2 * D : 3 * D] = dot(nm[s, rows], win_ref[s, :, 2 * D : 3 * D]).astype(BF)
            tmp[i] = transposed(pr[a, whole, 2 * D : 3 * D]).astype(BF)
        for i in range(n):
            for h in range(HEADS):
                own = slice(h * HEAD_DIM, (h + 1) * HEAD_DIM)
                att[a, own, columns(i)] = dot(tmp[i, own, 0:LIVE], pt[a, i, :, h * ROWS : (h + 1) * ROWS]).astype(BF)
        at_point("out", s)
        for i in range(n):
            attended = transposed(att[a, :, columns(i)]).astype(BF)
            out = mixed[rows_of(i)] + dot(attended[:LIVE], wout_ref[s, 0:D]) + vec[2:3]
            hs[s + 1, rows_of(i)] = out.astype(BF)

    def dense_forward(s):
        a = s // 2
        vec = vec_ref.at[s]
        for i in range(n):
            for part in chunks():
                here = rows_at(i, part.start, CHUNK)
                hat, inverse = ln_stats(hs[s, here].astype(F32))
                zh[s, here] = hat
                inv[s, here] = inverse
                nm[s, here] = (hat * vec[0:1] + vec[1:2]).astype(BF)
        for i in range(n):
            nmt[s, :, columns(i)] = transposed(nm[s, rows_of(i, ROWS)]).astype(BF)
        at_point("weights", s)
        at_point("values", s)
        for j in range(3):
            lanes = slice(j * D, (j + 1) * D)
            for i in range(n):
                rows = rows_of(i)
                hidden = dot(nm[s, rows], win_ref[s, :, lanes]) + vec[3 + j : 4 + j]
                value, slope = gelu_pair(hidden)
                act[a, rows, lanes] = value.astype(BF)
                gp[a, rows, lanes] = slope
        at_point("out", s)
        for i in range(n):
            rows = rows_of(i)
            out = hs[s, rows].astype(F32) + dot(act[a, rows], wout_ref[s]) + vec[2:3]
            if s + 1 < SECTIONS:
                live = (iota((LIVE, D), 0) & (PITCH - 1)) < SIDE
                hs[s + 1, rows] = jnp.where(live, out, 0.0).astype(BF)
            else:
                wide[rows] = out.astype(BF)
        for j in range(3):
            lanes = slice(j * D, (j + 1) * D)
            for i in range(n):
                actt[a, lanes, columns(i)] = transposed(act[a, rows_of(i, ROWS), lanes]).astype(BF)

    def norm_backward(s, here, d_normed, sums):
        vec = vec_ref.at[s]
        hat = zh[s, here]
        product = d_normed * hat
        scaled = d_normed * vec[0:1]
        first = jnp.mean(scaled, axis=-1, keepdims=True)
        second = jnp.mean(product * vec[0:1], axis=-1, keepdims=True)
        sums[0] = sums[0] + fold(product)
        sums[1] = sums[1] + fold(d_normed)
        return inv[s, here] * (scaled - first - hat * second)

    def fold(x):
        return jnp.sum(x.reshape(x.shape[0] // 8, 8, x.shape[1]), axis=0)

    def empty():
        return jnp.zeros((8, D), F32)

    def add_row(s, row, total):
        gvec_ref[s, row : row + 1] += col_sum(total)

    def dense_backward(s):
        a = s // 2
        at_point("first grads", s)
        for i in range(n):
            rows = rows_of(i)
            for j in range(3):
                lanes = slice(j * D, (j + 1) * D)
                d_active = dot(g[rows], wout_ref[s, lanes], 1, 1)
                d_hidden = (d_active * gp[a, rows, lanes]).astype(BF)
                dproj[rows, lanes] = d_hidden
                add_row(s, 3 + j, fold(d_hidden.astype(F32)))
        at_point("grads", s)
        for i in range(n):
            rows = rows_of(i)
            d_normed = dot(dproj[rows], win_ref[s], 1, 1)
            sums = [empty(), empty(), empty()]
            for part in chunks():
                here = rows_at(i, part.start, CHUNK)
                grad = g[here].astype(F32)
                sums[2] = sums[2] + fold(grad)
                out = grad + norm_backward(s, here, d_normed[part], sums)
                g[here] = out.astype(BF)
            for row in range(3):
                add_row(s, row, sums[row])
            at_point("image", 2 * s + i)

    def attention_backward(s):
        a = s // 2
        vec = vec_ref.at[s]
        nothing = jnp.zeros((), BF)
        for i in range(n):
            rows = rows_of(i)
            whole = rows_of(i, ROWS)
            km[whole] = dot(g[whole], wout_ref[s, 0:D], 1, 1).astype(BF)
            for h in range(HEADS):
                dom[h * ROWS : (h + 1) * ROWS] = jnp.where(own_lanes(h, ROWS), km[whole, half_of(h)], nothing)
            for half in range(2):
                lanes = slice(2 * D + half * LANES, 2 * D + (half + 1) * LANES)
                four = slice(half * 4 * ROWS, (half + 1) * 4 * ROWS)
                dproj[rows, lanes] = dot(pt[a, i, :, four], dom[four]).astype(BF)
        at_point("first grads", s)
        for i in range(n):
            whole = rows_of(i, ROWS)
            tmp[i] = transposed(pr[a, whole, D : 2 * D]).astype(BF)
            for h in range(HEADS):
                qm[i, h * ROWS : (h + 1) * ROWS] = jnp.where(own_lanes(h, ROWS), pr[a, whole, half_of(h)], nothing)
        for i in range(n):
            rows = rows_of(i)
            whole = rows_of(i, ROWS)
            for h in range(HEADS):
                lanes = half_of(h)
                row = slice(h * ROWS, (h + 1) * ROWS)
                values = jnp.where(own_lanes(h, LIVE), pr[a, rows, slice(2 * D + lanes.start, 2 * D + lanes.stop)], nothing)
                d_weights = dot(values, km[whole, lanes], 1, 1)
                weights = pt[a, i, :, row].astype(F32)
                dsb[i, :, row] = (weights * (d_weights - col_sum(weights * d_weights))).astype(BF)
            at_point("half", 2 * s + i)
        for i in range(n):
            rows = rows_of(i)
            for h in range(HEADS):
                own = slice(h * HEAD_DIM, (h + 1) * HEAD_DIM)
                dqt[own, columns(i)] = dot(tmp[i, own, 0:LIVE], dsb[i, :, h * ROWS : (h + 1) * ROWS])
            for half in range(2):
                lanes = slice(D + half * LANES, D + (half + 1) * LANES)
                four = slice(half * 4 * ROWS, (half + 1) * 4 * ROWS)
                dproj[rows, lanes] = (dot(dsb[i, :, four], qm[i, four]) * SCALE).astype(BF)
        for i in range(n):
            dproj[rows_of(i), 0:D] = (transposed(dqt[:, columns(i)].astype(BF))[:LIVE] * SCALE).astype(BF)
            at_point("image", 2 * s + i)
        at_point("grads", s)
        for i in range(n):
            rows = rows_of(i)
            d_normed = dot(dproj[rows], win_ref[s], 1, 1)
            sums = [empty(), empty(), empty(), empty()]
            for part in chunks():
                here = rows_at(i, part.start, CHUNK)
                grad = g[here].astype(F32)
                sums[2] = sums[2] + fold(grad)
                d_mixed = grad + norm_backward(s, here, d_normed[part], sums)
                sums[3] = sums[3] + fold(d_mixed)
                conv_load(part.start, CHUNK, d_mixed)
            for row, total in zip((0, 1, 2, 15), sums):
                add_row(s, row, total)
            at_point("norm", 2 * s + i)
            conv_shift()
            taps = [empty() for _ in range(9)]
            for r in range(SIDE):
                here = rows_at(i, r * PITCH, PITCH)
                start = hs[s, here].astype(F32)
                total = conv_at(r, 0, 0)
                for u in (-1, 0, 1):
                    for v in (-1, 0, 1):
                        j = 3 * (u + 1) + v + 1
                        moved = conv_at(r, -u, -v)
                        total = total + moved * vec[6 + j : 7 + j]
                        taps[j] = taps[j] + fold(moved * start)
                g[here] = jnp.where(iota((PITCH, D), 0) < SIDE, total, 0.0).astype(BF)
            for j in range(9):
                add_row(s, 6 + j, taps[j])
            at_point("conv", 2 * s + i)

    route_bias()
    at_point("routed", 0)
    attention_start(0)
    at_point("prepared", 0)
    for s in range(SECTIONS):
        if s == 2:
            attention_start(s)
        (attention_forward, dense_forward)[s % 2](s)
    for s in reversed(range(SECTIONS)):
        (attention_backward, dense_backward)[s % 2](s)

    def finish():
        pick = gather()
        fin_ref[...] = dot(pick, wide[...]).astype(BF).reshape(PATCHES, n, D)
        gin_ref[...] = dot(pick, g[...]).astype(BF).reshape(PATCHES, n, D)

    return finish


def layer_scratch(n):
    total = n * ROWS
    return [
        pltpu.VMEM((SECTIONS, total, D), BF),
        pltpu.VMEM((SECTIONS, total, D), F32),
        pltpu.VMEM((SECTIONS, total, 1), F32),
        pltpu.VMEM((SECTIONS, total, D), BF),
        pltpu.VMEM((SECTIONS, D, total), BF),
        pltpu.VMEM((2, total, HID), BF),
        pltpu.VMEM((2, n, LIVE, HEADS * ROWS), BF),
        pltpu.VMEM((2, D, total), BF),
        pltpu.VMEM((2, total, HID), BF),
        pltpu.VMEM((2, HID, total), BF),
        pltpu.VMEM((2, total, HID), F32),
        pltpu.VMEM((2, n, LIVE, ROWS), F32),
        pltpu.VMEM((total, D), F32),
        pltpu.VMEM((total, D), BF),
        pltpu.VMEM((total, HID), BF),
        pltpu.VMEM((LIVE + 2 * HALO, D), F32),
        pltpu.VMEM((LIVE + 2 * HALO, D), F32),
        pltpu.VMEM((LIVE + 2 * HALO, D), F32),
        pltpu.VMEM((HEADS * ROWS, LANES), BF),
        pltpu.VMEM((n, HEADS * ROWS, LANES), BF),
        pltpu.VMEM((n, LIVE, HEADS * ROWS), BF),
        pltpu.VMEM((n, D, ROWS), BF),
        pltpu.VMEM((D, total), F32),
        pltpu.VMEM((total, D), BF),
        pltpu.VMEM((total, D), BF),
    ]


def compute_kernel(n, *refs):
    x_ref, cot_ref, routes_ref, vec_ref, win_ref, wout_ref, fin_ref, gin_ref, gvec_ref, ga_ref, gb_ref = refs[:11]

    def at_point(name, s):
        if name != "grads":
            return
        count = 6 if s % 2 == 1 else 4
        for half in range(2):
            for b, value in enumerate(weight_grads(refs[11:], s, 0, count, half)):
                rows = slice(half * LANES, (half + 1) * LANES)
                if b < 3:
                    ga_ref[s, rows, b * D : (b + 1) * D] = value
                else:
                    gb_ref[s, (b - 3) * D + half * LANES : (b - 3) * D + (half + 1) * LANES] = value
        if s % 2 == 0:
            gb_ref[s, D:HID] = jnp.zeros((HID - D, D), F32)

    layers(n, at_point, x_ref, cot_ref, routes_ref, vec_ref, win_ref, wout_ref, fin_ref.at[0], gin_ref.at[0], gvec_ref, *refs[11:])()


def compute(x, cot, routes, vec, win, wout):
    n = x.shape[0]
    vmem = pl.BlockSpec(memory_space=pltpu.VMEM)
    by_token = jax.ShapeDtypeStruct((1, PATCHES, n, D), BF)
    fin, gin, gvec, ga, gb = pl.pallas_call(
        functools.partial(compute_kernel, n),
        out_shape=(
            by_token,
            by_token,
            jax.ShapeDtypeStruct((SECTIONS, VEC_ROWS, D), F32),
            jax.ShapeDtypeStruct((SECTIONS, D, HID), F32),
            jax.ShapeDtypeStruct((SECTIONS, HID, D), F32),
        ),
        in_specs=[vmem] * 6,
        out_specs=(vmem,) * 5,
        scratch_shapes=layer_scratch(n),
        compiler_params=pltpu.CompilerParams(vmem_limit_bytes=56 * 1024 * 1024),
        name="layers_alone",
    )(jnp.transpose(x, (1, 0, 2)), jnp.transpose(cot, (1, 0, 2)), jnp.swapaxes(routes, 2, 3), vec, win, wout)
    return jnp.transpose(fin, (0, 2, 1, 3)), jnp.transpose(gin, (0, 2, 1, 3)), gvec, ga, gb


MESH = pl.DeviceIdType.MESH
HALF = BLOCK // 2
PART = HALF // SECTIONS


def blocks_of(t):
    return 6 if t % 2 == 1 else 4


GROUPS = ((0, 0, 2), (1, 0, 6), (2, 0, 4), (3, 0, 6), (0, 2, 2))


def shares_of(dp):
    chips = dp // 2
    near = min(chips, 4)
    split = min(near, 2)
    return near, PART // split, BLOCK // (near // split), (chips // near).bit_length() - 1


def piece_slices(dp, piece):
    near, piece_rows, piece_lanes, _ = shares_of(dp)
    k, q = piece // near, piece % near
    rows = k * PART + q % (PART // piece_rows) * piece_rows
    lanes = q // (PART // piece_rows) * piece_lanes
    return slice(rows, rows + piece_rows), slice(lanes, lanes + piece_lanes)


def results_kernel(dp, images, fin_in, gin_in, gvec_in, result, fin_ref, gin_ref, gvec_ref, ga_ref, gb_ref, ga, gb, sems):
    copies = [
        pltpu.make_async_copy(fin_in, fin_ref.at[0], sems.at[0]),
        pltpu.make_async_copy(gin_in, gin_ref.at[0], sems.at[1]),
        pltpu.make_async_copy(ga, ga_ref.at[0], sems.at[2]),
        pltpu.make_async_copy(gb, gb_ref.at[0], sems.at[3]),
    ]
    copies[0].start()
    copies[1].start()
    gvec_ref[0] = gvec_in[...] * (1.0 / images)
    for target, first in ((ga, 0), (gb, 3)):
        for c in range(2):
            for piece in range(result.shape[1]):
                rows, lanes = piece_slices(dp, piece)
                for b in range(3):
                    value = result[c, piece, first + b].astype(F32) * (1.0 / images)
                    start = c * HALF + rows.start
                    if first == 0:
                        target[start : start + rows.stop - rows.start, b * D + lanes.start : b * D + lanes.stop] = value
                    else:
                        target[b * D + start : b * D + start + rows.stop - rows.start, lanes] = value
        if first == 0:
            copies[2].start()

    @pl.when(lax.rem(lax.axis_index("section"), 2) == 0)
    def _():
        gb[D:HID] = jnp.zeros((HID - D, D), F32)

    copies[3].start()
    for copy in copies:
        copy.wait()


def whole_kernel(
    n, dp, images,
    inputs_ref, cot_in_ref, routes_in_ref, vec_own, win_own, wout_own,
    fin_ref, gin_ref, gvec_ref, result,
    x_ref, cot_ref, routes_ref, vec_ref, win_ref, wout_ref, gvec_part,
    own_half, send_half, got_half, half_sum, got_part, part_sum, got_near, share, got_far, vec_got, vec_sum, vec_mate, vec_near, vec_far,
    in_sem, w_send, w_recv, f_send, f_recv, v_send, v_recv, h_send, h_recv, p_send, p_recv, n_send, n_recv, d_send, d_recv,
    r_send, r_recv, m_send, m_recv, gv_send, gv_recv, gm_send, gm_recv, gn_send, gn_recv, gd_send, gd_recv,
    *scratch,
):
    me, j = lax.axis_index("section"), lax.axis_index("dp")
    core = lax.rem(j, 2)
    chip = j // 2
    near, piece_rows, piece_lanes, far_steps = shares_of(dp)
    place = lax.rem(chip, near)
    xor = lax.bitwise_xor

    def device(k, q, other=0):
        return (xor(me, k), xor(j, 2 * q + other))

    mate = device(0, 0, 1)
    sections = [device(k, 0) for k in range(1, SECTIONS)]
    around = [(k, q) for k in range(SECTIONS) for q in range(near) if (k, q) != (0, 0)]
    far = [(me, xor(j, 2 * near << b)) for b in range(far_steps)]
    waiting = []

    def remote(src, dst, send, recv, to):
        return pltpu.make_async_remote_copy(src, dst, send, recv, device_id=to, device_id_type=MESH)

    def when(condition, act):
        if condition is None:
            act()
        else:
            pl.when(condition)(act)

    def go(copy, condition=None):
        when(condition, lambda: copy.start())
        waiting.append((copy, condition))

    loads = [
        pltpu.make_async_copy(inputs_ref.at[me], x_ref, in_sem.at[0]),
        pltpu.make_async_copy(cot_in_ref.at[me], cot_ref, in_sem.at[1]),
        pltpu.make_async_copy(routes_in_ref.at[0, me], routes_ref.at[0], in_sem.at[2]),
        pltpu.make_async_copy(routes_in_ref.at[1, me], routes_ref.at[1], in_sem.at[3]),
        pltpu.make_async_copy(vec_own.at[0], vec_ref.at[me], in_sem.at[4]),
        pltpu.make_async_copy(win_own.at[0], win_ref.at[me], in_sem.at[5]),
        pltpu.make_async_copy(wout_own.at[0], wout_ref.at[me], in_sem.at[6]),
    ]
    for copy in loads:
        copy.start()

    barrier = pltpu.get_barrier_semaphore()
    everyone = [device(k, q) for k, q in around] + [mate] + far
    for to in everyone:
        pl.semaphore_signal(barrier, inc=1, device_id=to, device_id_type=MESH)
    pl.semaphore_wait(barrier, len(everyone))

    own_rows = pl.ds(pl.multiple_of(core * HALF, HALF), HALF)
    tail_rows = pl.ds(pl.multiple_of(D + core * D, D), D)
    pieces = [(win_own, win_ref, own_rows), (wout_own, wout_ref, own_rows), (wout_own, wout_ref, tail_rows)]

    def needed(p, t):
        return None if p < 2 else lax.rem(t, 2) == 1

    def spot(p, t):
        return pieces[p][1].at[t, pieces[p][2]]

    vec_copies = [remote(vec_own.at[0], vec_ref.at[me], v_send.at[k], v_recv.at[k], to) for k, to in enumerate(sections)]
    out_copies = [
        [
            remote(source.at[0, rows], target.at[me, rows], w_send.at[p, k - 1], w_recv.at[p, me], device(k, 0))
            for k in (1, 2)
        ]
        for p, (source, target, rows) in enumerate(pieces)
    ]
    relayed, relay_to = xor(me, 1 + core), xor(me, 2 - core)
    relays = [remote(spot(p, relayed), spot(p, relayed), w_send.at[p, 2], w_recv.at[p, relayed], (relay_to, j)) for p in range(3)]
    origins = {"relayed": relayed, "other": relay_to, "corner": xor(me, 3)}
    arrivals, handings, takings = {}, {}, {}
    for p in range(3):
        for name, t in origins.items():
            arrivals[p, name] = remote(spot(p, t), spot(p, t), w_send.at[p, 0], w_recv.at[p, t], mate)
            handings[p, name] = remote(spot(p, t), spot(p, t), f_send.at[p, t], f_recv.at[p, t], mate)
        for t in range(SECTIONS):
            if p < 2 or t % 2 == 1:
                takings[p, t] = remote(spot(p, t), spot(p, t), f_send.at[p, t], f_recv.at[p, t], mate)
    foreign = [me != t for t in range(SECTIONS)]

    def send_weights(p):
        for copy in out_copies[p]:
            go(copy, needed(p, me))

    def pass_on(p, *names):
        for name in names:
            when(needed(p, origins[name]), lambda: arrivals[p, name].wait_recv())
            if name == "relayed":
                go(relays[p], needed(p, relayed))
        for name in names:
            go(handings[p, name], needed(p, origins[name]))

    def take_weights(t, p):
        if p < 2 or t % 2 == 1:
            pl.when(foreign[t])(lambda: takings[p, t].wait_recv())

    for copy in reversed(vec_copies):
        go(copy)
    send_weights(0)

    def piece_of(k, q):
        return k * near + q

    def quarter(k):
        return pl.ds(pl.multiple_of(k * near, near), near)

    mine = piece_of(me, place)
    steps = {}

    def halves_start(t):
        section, first, count = GROUPS[t]
        for b, value in enumerate(weight_grads(scratch, section, first, count, 1 - core)):
            send_half[t][b] = value.astype(BF)
        copy = remote(send_half[t], got_half[t], h_send.at[t], h_recv.at[t], mate)
        go(copy)
        for b, value in enumerate(weight_grads(scratch, section, first, count, core)):
            own_half[t][b] = value.astype(BF)
        steps[t] = [copy]

    def halves_end(t):
        steps[t][0].wait_recv()
        for b in range(GROUPS[t][2]):
            total = own_half[t][b] + got_half[t][b]
            for piece in range(SECTIONS * near):
                rows, lanes = piece_slices(dp, piece)
                half_sum[t][piece, b] = total[rows, lanes]

    def parts_start(t):
        steps[t] = [
            remote(half_sum[t].at[quarter(to[0])], got_part[t].at[k], p_send.at[t, k], p_recv.at[t, k], to)
            for k, to in enumerate(sections)
        ]
        for copy in reversed(steps[t]):
            go(copy)

    def parts_end(t):
        for copy in steps[t]:
            copy.wait_recv()
        for q in range(near):
            for b in range(GROUPS[t][2]):
                total = half_sum[t][piece_of(me, q), b].astype(F32)
                for k in range(SECTIONS - 1):
                    total = total + got_part[t][k, q, b].astype(F32)
                part_sum[t][q, b] = total.astype(BF)

    def near_start(t):
        steps[t] = []
        for q in reversed(range(1, near)):
            to_place = xor(place, q)
            source = part_sum[t].at[to_place]
            steps[t].append(remote(source, got_near[t].at[q], n_send.at[t, q], n_recv.at[t, q], device(0, q)))
        for copy in steps[t]:
            go(copy)

    def share_end(t, own, slots):
        for copy in steps[t]:
            copy.wait_recv()
        for b in range(GROUPS[t][2]):
            total = own(b).astype(F32)
            for slot in slots:
                total = total + got_near[t][slot, b].astype(F32)
            share[t][0, b] = total.astype(BF)
        for step in range(far_steps):
            copy = remote(share[t].at[step], got_far[t].at[step], d_send.at[t, step], d_recv.at[t, step], far[step])
            go(copy)
            copy.wait_recv()
            for b in range(GROUPS[t][2]):
                share[t][step + 1, b] = (share[t][step, b].astype(F32) + got_far[t][step, b].astype(F32)).astype(BF)
        deliver(t)

    def near_end(t):
        share_end(t, lambda b: part_sum[t][place, b], range(1, near))

    def deliver(t):
        section, first, count = GROUPS[t]
        last = share[t].at[far_steps]
        spot = result.at[core, mine, pl.ds(first, count)]
        for q in reversed(range(near)):
            to = (section, xor(j, 2 * q))
            go(remote(last, spot, r_send.at[t, q], r_recv.at[t // 4, me, place], to), None if q > 0 else me != section)

        @pl.when(me == section)
        def _():
            for b in range(count):
                result[core, mine, first + b] = share[t][far_steps, b]

    copies = {}

    def vectors_start():
        copies["sections"] = [
            remote(gvec_part.at[to[0]], vec_got.at[k], gv_send.at[k], gv_recv.at[k], to) for k, to in enumerate(sections)
        ]
        for copy in copies["sections"]:
            go(copy)

    def vectors_mate():
        for copy in copies["sections"]:
            copy.wait_recv()
        vec_sum[0] = gvec_part[me] + vec_got[0] + vec_got[1] + vec_got[2]
        copies["mate"] = remote(vec_sum.at[0], vec_mate, gm_send.at[0], gm_recv.at[0], mate)
        go(copies["mate"])

    def vectors_near():
        copies["mate"].wait_recv()
        vec_sum[1] = vec_sum[0] + vec_mate[...]
        copies["near"] = [remote(vec_sum.at[1], vec_near.at[q], gn_send.at[q], gn_recv.at[q], device(0, q)) for q in range(1, near)]
        for copy in copies["near"]:
            go(copy)

    def vectors_end():
        for copy in copies["near"]:
            copy.wait_recv()
        vec_near[0] = vec_sum[1]
        total = vec_near[place]
        for q in range(1, near):
            total = total + vec_near[xor(place, q)]
        vec_sum[2] = total
        for step in range(far_steps):
            copy = remote(vec_sum.at[2 + step], vec_far.at[step], gd_send.at[step], gd_recv.at[step], far[step])
            go(copy)
            copy.wait_recv()
            vec_sum[3 + step] = vec_sum[2 + step] + vec_far[step]
        gvec_ref[...] = vec_sum[2 + far_steps]

    def on(act, *rest):
        return lambda: act(*rest)

    def inputs_here():
        for copy in loads[:4]:
            copy.wait()

    def vectors_here():
        for copy in vec_copies:
            copy.wait_recv()
        for copy in loads[4:]:
            copy.wait()

    plan = {
        ("inputs", 0): [inputs_here],
        ("routed", 0): [on(send_weights, 1), on(send_weights, 2), vectors_here],
        ("prepared", 0): [
            on(pass_on, 0, "relayed", "other"),
            on(pass_on, 1, "relayed", "other"),
            on(pass_on, 2, "relayed", "other"),
            on(pass_on, 0, "corner"),
        ],
        ("weights", 1): [on(pass_on, 2, "corner")],
    }
    for t in range(SECTIONS):
        plan["weights", t] = plan.get(("weights", t), []) + [on(take_weights, t, 0)]
        plan["out", t] = [on(take_weights, t, 1), on(take_weights, t, 2)]
        plan["grads", t] = [on(halves_start, t)]
    plan["scores", 0] = [on(pass_on, 1, "corner")]
    plan["first grads", 0] = [on(halves_start, 4)]
    plan["half", 4] = [on(halves_end, 3), on(parts_start, 3)]
    plan["conv", 5] = [on(halves_end, 2), on(parts_start, 2)]
    plan["first grads", 0] = [on(halves_end, 1), on(parts_start, 1), on(halves_start, 4)]
    plan["half", 1] = [on(parts_end, 3), on(near_start, 3), on(halves_end, 4), on(parts_start, 4)]
    plan["image", 1] = [on(parts_end, 2), on(near_start, 2)]
    plan["norm", 1] = [on(halves_end, 0), on(parts_start, 0)]
    plan["conv", 1] = [vectors_start, on(near_end, 3)]
    done = []

    def at_point(name, s):
        for act in plan.get((name, s), []):
            act()
        done.append((name, s))

    finish = layers(
        n, at_point,
        x_ref, cot_ref, routes_ref, vec_ref, win_ref, wout_ref, fin_ref, gin_ref, gvec_part, *scratch,
    )
    assert all(key in done or not plan[key] for key in plan)
    for t in (1, 4):
        parts_end(t)
        near_start(t)
    near_end(2)
    parts_end(0)
    near_start(0)
    finish()
    vectors_mate()
    near_end(1)
    vectors_near()
    near_end(4)
    near_end(0)
    vectors_end()

    for section in range(SECTIONS):
        half = result.at[core, :, pl.ds(0, blocks_of(section))]

        @pl.when(me == section)
        def _():
            for t, (owner, first, count) in enumerate(GROUPS):
                if owner == section:
                    for k, q in around:
                        from_me, from_place = xor(me, k), xor(place, q)
                        spot = result.at[core, piece_of(from_me, from_place), pl.ds(first, count)]
                        remote(spot, spot, r_send.at[0, 0], r_recv.at[t // 4, from_me, from_place], mate).wait_recv()

        go(remote(half, half, m_send.at[section], m_recv.at[section], mate), me == section)

    for section in range(SECTIONS):
        half = result.at[1 - core, :, pl.ds(0, blocks_of(section))]
        copy = remote(half, half, m_send.at[section], m_recv.at[section], mate)
        pl.when(me == section)(lambda copy=copy: copy.wait_recv())

    for copy, condition in waiting:
        when(condition, lambda copy=copy: copy.wait_send())


def per_device(inputs, cotangent, routes, vectors, in_weight, out_weight):
    micro, n = inputs.shape[:2]
    dp = lax.axis_size("dp")
    near, piece_rows, piece_lanes, far_steps = shares_of(dp)
    images = micro * n * dp
    vmem = pl.BlockSpec(memory_space=pltpu.VMEM)
    hbm = pl.BlockSpec(memory_space=pltpu.HBM)
    dma = pltpu.SemaphoreType.DMA
    some, groups = max(far_steps, 1), len(GROUPS)

    def grad_buffer(*shape):
        return [pltpu.VMEM(tuple(count if size == "blocks" else size for size in shape), BF) for _, _, count in GROUPS]

    made = pl.pallas_call(
        functools.partial(whole_kernel, n, dp, images),
        out_shape=(
            jax.ShapeDtypeStruct((PATCHES, n, D), BF),
            jax.ShapeDtypeStruct((PATCHES, n, D), BF),
            jax.ShapeDtypeStruct((VEC_ROWS, D), F32),
            jax.ShapeDtypeStruct((2, SECTIONS * near, 6, piece_rows, piece_lanes), BF),
        ),
        in_specs=[hbm] * 6,
        out_specs=(vmem,) * 4,
        scratch_shapes=[
            pltpu.VMEM((PATCHES, n, D), BF),
            pltpu.VMEM((PATCHES, n, D), BF),
            pltpu.VMEM((2, n, TOPK, REGIONS), jnp.int32),
            pltpu.VMEM((SECTIONS, VEC_ROWS, D), F32),
            pltpu.VMEM((SECTIONS, D, HID), BF),
            pltpu.VMEM((SECTIONS, HID, D), BF),
            pltpu.VMEM((SECTIONS, VEC_ROWS, D), F32),
            grad_buffer("blocks", HALF, BLOCK),
            grad_buffer("blocks", HALF, BLOCK),
            grad_buffer("blocks", HALF, BLOCK),
            grad_buffer(SECTIONS * near, "blocks", piece_rows, piece_lanes),
            grad_buffer(3, near, "blocks", piece_rows, piece_lanes),
            grad_buffer(near, "blocks", piece_rows, piece_lanes),
            grad_buffer(near, "blocks", piece_rows, piece_lanes),
            grad_buffer(far_steps + 1, "blocks", piece_rows, piece_lanes),
            grad_buffer(some, "blocks", piece_rows, piece_lanes),
            pltpu.VMEM((3, VEC_ROWS, D), F32),
            pltpu.VMEM((3 + far_steps, VEC_ROWS, D), F32),
            pltpu.VMEM((VEC_ROWS, D), F32),
            pltpu.VMEM((near, VEC_ROWS, D), F32),
            pltpu.VMEM((some, VEC_ROWS, D), F32),
            dma((7,)),
            dma((3, 3)), dma((3, SECTIONS)),
            dma((3, SECTIONS)), dma((3, SECTIONS)),
            dma((3,)), dma((3,)),
            dma((groups,)), dma((groups,)),
            dma((groups, 3)), dma((groups, 3)),
            dma((groups, near)), dma((groups, near)),
            dma((groups, some)), dma((groups, some)),
            dma((groups, near)), dma((2, SECTIONS, near)),
            dma((SECTIONS,)), dma((SECTIONS,)),
            dma((3,)), dma((3,)),
            dma((1,)), dma((1,)),
            dma((near,)), dma((near,)),
            dma((some,)), dma((some,)),
        ]
        + layer_scratch(n),
        compiler_params=pltpu.CompilerParams(
            vmem_limit_bytes=60 * 1024 * 1024, collective_id=0, has_side_effects=True
        ),
        name="two_layers",
    )(
        jnp.transpose(inputs, (0, 2, 1, 3)),
        jnp.transpose(cotangent, (0, 2, 1, 3)),
        jnp.swapaxes(routes, 3, 4),
        vectors,
        in_weight,
        out_weight,
    )
    by_token = jax.ShapeDtypeStruct((1, PATCHES, n, D), BF)
    fin, gin, gvec, ga, gb = pl.pallas_call(
        functools.partial(results_kernel, dp, images),
        out_shape=(
            by_token,
            by_token,
            jax.ShapeDtypeStruct((1, VEC_ROWS, D), F32),
            jax.ShapeDtypeStruct((1, D, HID), F32),
            jax.ShapeDtypeStruct((1, HID, D), F32),
        ),
        in_specs=[vmem] * 4,
        out_specs=(hbm, hbm, vmem, hbm, hbm),
        scratch_shapes=[pltpu.VMEM((D, HID), F32), pltpu.VMEM((HID, D), F32), dma((4,))],
        compiler_params=pltpu.CompilerParams(vmem_limit_bytes=60 * 1024 * 1024),
        name="results",
    )(*made)
    return jnp.transpose(fin, (0, 2, 1, 3)), jnp.transpose(gin, (0, 2, 1, 3)), gvec, ga, gb


def solution(mesh):
    in_specs = (
        P(None, "dp", None, None),
        P(None, "dp", None, None),
        P(None, None, "dp", None, None),
        P("section", None, None),
        P("section", None, None),
        P("section", None, None),
    )
    out_specs = (
        P("section", "dp", None, None),
        P("section", "dp", None, None),
        P("section", None, None),
        P("section", None, None),
        P("section", None, None),
    )
    return jax.shard_map(
        per_device, mesh=mesh, in_specs=in_specs, out_specs=out_specs, check_vma=False
    )
```
